32 devices in a mesh: brick: 16 (over z, x, core), relay: 2 (over y).
Axes of the slice: x: 2, y: 2, z: 4, core: 2. Of those that a mesh axis runs over, the one named last changes fastest.
Arguments:
- target: float32 [8, 128, 1536], P('relay', 'brick'), may hold values from 0.1 to 9, as said below
- frag_brick: int32 [2048, 1], P(('brick', 'relay')), may hold values from 0 to 15; in each aligned block of 64 rows (0 to 63, 64 to 127, ...) at most 8 rows name the same one
- bead_cell: int32 [2048, 128], P(('brick', 'relay')), may hold values from 0 to 49151
- bead_weight: bfloat16 [2048, 128], P(('brick', 'relay')), may hold values from 0.29882812 to 3
- bead_arm: float32 [3, 2048, 128], P(None, ('brick', 'relay')), may hold values from -12 to 12
- frag_angle: float32 [3, 2048], P(None, ('brick', 'relay')), may hold values from -3.140625 to 3.140625
Outputs:
- frag_grad: float32 [6, 2048], P(None, ('brick', 'relay'))
The draws below stay inside these ranges and needn't reach their ends.
Inputs may be any that keep to these rules, and one draw needn't show every extreme that they name: `frag_brick`: each device's 64 fragments name at most 8 fragments for one strip. `bead_cell`: A bead's voxel numbered (plane * 8 + x) * 1536 + y within the block of its fragment's strip on its owner's relay index. `target`: positive map intensity.
All inputs are finite; a program needn't handle non-finite values.
Results may differ from the reference program's by a relative error of at most 0.0003.
Values may be sent and summed in bfloat16 or wider, within the bound.
No kernel may reach another device: no remote copies, remote signals or barrier semaphores. Data moves between devices by JAX's collectives and lax.ppermute only.
A program may use at most 128 MiB of HBM per device.

```python
import math
import jax
import jax.numpy as jnp
import numpy as np
from jax import lax

CX = 8
NY = 1536
CZ = 4
F_DEV = 64
BEADS = 128
KR = 4
MOST = 8
NX = 128
NZ = 8
FRAGS = 2048
N_BRICK = 16
N_RELAY = 2


def draw_target(key, part):
    shape = (NZ, NX, NY)
    across = jnp.arange(NX, dtype=jnp.float32)[None, :, None] / max(NX - 1, 1)
    profile = 1.0 + 2.0 * across
    rough = jax.random.uniform(key, shape, jnp.float32, 0.2, 1.8)
    return rough * profile


def plant(values, own_key, smallest, largest):
    place = [jax.random.randint(jax.random.fold_in(own_key, axis), (), 0, length) for axis, length in enumerate(values.shape)]
    widest = values.shape.index(max(values.shape))
    next_to = place[:widest] + [(place[widest] + 1) % values.shape[widest]] + place[widest + 1:]
    return values.at[tuple(place)].set(smallest).at[tuple(next_to)].set(largest)


def steps_of(rng, dims, cuts, smallest, high):
    def one(position, shards_of):
        draws = jax.random.uniform(jax.random.fold_in(jax.random.fold_in(rng, 6), position), (shards_of,), jnp.float32, smallest / len(cuts), high / len(cuts))
        return jnp.repeat(jnp.exp(draws), dims[position] // shards_of).reshape((-1,) + (1,) * (len(dims) - position - 1))

    gain = one(*cuts[0])
    for cut in cuts[1:]:
        gain = gain * one(*cut)
    return gain


def assign_block(stream_key, own, number, rows, amount, top, bound, skew):
    sequence = jax.random.permutation(stream_key, amount)
    heavy_load, ordinary = load_shares(amount, rows * top, bound, skew, True), load_shares(amount, rows * top, bound, skew, False)
    places = jnp.arange(amount)

    def named(tallies, offset_by):
        used = int((tallies > 0).sum())
        fixed = max(1, used // 4)
        moved = fixed + (places - fixed + offset_by * (used - fixed)) % max(1, amount - fixed)
        return jnp.zeros((amount,), jnp.int32).at[sequence[jnp.where(places < fixed, places, moved)]].set(jnp.asarray(tallies, jnp.int32))

    tallies = jnp.where(number % 4 == 0, named(heavy_load, number // 4), named(ordinary, number - number // 4 - 1))
    mixed = jax.random.permutation(jax.random.fold_in(own, 3), amount)
    source_of, sink = mixed[0:amount // 2 * 2:2], mixed[1:amount // 2 * 2:2]
    slack = jnp.minimum(tallies[source_of] - 1, bound - tallies[sink]) // 2
    slack = jnp.where((source_of == sequence[0]) | (sink == sequence[0]) | (tallies[sink] == 0), 0, jnp.maximum(slack, 0))
    moved = jax.random.randint(jax.random.fold_in(own, 4), (amount // 2,), 0, 1 << 20) % (slack + 1)
    tallies = tallies.at[source_of].add(-moved).at[sink].add(moved)
    members = jnp.searchsorted(jnp.cumsum(tallies), jnp.arange(rows * top), side="right").astype(jnp.int32)
    table = members.reshape(top, rows).T
    table = table[jax.random.permutation(jax.random.fold_in(own, 1), rows)]
    offset_by = jax.random.randint(jax.random.fold_in(own, 2), (rows, 1), 0, top)
    return jnp.take_along_axis(table, (jnp.arange(top)[None, :] + offset_by) % top, axis=1)


def load_shares(amount, total, bound, lean, full):
    portions = [(1 << 20) // math.isqrt(standing ** lean) + 1 for standing in range(1, amount + 1)]
    largest = bound if full else min(bound, max(-(-total // amount), total * portions[0] // sum(portions)))
    least = 1 if total - largest >= amount - 1 else 0
    counts, spare = [largest] + [least] * (amount - 1), total - largest - least * (amount - 1)
    while spare > 0:
        candidates = [i for i in range(1, amount) if counts[i] < largest] or [i for i in range(1, amount) if counts[i] < bound]
        whole, budget = sum([portions[i] for i in candidates]), spare
        for i in candidates:
            extra = min(bound - counts[i], max(1, budget * portions[i] // whole), spare)
            counts[i] = counts[i] + extra
            spare = spare - extra
    return np.array(counts)


def scatter_about(stream_key, dims, scale, limit, shards=(), held_as=jnp.bfloat16):
    values = jax.random.normal(stream_key, dims, jnp.float32) * scale
    if len(shards) > 0:
        values = steps_of(stream_key, dims, shards, -0.22, 0.18) * values
    return jnp.clip(values, min=-limit, max=limit).astype(held_as)


def setup_inputs(seed: int = 0) -> dict:
    key_list = jax.random.split(jax.random.key(seed), 7)
    target = draw_target(jax.random.fold_in(key_list[6], 71), 0)
    frag_brick_keys = jax.random.split(jax.random.fold_in(key_list[1], 1), FRAGS // F_DEV)
    frag_brick_turns = jax.random.permutation(jax.random.fold_in(key_list[1], 3), FRAGS // F_DEV)
    frag_brick = jax.vmap(lambda own, number: assign_block(jax.random.fold_in(key_list[1], 2), own, number, F_DEV, N_BRICK, 1, MOST, 2))(frag_brick_keys, frag_brick_turns).reshape((FRAGS, 1))
    bead_cell = plant(jax.random.randint(key_list[2], (FRAGS, BEADS), 0, CZ * CX * NY), jax.random.fold_in(key_list[2], 1), 0, (CZ * CX * NY) - 1).astype(jnp.int32)
    bead_weight = jnp.clip(jnp.exp(math.log(3.0) - 2.306499 * jax.random.uniform(key_list[3], (FRAGS, BEADS), jnp.float32) ** steps_of(key_list[3], (FRAGS, BEADS), ((0, 32),), -0.2, 0.2)), 0.29882812, 3.0).astype(jnp.bfloat16)
    bead_arm = scatter_about(key_list[4], (3, FRAGS, BEADS), 3.0, 12.0, ((1, 32),), jnp.float32)
    frag_angle = jnp.clip(jax.random.uniform(key_list[5], (3, FRAGS), jnp.float32, -3.140625, 3.140625), -3.140625, 3.140625)
    return dict(target=target, frag_brick=frag_brick, bead_cell=bead_cell, bead_weight=bead_weight, bead_arm=bead_arm, frag_angle=frag_angle)


SIGMA = 1.5
EPSILON = 1e-06

def kernel_values(half_width, derivative):
    offsets = np.arange(-half_width, half_width + 1) * 1.0
    gaussian = np.exp(-offsets ** 2 / (2.0 * SIGMA ** 2))
    gaussian = gaussian / gaussian.sum()
    if derivative:
        return -offsets / SIGMA ** 2 * gaussian
    return gaussian

def pass_taps(volume, along_dim, derivative):
    taps = kernel_values(KR, derivative)
    widths = [(KR, KR) if dim_id == along_dim else (0, 0) for dim_id in range(3)]
    widened = jnp.pad(volume, widths)
    out_len = volume.shape[along_dim]
    total = jnp.zeros(volume.shape, jnp.float32)
    for tap_id in range(2 * KR + 1):
        total = total + float(taps[2 * KR - tap_id]) * lax.slice_in_dim(widened, tap_id, tap_id + out_len, axis=along_dim)
    return total

def rotate_arms(angles, arms):
    cos_a, sin_a = (jnp.cos(angles[0]), jnp.sin(angles[0]))
    cos_b, sin_b = (jnp.cos(angles[1]), jnp.sin(angles[1]))
    cos_c, sin_c = (jnp.cos(angles[2]), jnp.sin(angles[2]))
    rot_rows = [[cos_a * cos_b, cos_a * sin_b * sin_c - sin_a * cos_c, cos_a * sin_b * cos_c + sin_a * sin_c], [sin_a * cos_b, sin_a * sin_b * sin_c + cos_a * cos_c, sin_a * sin_b * cos_c - cos_a * sin_c], [-sin_b, cos_b * sin_c, cos_b * cos_c]]
    return [sum((rot_rows[row_id][col_id][:, None] * arms[col_id] for col_id in range(3))) for row_id in range(3)]

def fragment_gradient(force, angles, arms):
    lever = rotate_arms(angles, arms)
    torque_x = lax.optimization_barrier(jnp.sum(lever[1] * force[2] - lever[2] * force[1], axis=1))
    torque_y = lax.optimization_barrier(jnp.sum(lever[2] * force[0] - lever[0] * force[2], axis=1))
    torque_z = lax.optimization_barrier(jnp.sum(lever[0] * force[1] - lever[1] * force[0], axis=1))
    return jnp.stack([lax.optimization_barrier(jnp.sum(force[0], axis=1)), lax.optimization_barrier(jnp.sum(force[1], axis=1)), lax.optimization_barrier(jnp.sum(force[2], axis=1)), torque_x, torque_y, torque_z])

def reference(target, frag_brick, bead_cell, bead_weight, bead_arm, frag_angle):
    frag_count = frag_brick.shape[0]
    layer = (jnp.arange(frag_count, dtype=jnp.int32) // F_DEV % N_RELAY).astype(jnp.int32)
    brick_of = frag_brick[:, 0].astype(jnp.int32)
    plane = layer[:, None] * CZ + bead_cell // (CX * NY)
    column = brick_of[:, None] * CX + bead_cell // NY % CX
    row_pos = bead_cell % NY
    flat_ids = ((plane * NX + column) * NY + row_pos).reshape(-1).astype(jnp.int32)
    weights = bead_weight.astype(jnp.float32)
    density = jnp.zeros((NZ * NX * NY,), jnp.float32).at[flat_ids].add(weights.reshape(-1)).reshape(NZ, NX, NY)
    model_map = pass_taps(pass_taps(pass_taps(density, 2, False), 1, False), 0, False)
    cross = jnp.sum(model_map * target)
    model_sq = jnp.sum(model_map * model_map)
    target_sq = jnp.sum(target * target)
    norm_model = jnp.sqrt(model_sq + EPSILON)
    norm_target = jnp.sqrt(target_sq + EPSILON)
    corr = cross / (norm_model * norm_target)
    scale = float(NX * NY * NZ)
    residual = scale * (target / (norm_model * norm_target) - corr * model_map / (norm_model * norm_model))
    along_z = pass_taps(residual, 0, False)
    slope_z = pass_taps(residual, 0, True)
    grad_x = pass_taps(pass_taps(along_z, 2, False), 1, True)
    grad_y = pass_taps(pass_taps(along_z, 2, True), 1, False)
    grad_z = pass_taps(pass_taps(slope_z, 2, False), 1, False)
    sampled = jnp.stack([grad_x.reshape(-1)[flat_ids], grad_y.reshape(-1)[flat_ids], grad_z.reshape(-1)[flat_ids]])
    force = sampled.reshape(3, frag_count, -1) * weights[None]
    return fragment_gradient(force, frag_angle, bead_arm)
```

```python
import functools

import jax
import jax.numpy as jnp
import numpy as np
from jax import lax
from jax.experimental import pallas as pl
from jax.experimental.pallas import tpu as pltpu
from jax.sharding import PartitionSpec as P

KR = 4
SIGMA = 1.5
EPSILON = 1e-06
HIGHEST = lax.Precision.HIGHEST
LO = 256
WEIGHT_SCALE = 512.0
LEVER_SCALE = 32768.0
LEVER_BIAS = 1 << 20
VMEM_BYTES = 48 << 20
F32 = jnp.float32
BF16 = jnp.bfloat16
I32 = jnp.int32


def taps_of(derivative):
    offsets = np.arange(-KR, KR + 1) * 1.0
    gaussian = np.exp(-(offsets**2) / (2.0 * SIGMA**2))
    gaussian = gaussian / gaussian.sum()
    if derivative:
        return -offsets / SIGMA**2 * gaussian
    return gaussian


def axis_matrix(length, derivative):
    offsets = np.arange(length)[:, None] - np.arange(length)[None, :]
    return np.where(
        np.abs(offsets) <= KR, taps_of(derivative)[np.clip(offsets + KR, 0, 2 * KR)], 0.0
    )


def columns_at(matrix, rows, wanted):
    inside = (wanted >= 0) & (wanted < matrix.shape[1])
    picked = matrix[rows][:, np.clip(wanted, 0, matrix.shape[1] - 1)]
    return np.where(inside[None, :], picked, 0.0)


def unique_tables(tables):
    flat = np.stack([t.reshape(-1) for t in tables])
    kept, inverse = np.unique(np.round(flat, 14), axis=0, return_inverse=True)
    return kept.reshape((-1,) + tables[0].shape), inverse.reshape(-1).astype(np.int32)


def pieces_np(table):
    import ml_dtypes

    high = table.astype(np.float32).astype(ml_dtypes.bfloat16)
    low = (table - high.astype(np.float64)).astype(ml_dtypes.bfloat16)
    return np.concatenate([high, high, low], axis=-1)


def weight_table(z_kinds, x_kinds, z_len, z_count, z_blocks, x_len, x_count, x_parts):
    z_tables = []
    for r in range(z_count):
        wanted = np.concatenate([np.arange(z_len) + z_len * block for block in z_blocks(r)])
        rows = np.arange(z_len) + z_len * r
        z_tables.append(np.stack([columns_at(m, rows, wanted) for m in z_kinds]))
    x_tables = []
    for b in range(x_count):
        wanted = np.concatenate([x_len * b + part for part in x_parts])
        rows = np.arange(x_len) + x_len * b
        x_tables.append(np.stack([columns_at(m, rows, wanted) for m in x_kinds]))
    z_tables, z_inverse = unique_tables(z_tables)
    x_tables, x_inverse = unique_tables(x_tables)
    kinds = len(z_kinds)
    parts, start = [], 0
    for part in x_parts:
        piece = x_tables[:, :, :, start : start + len(part)]
        start += len(part)
        full = np.einsum("rkzi,bkxj->rbkzxij", z_tables, piece)
        parts.append(
            full.reshape(len(z_tables) * len(x_tables), kinds * z_len * x_len, -1)
        )
    table = pieces_np(np.concatenate(parts, axis=-1))
    return table, z_inverse, x_inverse, len(x_tables)


def eye_column(row, eye):
    return jnp.sum(jnp.where(eye, row, jnp.zeros_like(row)), axis=1, keepdims=True)


def pack_kernel(most, lines, row_count, brick_ref, cell_ref, weight_ref, arm_ref, angle_ref, out_ref):
    frags, beads = cell_ref.shape
    slots = out_ref.shape[0]
    sub = lax.broadcasted_iota(I32, (frags, frags), 0)
    lane = lax.broadcasted_iota(I32, (frags, frags), 1)
    eye = sub == lane
    col = brick_ref[...]
    row = jnp.sum(jnp.where(eye, col, 0), axis=0, keepdims=True)
    earlier = jnp.logical_and(col == row, sub < lane)
    rank = jnp.sum(jnp.where(earlier, 1, 0), axis=0, keepdims=True)
    slot = row * most + rank
    place = jnp.where(lax.broadcasted_iota(I32, (slots, frags), 0) == slot, 1.0, 0.0).astype(F32)

    angles = angle_ref[...]
    cos, sin = jnp.cos(angles), jnp.sin(angles)
    cos_a, cos_b, cos_c = cos[0:1], cos[1:2], cos[2:3]
    sin_a, sin_b, sin_c = sin[0:1], sin[1:2], sin[2:3]
    turn = [
        [cos_a * cos_b, cos_a * sin_b * sin_c - sin_a * cos_c, cos_a * sin_b * cos_c + sin_a * sin_c],
        [sin_a * cos_b, sin_a * sin_b * sin_c + cos_a * cos_c, sin_a * sin_b * cos_c - cos_a * sin_c],
        [-sin_b, cos_b * sin_c, cos_b * cos_c],
    ]
    levers = []
    for i in range(3):
        total = eye_column(turn[i][0], eye) * arm_ref[0]
        for j in (1, 2):
            total = total + eye_column(turn[i][j], eye) * arm_ref[j]
        levers.append(jnp.round(total * LEVER_SCALE))

    cell = cell_ref[...]
    line = ((cell.astype(F32) + 0.5) * (1.0 / row_count)).astype(I32)
    y = cell - line * row_count
    code = (((y // LO) * lines + line) * LO + (y % LO)).astype(F32)
    weight = weight_ref[...].astype(F32) * WEIGHT_SCALE
    payload = jnp.concatenate([code, weight] + levers, axis=1)
    placed = jnp.dot(place, payload, precision=HIGHEST, preferred_element_type=F32)
    placed = placed.astype(I32)
    code, weight, lx, ly, lz = [placed[:, k * beads : (k + 1) * beads] for k in range(5)]
    lz = lz + LEVER_BIAS
    out_ref[:, 0:beads] = code | (weight << 16)
    out_ref[:, beads : 2 * beads] = (lx << 11) | (lz >> 10)
    out_ref[:, 2 * beads : 3 * beads] = (ly << 11) | (lz & 1023)


def splat_kernel(lines, rb, got_ref, out_ref, acc_ref):
    slots = got_ref.shape[0]
    beads = got_ref.shape[1] // 3
    his = acc_ref.shape[0]
    acc_ref[...] = jnp.zeros_like(acc_ref)
    hi_iota = lax.broadcasted_iota(I32, (his, beads), 0)
    lo_iota = lax.broadcasted_iota(I32, (LO, beads), 0)

    def body(i, carry):
        word = got_ref[pl.ds(i * rb, rb), 0:beads]
        lo = word & (LO - 1)
        hi = (word >> 8) & 255
        weight = (word >> 16).astype(F32) * (1.0 / WEIGHT_SCALE)
        left, right = [], []
        for q in range(rb):
            left.append(jnp.where(hi_iota == hi[q : q + 1], weight[q : q + 1], 0.0).astype(BF16))
            right.append(jnp.where(lo_iota == lo[q : q + 1], 1.0, 0.0).astype(BF16))
        acc_ref[...] += lax.dot_general(
            jnp.concatenate(left, axis=1),
            jnp.concatenate(right, axis=1),
            (((1,), (1,)), ((), ())),
            preferred_element_type=F32,
        )
        return carry

    lax.fori_loop(0, slots // rb, body, 0)
    for yh in range(his // lines):
        out_ref[:, yh * LO : (yh + 1) * LO] = acc_ref[yh * lines : (yh + 1) * lines, :]


def line_blur(value, derivative):
    taps = taps_of(derivative)
    rows, length = value.shape
    wide = jnp.concatenate([value, jnp.zeros((rows, 128), F32)], axis=1)
    total = None if derivative else float(taps[KR]) * value
    for d in range(1, KR + 1):
        up = pltpu.roll(wide, d, 1)[:, :length]
        down = pltpu.roll(wide, length + 128 - d, 1)[:, :length]
        pair = up - down if derivative else up + down
        term = float(taps[KR + d]) * pair
        total = term if total is None else total + term
    return total


def split(value):
    high = value.astype(BF16)
    low = (value - high.astype(F32)).astype(BF16)
    return high, low


def mix_lines(table_ref, parts):
    value = jnp.concatenate(parts, axis=0)
    high, low = split(value)
    return jnp.dot(
        table_ref[0], jnp.concatenate([high, low, high], axis=0), preferred_element_type=F32
    )


def store_fields(fields, lines, out_ref):
    his = fields[0].shape[1] // LO * lines
    for k, field in enumerate(fields):
        for yh in range(field.shape[1] // LO):
            high, low = split(field[:, yh * LO : (yh + 1) * LO])
            rows = slice(k * his + yh * lines, k * his + (yh + 1) * lines)
            out_ref[rows, 0:LO] = high
            out_ref[rows, LO : 2 * LO] = low


def target_kernel(lines, count, _, table_ref, *refs):
    parts, out_ref = refs[:count], refs[count]
    mixed = mix_lines(table_ref, [ref[...] for ref in parts])
    grad_x = line_blur(mixed[0:lines], False)
    grad_y = line_blur(mixed[lines : 2 * lines], True)
    grad_z = line_blur(mixed[2 * lines : 3 * lines], False)
    store_fields([grad_x, grad_y, grad_z], lines, out_ref)


def model_kernel(lines, count, _, table_ref, target_ref, *refs):
    parts, out_ref, sum_ref = refs[:count], refs[count], refs[count + 1]
    mixed = mix_lines(table_ref, [ref[...] for ref in parts])
    smooth = line_blur(mixed, False)
    model = smooth[3 * lines :]
    target = target_ref[...]
    sums = [jnp.sum(model * target), jnp.sum(model * model), jnp.sum(target * target)]
    lane = lax.broadcasted_iota(I32, sum_ref.shape, 1)
    total = jnp.zeros(sum_ref.shape, F32)
    for k, value in enumerate(sums):
        total = jnp.where(lane == k, value, total)
    sum_ref[...] = total
    grad_x = line_blur(smooth[0:lines], False)
    grad_y = line_blur(smooth[lines : 2 * lines], True)
    grad_z = line_blur(smooth[2 * lines : 3 * lines], False)
    store_fields([grad_x, grad_y, grad_z], lines, out_ref)


def sample_kernel(his, rb, got_ref, field_ref, out_ref, force_ref):
    slots = got_ref.shape[0]
    beads = got_ref.shape[1] // 3
    lo_iota = lax.broadcasted_iota(I32, (LO, beads), 0)
    sub_iota = lax.broadcasted_iota(I32, (8, beads), 0)

    def body(i, carry):
        word = got_ref[pl.ds(i * rb, rb), 0:beads]
        lo = word & (LO - 1)
        hi = (word >> 8) & 255
        picks = [
            jnp.where(lo_iota == lo[q : q + 1], 1.0, 0.0).astype(BF16) for q in range(rb)
        ]
        pick = jnp.concatenate(picks, axis=1)
        sampled = jnp.dot(
            field_ref[...], jnp.concatenate([pick, pick], axis=0), preferred_element_type=F32
        )
        for q in range(rb):
            own = jnp.broadcast_to(hi[q : q + 1], (8, beads))
            group, within = own >> 3, (own & 7) == sub_iota
            found = [jnp.zeros((8, beads), F32)] * 3
            for j in range(his // 8):
                here = group == j
                for k in range(3):
                    rows = slice(k * his + 8 * j, k * his + 8 * j + 8)
                    found[k] = jnp.where(
                        here, sampled[rows, q * beads : (q + 1) * beads], found[k]
                    )
            for k in range(3):
                value = jnp.sum(jnp.where(within, found[k], 0.0), axis=0, keepdims=True)
                force_ref[k, pl.ds(i * rb + q, 1), :] = value
        return carry

    lax.fori_loop(0, slots // rb, body, 0)
    first, second = got_ref[:, beads : 2 * beads], got_ref[:, 2 * beads : 3 * beads]
    weight = (got_ref[:, 0:beads] >> 16).astype(F32) * (1.0 / WEIGHT_SCALE)
    lever_z = (((first & 2047) << 10) | (second & 1023)) - LEVER_BIAS
    levers = [
        v.astype(F32) * (1.0 / LEVER_SCALE) for v in (first >> 11, second >> 11, lever_z)
    ]
    force = [force_ref[k] * weight for k in range(3)]
    terms = force + [
        levers[1] * force[2] - levers[2] * force[1],
        levers[2] * force[0] - levers[0] * force[2],
        levers[0] * force[1] - levers[1] * force[0],
    ]
    lane = lax.broadcasted_iota(I32, out_ref.shape, 1)
    total = jnp.zeros(out_ref.shape, F32)
    for k, term in enumerate(terms):
        total = jnp.where(lane == k, jnp.sum(term, axis=1, keepdims=True), total)
    out_ref[...] = total


def return_kernel(target_ref, model_ref, sum_ref, out_ref):
    lane = lax.broadcasted_iota(I32, out_ref.shape, 1)
    sums = sum_ref[0:1, :]
    for k in range(1, sum_ref.shape[0] // 8):
        sums = sums + sum_ref[8 * k : 8 * k + 1, :]
    total = jnp.where(lane < 6, target_ref[...], 0.0)
    total = jnp.where((lane >= 8) & (lane < 14), pltpu.roll(model_ref[...], 8, 1), total)
    out_ref[...] = jnp.where(lane >= 16, pltpu.roll(sums, 16, 1), total)


def finish_kernel(most, voxel_total, brick_ref, back_ref, out_ref):
    frags = out_ref.shape[1]
    slots = back_ref.shape[0]
    sub = lax.broadcasted_iota(I32, (frags, frags), 0)
    lane = lax.broadcasted_iota(I32, (frags, frags), 1)
    col = brick_ref[...]
    row = jnp.sum(jnp.where(sub == lane, col, 0), axis=0, keepdims=True)
    earlier = jnp.logical_and(col == row, sub < lane)
    rank = jnp.sum(jnp.where(earlier, 1, 0), axis=0, keepdims=True)
    slot = row * most + rank
    place = jnp.where(lax.broadcasted_iota(I32, (slots, frags), 0) == slot, 1.0, 0.0).astype(F32)
    back = back_ref[...]
    first = lax.broadcasted_iota(I32, (slots, 128), 0) % most == 0
    sums = jnp.sum(jnp.where(first, back, 0.0), axis=0, keepdims=True)
    cross, model_sq, target_sq = sums[:, 16:17], sums[:, 17:18], sums[:, 18:19]
    norm_model = jnp.sqrt(model_sq + EPSILON)
    norm_target = jnp.sqrt(target_sq + EPSILON)
    corr = cross / (norm_model * norm_target)
    scale_target = voxel_total / (norm_model * norm_target)
    scale_model = voxel_total * corr / (norm_model * norm_model)
    mine = lax.dot_general(
        back, place, (((0,), (0,)), ((), ())), precision=HIGHEST, preferred_element_type=F32
    )
    out_ref[...] = scale_target * mine[0:6] - scale_model * mine[8:14]


def call(kernel, out_shape, *args, scratch=(), name=None):
    return pl.pallas_call(
        kernel,
        out_shape=out_shape,
        scratch_shapes=list(scratch),
        compiler_params=pltpu.CompilerParams(vmem_limit_bytes=VMEM_BYTES),
        name=name,
    )(*args)


def call_at(kernel, out_shape, index, table, *args, name=None):
    def whole(shape):
        return pl.BlockSpec(shape, lambda i, s: (0,) * len(shape))

    single = not isinstance(out_shape, list)
    outs = [out_shape] if single else out_shape
    specs = [whole(o.shape) for o in outs]
    return pl.pallas_call(
        kernel,
        out_shape=out_shape,
        grid_spec=pltpu.PrefetchScalarGridSpec(
            num_scalar_prefetch=1,
            grid=(1,),
            in_specs=[pl.BlockSpec((1,) + table.shape[1:], lambda i, s: (s[0], 0, 0))]
            + [whole(a.shape) for a in args],
            out_specs=specs[0] if single else specs,
        ),
        compiler_params=pltpu.CompilerParams(vmem_limit_bytes=VMEM_BYTES),
        name=name,
    )(index, table, *args)


def shifted(value, axis, step):
    size = lax.axis_size(axis)
    pairs = [(i, i + step) for i in range(size) if 0 <= i + step < size]
    return lax.ppermute(value, axis, pairs)


def relay_blocks(value, reach):
    size = lax.axis_size("relay")
    if size == 2:
        return [value, lax.ppermute(value, "relay", [(0, 1), (1, 0)])]
    blocks = [value]
    for step in range(1, min(reach, size - 1) + 1):
        blocks += [shifted(value, "relay", step), shifted(value, "relay", -step)]
    return blocks


def relay_order(size, reach):
    if size == 2:
        return lambda r: [r, 1 - r]
    steps = [0]
    for step in range(1, min(reach, size - 1) + 1):
        steps += [-step, step]
    return lambda r: [r + s for s in steps]


def relay_total(value):
    size = lax.axis_size("relay")
    values, moving = [value], value
    for _ in range(size - 1):
        moving = lax.ppermute(moving, "relay", [(i, (i + 1) % size) for i in range(size)])
        values.append(moving)
    return jnp.concatenate(values, axis=0)


def shards(target, frag_brick, bead_cell, bead_weight, bead_arm, frag_angle):
    brick_count, relay_count = lax.axis_size("brick"), lax.axis_size("relay")
    frags, beads = bead_cell.shape
    planes, columns, rows = target.shape
    lines = planes * columns
    his = lines * (rows // LO)
    assert rows % LO == 0 and his <= 256 and columns >= 2 * KR
    voxel_total = float(brick_count * columns * relay_count * planes * rows)
    most = max(2, 2 * frags // brick_count)
    slots = brick_count * most

    z_total, x_total = relay_count * planes, brick_count * columns
    gz, dz = axis_matrix(z_total, False), axis_matrix(z_total, True)
    gx, dx = axis_matrix(x_total, False), axis_matrix(x_total, True)
    reach_one, reach_two = -(-KR // planes), -(-2 * KR // planes)
    target_table, tz, tx, tn = weight_table(
        [gz, gz, dz], [dx, gx, gx], planes, relay_count, relay_order(relay_count, reach_one),
        columns, brick_count,
        [np.arange(columns), np.arange(-KR, 0), np.arange(columns, columns + KR)],
    )
    model_table, mz, mx, mn = weight_table(
        [gz @ gz, gz @ gz, dz @ gz, gz], [dx @ gx, gx @ gx, gx @ gx, gx],
        planes, relay_count, relay_order(relay_count, reach_two), columns, brick_count,
        [np.arange(columns), np.arange(-columns, 0), np.arange(columns, 2 * columns)],
    )
    r, b = lax.axis_index("relay"), lax.axis_index("brick")
    target_index = (jnp.asarray(tz)[r] * tn + jnp.asarray(tx)[b]).reshape(1)
    model_index = (jnp.asarray(mz)[r] * mn + jnp.asarray(mx)[b]).reshape(1)

    target_lines = target.reshape(lines, rows)
    target_blocks = relay_blocks(target, reach_one)
    left_edge = jnp.concatenate([t[:, columns - KR :] for t in target_blocks], axis=0)
    right_edge = jnp.concatenate([t[:, :KR] for t in target_blocks], axis=0)
    from_left = shifted(left_edge.reshape(-1, rows), "brick", 1)
    from_right = shifted(right_edge.reshape(-1, rows), "brick", -1)
    target_parts = [t.reshape(lines, rows) for t in target_blocks] + [from_left, from_right]

    sent = call(
        functools.partial(pack_kernel, most, lines, rows),
        jax.ShapeDtypeStruct((slots, 3 * beads), I32),
        frag_brick, bead_cell, bead_weight, bead_arm, frag_angle,
        name="pack",
    )
    got = lax.all_to_all(sent, "brick", split_axis=0, concat_axis=0, tiled=True)
    density = call(
        functools.partial(splat_kernel, lines, 8),
        jax.ShapeDtypeStruct((lines, rows), F32),
        got,
        scratch=[pltpu.VMEM((his, LO), F32)],
        name="splat",
    )
    blocks = jnp.concatenate(relay_blocks(density, reach_two), axis=0)
    model_parts = [blocks, shifted(blocks, "brick", 1), shifted(blocks, "brick", -1)]

    field_shape = jax.ShapeDtypeStruct((3 * his, 2 * LO), BF16)

    def sample(field, name):
        return call(
            functools.partial(sample_kernel, his, 8),
            jax.ShapeDtypeStruct((slots, 128), F32),
            got, field,
            scratch=[pltpu.VMEM((3, slots, beads), F32)],
            name=name,
        )

    target_field = call_at(
        functools.partial(target_kernel, lines, len(target_parts)),
        field_shape, target_index, jnp.asarray(target_table), *target_parts,
        name="target_fields",
    )
    target_sums = sample(target_field, "target_sample")
    model_field, partial = call_at(
        functools.partial(model_kernel, lines, len(model_parts)),
        [field_shape, jax.ShapeDtypeStruct((8, 128), F32)],
        model_index, jnp.asarray(model_table), target_lines, *model_parts,
        name="model_fields",
    )
    partials = relay_total(partial)
    model_sums = sample(model_field, "model_sample")
    leaving = call(
        return_kernel, jax.ShapeDtypeStruct((slots, 128), F32), target_sums, model_sums, partials,
        name="join",
    )
    back = lax.all_to_all(leaving, "brick", split_axis=0, concat_axis=0, tiled=True)
    return call(
        functools.partial(finish_kernel, most, voxel_total),
        jax.ShapeDtypeStruct((6, frags), F32),
        frag_brick, back,
        name="finish",
    )


def solution(mesh):
    placed = (
        P("relay", "brick", None),
        P(("brick", "relay"), None),
        P(("brick", "relay"), None),
        P(("brick", "relay"), None),
        P(None, ("brick", "relay"), None),
        P(None, ("brick", "relay")),
    )
    return jax.shard_map(
        shards, mesh=mesh, in_specs=placed, out_specs=P(None, ("brick", "relay")), check_vma=False
    )
```

```python
import functools

import jax
import jax.numpy as jnp
import numpy as np
from jax import lax
from jax.experimental import pallas as pl
from jax.experimental.pallas import tpu as pltpu
from jax.sharding import PartitionSpec as P

KR = 4
SIGMA = 1.5
EPSILON = 1e-06
HIGHEST = lax.Precision.HIGHEST
LO = 256
FIELDS = 16
WEIGHT_SCALE = 512.0
LEVER_SCALE = 32768.0
LEVER_BIAS = 1 << 20
VMEM_BYTES = 48 << 20
F32 = jnp.float32
BF16 = jnp.bfloat16
I32 = jnp.int32


def taps_of(derivative):
    offsets = np.arange(-KR, KR + 1) * 1.0
    gaussian = np.exp(-(offsets**2) / (2.0 * SIGMA**2))
    gaussian = gaussian / gaussian.sum()
    if derivative:
        return -offsets / SIGMA**2 * gaussian
    return gaussian


def axis_matrix(length, derivative):
    offsets = np.arange(length)[:, None] - np.arange(length)[None, :]
    return np.where(
        np.abs(offsets) <= KR, taps_of(derivative)[np.clip(offsets + KR, 0, 2 * KR)], 0.0
    )


def columns_at(matrix, rows, wanted):
    inside = (wanted >= 0) & (wanted < matrix.shape[1])
    picked = matrix[rows][:, np.clip(wanted, 0, matrix.shape[1] - 1)]
    return np.where(inside[None, :], picked, 0.0)


def unique_tables(tables):
    flat = np.stack([t.reshape(-1) for t in tables])
    kept, inverse = np.unique(np.round(flat, 14), axis=0, return_inverse=True)
    return kept.reshape((-1,) + tables[0].shape), inverse.reshape(-1).astype(np.int32)


def pieces_np(table):
    import ml_dtypes

    high = table.astype(np.float32).astype(ml_dtypes.bfloat16)
    low = (table - high.astype(np.float64)).astype(ml_dtypes.bfloat16)
    return np.concatenate([high, high, low], axis=-1)


def weight_table(z_kinds, x_kinds, z_len, z_count, z_blocks, x_len, x_count, x_parts):
    z_tables = []
    for r in range(z_count):
        wanted = np.concatenate([np.arange(z_len) + z_len * block for block in z_blocks(r)])
        rows = np.arange(z_len) + z_len * r
        z_tables.append(np.stack([columns_at(m, rows, wanted) for m in z_kinds]))
    x_tables = []
    for b in range(x_count):
        wanted = np.concatenate([x_len * b + part for part in x_parts])
        rows = np.arange(x_len) + x_len * b
        x_tables.append(np.stack([columns_at(m, rows, wanted) for m in x_kinds]))
    z_tables, z_inverse = unique_tables(z_tables)
    x_tables, x_inverse = unique_tables(x_tables)
    kinds = len(z_kinds)
    parts, start = [], 0
    for part in x_parts:
        piece = x_tables[:, :, :, start : start + len(part)]
        start += len(part)
        full = np.einsum("rkzi,bkxj->rbkzxij", z_tables, piece)
        parts.append(
            full.reshape(len(z_tables) * len(x_tables), kinds * z_len * x_len, -1)
        )
    table = pieces_np(np.concatenate(parts, axis=-1))
    return table, z_inverse, x_inverse, len(x_tables)


def eye_column(row, eye):
    return jnp.sum(jnp.where(eye, row, jnp.zeros_like(row)), axis=1, keepdims=True)


def slot_row(row, most):
    frags = row.shape[1]
    sub = lax.broadcasted_iota(I32, (frags, frags), 0)
    lane = lax.broadcasted_iota(I32, (frags, frags), 1)
    eye = sub == lane
    earlier = jnp.logical_and(eye_column(row, eye) == row, sub < lane)
    return jnp.sum(jnp.where(earlier, 1, 0), axis=0, keepdims=True), eye


def pack_kernel(
    most, lines, row_count, brick_ref, angle_ref, cell_in, weight_in, arm_in, out_ref,
    cell_ref, weight_ref, arm_ref, sems,
):
    copies = [
        pltpu.make_async_copy(source, target, sems.at[k])
        for k, (source, target) in enumerate(
            [(cell_in, cell_ref), (weight_in, weight_ref), (arm_in, arm_ref)]
        )
    ]
    for copy in copies:
        copy.start()
    frags, beads = cell_ref.shape
    slots = out_ref.shape[0]
    row = brick_ref[...]
    rank, eye = slot_row(row, most)
    slot = row * most + rank
    place = jnp.where(lax.broadcasted_iota(I32, (slots, frags), 0) == slot, 1.0, 0.0).astype(F32)

    angles = angle_ref[...]
    cos, sin = jnp.cos(angles), jnp.sin(angles)
    cos_a, cos_b, cos_c = cos[0:1], cos[1:2], cos[2:3]
    sin_a, sin_b, sin_c = sin[0:1], sin[1:2], sin[2:3]
    turn = [
        [cos_a * cos_b, cos_a * sin_b * sin_c - sin_a * cos_c, cos_a * sin_b * cos_c + sin_a * sin_c],
        [sin_a * cos_b, sin_a * sin_b * sin_c + cos_a * cos_c, sin_a * sin_b * cos_c - cos_a * sin_c],
        [-sin_b, cos_b * sin_c, cos_b * cos_c],
    ]
    turn = [[eye_column(value, eye) for value in values] for values in turn]
    for copy in copies:
        copy.wait()
    levers = []
    for i in range(3):
        total = turn[i][0] * arm_ref[0]
        for j in (1, 2):
            total = total + turn[i][j] * arm_ref[j]
        levers.append(jnp.round(total * LEVER_SCALE))

    cell = cell_ref[...]
    line = ((cell.astype(F32) + 0.5) * (1.0 / row_count)).astype(I32)
    y = cell - line * row_count
    code = (((y // LO) * lines + line) * LO + (y % LO)).astype(F32)
    weight = weight_ref[...].astype(F32) * WEIGHT_SCALE
    payload = jnp.concatenate([code, weight] + levers, axis=1)
    placed = jnp.dot(place, payload, precision=HIGHEST, preferred_element_type=F32)
    placed = placed.astype(I32)
    code, weight, lx, ly, lz = [placed[:, k * beads : (k + 1) * beads] for k in range(5)]
    lz = lz + LEVER_BIAS
    out_ref[:, 0:beads] = code | (weight << 16)
    out_ref[:, beads : 2 * beads] = (lx << 11) | (lz >> 10)
    out_ref[:, 2 * beads : 3 * beads] = (ly << 11) | (lz & 1023)


def line_blur(value, derivative):
    taps = taps_of(derivative)
    rows, length = value.shape
    wide = jnp.concatenate([value, jnp.zeros((rows, 128), F32)], axis=1)
    total = None if derivative else float(taps[KR]) * value
    for d in range(1, KR + 1):
        up = pltpu.roll(wide, d, 1)[:, :length]
        down = pltpu.roll(wide, length + 128 - d, 1)[:, :length]
        pair = up - down if derivative else up + down
        term = float(taps[KR + d]) * pair
        total = term if total is None else total + term
    return total


def splat_kernel(lines, rb, got_ref, out_ref, acc_ref):
    slots = got_ref.shape[0]
    beads = got_ref.shape[1] // 3
    his = acc_ref.shape[0]
    acc_ref[...] = jnp.zeros_like(acc_ref)
    hi_iota = lax.broadcasted_iota(I32, (his, beads), 0)
    lo_iota = lax.broadcasted_iota(I32, (LO, beads), 0)

    def body(i, carry):
        word = got_ref[pl.ds(i * rb, rb), 0:beads]
        lo = word & (LO - 1)
        hi = (word >> 8) & 255
        weight = (word >> 16).astype(F32) * (1.0 / WEIGHT_SCALE)
        left, right = [], []
        for q in range(rb):
            left.append(jnp.where(hi_iota == hi[q : q + 1], weight[q : q + 1], 0.0).astype(BF16))
            right.append(jnp.where(lo_iota == lo[q : q + 1], 1.0, 0.0).astype(BF16))
        acc_ref[...] += lax.dot_general(
            jnp.concatenate(left, axis=1),
            jnp.concatenate(right, axis=1),
            (((1,), (1,)), ((), ())),
            preferred_element_type=F32,
        )
        return carry

    lax.fori_loop(0, slots // rb, body, 0)
    density = [acc_ref[yh * lines : (yh + 1) * lines, :] for yh in range(his // lines)]
    out_ref[...] = line_blur(jnp.concatenate(density, axis=1), False)


def split(value):
    high = value.astype(BF16)
    low = (value - high.astype(F32)).astype(BF16)
    return high, low


def mix_lines(table_ref, parts):
    value = jnp.concatenate(parts, axis=0)
    high, low = split(value)
    return jnp.dot(
        table_ref[0], jnp.concatenate([high, low, high], axis=0), preferred_element_type=F32
    )


def store_fields(fields, lines, out_ref):
    his = fields[0].shape[1] // LO * lines
    for k, field in enumerate(fields):
        for yh in range(field.shape[1] // LO):
            high, low = split(field[:, yh * LO : (yh + 1) * LO])
            rows = slice(k * his + yh * lines, k * his + (yh + 1) * lines)
            out_ref[rows, 0:LO] = high
            out_ref[rows, LO : 2 * LO] = low


def target_kernel(lines, count, _, table_ref, *refs):
    parts, out_ref = refs[:count], refs[count]
    mixed = mix_lines(table_ref, [ref[...] for ref in parts])
    grad_x = line_blur(mixed[0:lines], False)
    grad_y = line_blur(mixed[lines : 2 * lines], True)
    grad_z = line_blur(mixed[2 * lines : 3 * lines], False)
    store_fields([grad_x, grad_y, grad_z], lines, out_ref)


def model_kernel(lines, count, _, table_ref, target_ref, *refs):
    parts, out_ref, sum_ref = refs[:count], refs[count], refs[count + 1]
    smooth = mix_lines(table_ref, [ref[...] for ref in parts])
    model = smooth[3 * lines :]
    target = target_ref[...]
    sums = [jnp.sum(model * target), jnp.sum(model * model), jnp.sum(target * target)]
    lane = lax.broadcasted_iota(I32, sum_ref.shape, 1)
    total = jnp.zeros(sum_ref.shape, F32)
    for k, value in enumerate(sums):
        total = jnp.where(lane == k, value, total)
    sum_ref[...] = total
    grad_x = line_blur(smooth[0:lines], False)
    grad_y = line_blur(smooth[lines : 2 * lines], True)
    grad_z = line_blur(smooth[2 * lines : 3 * lines], False)
    store_fields([grad_x, grad_y, grad_z], lines, out_ref)


def sample_kernel(his, rb, got_ref, field_ref, out_ref, force_ref):
    slots = got_ref.shape[0]
    beads = got_ref.shape[1] // 3
    lo_iota = lax.broadcasted_iota(I32, (LO, beads), 0)
    sub_iota = lax.broadcasted_iota(I32, (8, beads), 0)

    def body(i, carry):
        word = got_ref[pl.ds(i * rb, rb), 0:beads]
        lo = word & (LO - 1)
        hi = (word >> 8) & 255
        picks = [
            jnp.where(lo_iota == lo[q : q + 1], 1.0, 0.0).astype(BF16) for q in range(rb)
        ]
        pick = jnp.concatenate(picks, axis=1)
        sampled = jnp.dot(
            field_ref[...], jnp.concatenate([pick, pick], axis=0), preferred_element_type=F32
        )
        for q in range(rb):
            own = jnp.broadcast_to(hi[q : q + 1], (8, beads))
            group, within = own >> 3, (own & 7) == sub_iota
            found = [jnp.zeros((8, beads), F32)] * 3
            for j in range(his // 8):
                here = group == j
                for k in range(3):
                    rows = slice(k * his + 8 * j, k * his + 8 * j + 8)
                    found[k] = jnp.where(
                        here, sampled[rows, q * beads : (q + 1) * beads], found[k]
                    )
            for k in range(3):
                value = jnp.sum(jnp.where(within, found[k], 0.0), axis=0, keepdims=True)
                force_ref[k, pl.ds(i * rb + q, 1), :] = value
        return carry

    lax.fori_loop(0, slots // rb, body, 0)
    first, second = got_ref[:, beads : 2 * beads], got_ref[:, 2 * beads : 3 * beads]
    weight = (got_ref[:, 0:beads] >> 16).astype(F32) * (1.0 / WEIGHT_SCALE)
    lever_z = (((first & 2047) << 10) | (second & 1023)) - LEVER_BIAS
    levers = [
        v.astype(F32) * (1.0 / LEVER_SCALE) for v in (first >> 11, second >> 11, lever_z)
    ]
    force = [force_ref[k] * weight for k in range(3)]
    terms = force + [
        levers[1] * force[2] - levers[2] * force[1],
        levers[2] * force[0] - levers[0] * force[2],
        levers[0] * force[1] - levers[1] * force[0],
    ]
    lane = lax.broadcasted_iota(I32, out_ref.shape, 1)
    total = jnp.zeros(out_ref.shape, F32)
    for k, term in enumerate(terms):
        total = jnp.where(lane == k, jnp.sum(term, axis=1, keepdims=True), total)
    out_ref[...] = total


def join_kernel(most, target_ref, model_ref, sum_ref, out_ref):
    bricks = out_ref.shape[0]
    lane = lax.broadcasted_iota(I32, out_ref.shape, 1)
    sums = sum_ref[0:1, :]
    for k in range(1, sum_ref.shape[0] // 8):
        sums = sums + sum_ref[8 * k : 8 * k + 1, :]
    total = jnp.zeros(out_ref.shape, F32)
    for k in range(most):
        rows = pl.ds(k, bricks, stride=most)
        own = jnp.where(lane < 6, target_ref[rows, :], 0.0)
        own = own + pltpu.roll(jnp.where(lane < 6, model_ref[rows, :], 0.0), 6, 1)
        if k == 0:
            own = own + pltpu.roll(jnp.where(lane < 3, sums, 0.0), 12, 1)
        total = total + (pltpu.roll(own, FIELDS * k, 1) if k else own)
    out_ref[...] = total


def finish_kernel(most, voxel_total, brick_ref, back_ref, out_ref):
    frags = out_ref.shape[1]
    bricks = back_ref.shape[0]
    row = brick_ref[...]
    rank, _ = slot_row(row, most)
    place = jnp.where(lax.broadcasted_iota(I32, (bricks, frags), 0) == row, 1.0, 0.0).astype(F32)
    back = back_ref[...]
    sums = jnp.sum(back, axis=0, keepdims=True)
    cross, model_sq, target_sq = sums[:, 12:13], sums[:, 13:14], sums[:, 14:15]
    norm_model = jnp.sqrt(model_sq + EPSILON)
    norm_target = jnp.sqrt(target_sq + EPSILON)
    corr = cross / (norm_model * norm_target)
    scale_target = voxel_total / (norm_model * norm_target)
    scale_model = voxel_total * corr / (norm_model * norm_model)
    found = lax.dot_general(
        back, place, (((0,), (0,)), ((), ())), precision=HIGHEST, preferred_element_type=F32
    )
    mine = jnp.zeros((FIELDS, frags), F32)
    for k in range(most):
        mine = jnp.where(rank == k, found[FIELDS * k : FIELDS * (k + 1)], mine)
    out_ref[...] = scale_target * mine[0:6] - scale_model * mine[6:12]


def cost(macs, nbytes):
    return pl.CostEstimate(flops=2 * macs, bytes_accessed=nbytes, transcendentals=0)


def call(kernel, out_shape, *args, scratch=(), name=None, macs=0, in_specs=None):
    kwargs = {} if in_specs is None else {"in_specs": in_specs}
    return pl.pallas_call(
        kernel,
        out_shape=out_shape,
        scratch_shapes=list(scratch),
        compiler_params=pltpu.CompilerParams(vmem_limit_bytes=VMEM_BYTES),
        cost_estimate=cost(macs, 4 * sum(a.size for a in args)),
        name=name,
        **kwargs,
    )(*args)


def call_at(kernel, out_shape, index, table, *args, name=None, macs=0):
    def whole(shape):
        return pl.BlockSpec(shape, lambda i, s: (0,) * len(shape))

    single = not isinstance(out_shape, list)
    outs = [out_shape] if single else out_shape
    specs = [whole(o.shape) for o in outs]
    return pl.pallas_call(
        kernel,
        out_shape=out_shape,
        grid_spec=pltpu.PrefetchScalarGridSpec(
            num_scalar_prefetch=1,
            grid=(1,),
            in_specs=[pl.BlockSpec((1,) + table.shape[1:], lambda i, s: (s[0], 0, 0))]
            + [whole(a.shape) for a in args],
            out_specs=specs[0] if single else specs,
        ),
        compiler_params=pltpu.CompilerParams(vmem_limit_bytes=VMEM_BYTES),
        cost_estimate=cost(macs, 4 * sum(a.size for a in args)),
        name=name,
    )(index, table, *args)


def looked_up(values, position):
    found = jnp.full((), int(values[0]), I32)
    for i in range(1, len(values)):
        step = int(values[i]) - int(values[i - 1])
        if step:
            found = found + step * (position >= i).astype(I32)
    return found


def shifted(value, axis, step):
    size = lax.axis_size(axis)
    pairs = [(i, i + step) for i in range(size) if 0 <= i + step < size]
    return lax.ppermute(value, axis, pairs)


def relay_blocks(value, reach):
    size = lax.axis_size("relay")
    if size == 2:
        return [value, lax.ppermute(value, "relay", [(0, 1), (1, 0)])]
    blocks = [value]
    for step in range(1, min(reach, size - 1) + 1):
        blocks += [shifted(value, "relay", step), shifted(value, "relay", -step)]
    return blocks


def relay_order(size, reach):
    if size == 2:
        return lambda r: [r, 1 - r]
    steps = [0]
    for step in range(1, min(reach, size - 1) + 1):
        steps += [-step, step]
    return lambda r: [r + s for s in steps]


def relay_total(value):
    size = lax.axis_size("relay")
    values, moving = [value], value
    for _ in range(size - 1):
        moving = lax.ppermute(moving, "relay", [(i, (i + 1) % size) for i in range(size)])
        values.append(moving)
    return jnp.concatenate(values, axis=0)


def shards(target, frag_brick, bead_cell, bead_weight, bead_arm, frag_angle):
    brick_count, relay_count = lax.axis_size("brick"), lax.axis_size("relay")
    frags, beads = bead_cell.shape
    planes, columns, rows = target.shape
    lines = planes * columns
    his = lines * (rows // LO)
    assert rows % LO == 0 and his <= 256 and columns >= 2 * KR
    voxel_total = float(brick_count * columns * relay_count * planes * rows)
    most = max(2, 2 * frags // brick_count)
    slots = brick_count * most
    assert most * FIELDS <= 128

    z_total, x_total = relay_count * planes, brick_count * columns
    gz, dz = axis_matrix(z_total, False), axis_matrix(z_total, True)
    gx, dx = axis_matrix(x_total, False), axis_matrix(x_total, True)
    reach_one, reach_two = -(-KR // planes), -(-2 * KR // planes)
    target_table, tz, tx, tn = weight_table(
        [gz, gz, dz], [dx, gx, gx], planes, relay_count, relay_order(relay_count, reach_one),
        columns, brick_count,
        [np.arange(columns), np.arange(-KR, 0), np.arange(columns, columns + KR)],
    )
    model_table, mz, mx, mn = weight_table(
        [gz @ gz, gz @ gz, dz @ gz, gz], [dx @ gx, gx @ gx, gx @ gx, gx],
        planes, relay_count, relay_order(relay_count, reach_two), columns, brick_count,
        [np.arange(columns), np.arange(-columns, 0), np.arange(columns, 2 * columns)],
    )
    r, b = lax.axis_index("relay"), lax.axis_index("brick")
    target_index = (looked_up(tz, r) * tn + looked_up(tx, b)).reshape(1)
    model_index = (looked_up(mz, r) * mn + looked_up(mx, b)).reshape(1)

    target_lines = target.reshape(lines, rows)
    target_blocks = relay_blocks(target, reach_one)
    left_edge = jnp.concatenate([t[:, columns - KR :] for t in target_blocks], axis=0)
    right_edge = jnp.concatenate([t[:, :KR] for t in target_blocks], axis=0)
    from_left = shifted(left_edge.reshape(-1, rows), "brick", 1)
    from_right = shifted(right_edge.reshape(-1, rows), "brick", -1)

    brick_row = frag_brick.reshape(1, frags)
    vmem, anywhere = pl.BlockSpec(memory_space=pltpu.VMEM), pl.BlockSpec(memory_space=pl.ANY)
    sent = call(
        functools.partial(pack_kernel, most, lines, rows),
        jax.ShapeDtypeStruct((slots, 3 * beads), I32),
        brick_row, frag_angle, bead_cell, bead_weight, bead_arm,
        in_specs=[vmem, vmem, anywhere, anywhere, anywhere],
        scratch=[
            pltpu.VMEM(bead_cell.shape, I32),
            pltpu.VMEM(bead_weight.shape, BF16),
            pltpu.VMEM(bead_arm.shape, F32),
            pltpu.SemaphoreType.DMA((3,)),
        ],
        name="pack",
    )
    got = lax.all_to_all(sent, "brick", split_axis=0, concat_axis=0, tiled=True)
    got, from_left, from_right = lax.optimization_barrier((got, from_left, from_right))
    target_parts = [t.reshape(lines, rows) for t in target_blocks] + [from_left, from_right]
    smooth = call(
        functools.partial(splat_kernel, lines, min(32, slots)),
        jax.ShapeDtypeStruct((lines, rows), F32),
        got,
        scratch=[pltpu.VMEM((his, LO), F32)],
        name="splat",
        macs=slots * beads * his * LO,
    )
    blocks = jnp.concatenate(relay_blocks(smooth, reach_two), axis=0)
    target_field = call_at(
        functools.partial(target_kernel, lines, len(target_parts)),
        jax.ShapeDtypeStruct((3 * his, 2 * LO), BF16),
        target_index, jnp.asarray(target_table), *target_parts,
        name="target_fields",
        macs=9 * lines * rows * 128,
    )
    blocks, target_field = lax.optimization_barrier((blocks, target_field))
    model_parts = [blocks, shifted(blocks, "brick", 1), shifted(blocks, "brick", -1)]

    def sample(field, name):
        return call(
            functools.partial(sample_kernel, his, min(32, slots)),
            jax.ShapeDtypeStruct((slots, 128), F32),
            got, field,
            scratch=[pltpu.VMEM((3, slots, beads), F32)],
            name=name,
            macs=6 * slots * beads * his * LO,
        )

    target_sums = sample(target_field, "target_sample")
    target_sums, *model_parts = lax.optimization_barrier((target_sums, *model_parts))
    model_field, partial = call_at(
        functools.partial(model_kernel, lines, len(model_parts)),
        [
            jax.ShapeDtypeStruct((3 * his, 2 * LO), BF16),
            jax.ShapeDtypeStruct((8, 128), F32),
        ],
        model_index, jnp.asarray(model_table), target_lines, *model_parts,
        name="model_fields",
    )
    partials = relay_total(partial)
    model_sums = sample(model_field, "model_sample")
    leaving = call(
        functools.partial(join_kernel, most),
        jax.ShapeDtypeStruct((brick_count, 128), F32),
        target_sums, model_sums, partials,
        name="join",
    )
    back = lax.all_to_all(leaving, "brick", split_axis=0, concat_axis=0, tiled=True)
    return call(
        functools.partial(finish_kernel, most, voxel_total),
        jax.ShapeDtypeStruct((6, frags), F32),
        brick_row, back,
        name="finish",
    )


def solution(mesh):
    placed = (
        P("relay", "brick", None),
        P(("brick", "relay"), None),
        P(("brick", "relay"), None),
        P(("brick", "relay"), None),
        P(None, ("brick", "relay"), None),
        P(None, ("brick", "relay")),
    )
    return jax.shard_map(
        shards, mesh=mesh, in_specs=placed, out_specs=P(None, ("brick", "relay")), check_vma=False
    )
```

```python
import functools

import jax
import jax.numpy as jnp
import numpy as np
from jax import lax
from jax.experimental import pallas as pl
from jax.experimental.pallas import tpu as pltpu
from jax.sharding import PartitionSpec as P

KR = 4
SIGMA = 1.5
EPSILON = 1e-06
HIGHEST = lax.Precision.HIGHEST
LO = 256
FIELDS = 16
WEIGHT_SCALE = 512.0
LEVER_SCALE = 32768.0
LEVER_BIAS = 1 << 20
VMEM_BYTES = 48 << 20
PACK_VMEM_BYTES = 60 << 20
F32 = jnp.float32
BF16 = jnp.bfloat16
I32 = jnp.int32


def taps_of(derivative):
    offsets = np.arange(-KR, KR + 1) * 1.0
    gaussian = np.exp(-(offsets**2) / (2.0 * SIGMA**2))
    gaussian = gaussian / gaussian.sum()
    if derivative:
        return -offsets / SIGMA**2 * gaussian
    return gaussian


def axis_matrix(length, derivative):
    offsets = np.arange(length)[:, None] - np.arange(length)[None, :]
    return np.where(
        np.abs(offsets) <= KR, taps_of(derivative)[np.clip(offsets + KR, 0, 2 * KR)], 0.0
    )


def columns_at(matrix, rows, wanted):
    inside = (wanted >= 0) & (wanted < matrix.shape[1])
    picked = matrix[rows][:, np.clip(wanted, 0, matrix.shape[1] - 1)]
    return np.where(inside[None, :], picked, 0.0)


def unique_tables(tables):
    flat = np.stack([t.reshape(-1) for t in tables])
    kept, inverse = np.unique(np.round(flat, 14), axis=0, return_inverse=True)
    return kept.reshape((-1,) + tables[0].shape), inverse.reshape(-1).astype(np.int32)


def pieces_np(table):
    import ml_dtypes

    high = table.astype(np.float32).astype(ml_dtypes.bfloat16)
    low = (table - high.astype(np.float64)).astype(ml_dtypes.bfloat16)
    return np.concatenate([high, high, low], axis=-1)


def weight_table(z_kinds, x_kinds, z_len, z_count, z_blocks, x_len, x_count, x_parts):
    z_tables = []
    for r in range(z_count):
        wanted = np.concatenate([np.arange(z_len) + z_len * block for block in z_blocks(r)])
        rows = np.arange(z_len) + z_len * r
        z_tables.append(np.stack([columns_at(m, rows, wanted) for m in z_kinds]))
    x_tables = []
    for b in range(x_count):
        wanted = np.concatenate([x_len * b + part for part in x_parts])
        rows = np.arange(x_len) + x_len * b
        x_tables.append(np.stack([columns_at(m, rows, wanted) for m in x_kinds]))
    z_tables, z_inverse = unique_tables(z_tables)
    x_tables, x_inverse = unique_tables(x_tables)
    kinds = len(z_kinds)
    parts, start = [], 0
    for part in x_parts:
        piece = x_tables[:, :, :, start : start + len(part)]
        start += len(part)
        full = np.einsum("rkzi,bkxj->rbkzxij", z_tables, piece)
        parts.append(
            full.reshape(len(z_tables) * len(x_tables), kinds * z_len * x_len, -1)
        )
    table = pieces_np(np.concatenate(parts, axis=-1))
    return table, z_inverse, x_inverse, len(x_tables)


def eye_column(row, eye):
    return jnp.sum(jnp.where(eye, row, jnp.zeros_like(row)), axis=1, keepdims=True)


def slot_row(row, most):
    frags = row.shape[1]
    sub = lax.broadcasted_iota(I32, (frags, frags), 0)
    lane = lax.broadcasted_iota(I32, (frags, frags), 1)
    eye = sub == lane
    earlier = jnp.logical_and(eye_column(row, eye) == row, sub < lane)
    return jnp.sum(jnp.where(earlier, 1, 0), axis=0, keepdims=True), eye


def pack_kernel(
    most, lines, row_count, brick_ref, angle_ref, cell_in, weight_in, arm_in, out_ref,
    cell_ref, weight_ref, arm_ref, sems,
):
    copies = [
        pltpu.make_async_copy(source, target, sems.at[k])
        for k, (source, target) in enumerate(
            [(cell_in, cell_ref), (weight_in, weight_ref), (arm_in, arm_ref)]
        )
    ]
    for copy in copies:
        copy.start()
    frags, beads = cell_ref.shape
    slots = out_ref.shape[0]
    row = brick_ref[...]
    rank, eye = slot_row(row, most)
    slot = row * most + rank
    place = jnp.where(lax.broadcasted_iota(I32, (slots, frags), 0) == slot, 1.0, 0.0).astype(F32)

    angles = angle_ref[...]
    cos, sin = jnp.cos(angles), jnp.sin(angles)
    cos_a, cos_b, cos_c = cos[0:1], cos[1:2], cos[2:3]
    sin_a, sin_b, sin_c = sin[0:1], sin[1:2], sin[2:3]
    turn = [
        [cos_a * cos_b, cos_a * sin_b * sin_c - sin_a * cos_c, cos_a * sin_b * cos_c + sin_a * sin_c],
        [sin_a * cos_b, sin_a * sin_b * sin_c + cos_a * cos_c, sin_a * sin_b * cos_c - cos_a * sin_c],
        [-sin_b, cos_b * sin_c, cos_b * cos_c],
    ]
    turn = [[eye_column(value, eye) for value in values] for values in turn]
    for copy in copies:
        copy.wait()
    levers = []
    for i in range(3):
        total = turn[i][0] * arm_ref[0]
        for j in (1, 2):
            total = total + turn[i][j] * arm_ref[j]
        levers.append(jnp.round(total * LEVER_SCALE))

    cell = cell_ref[...]
    line = ((cell.astype(F32) + 0.5) * (1.0 / row_count)).astype(I32)
    y = cell - line * row_count
    code = (((y // LO) * lines + line) * LO + (y % LO)).astype(F32)
    weight = weight_ref[...].astype(F32) * WEIGHT_SCALE
    payload = jnp.concatenate([code, weight] + levers, axis=1)
    placed = jnp.dot(place, payload, precision=HIGHEST, preferred_element_type=F32)
    placed = placed.astype(I32)
    code, weight, lx, ly, lz = [placed[:, k * beads : (k + 1) * beads] for k in range(5)]
    lz = lz + LEVER_BIAS
    out_ref[:, 0:beads] = code | (weight << 16)
    out_ref[:, beads : 2 * beads] = (lx << 11) | (lz >> 10)
    out_ref[:, 2 * beads : 3 * beads] = (ly << 11) | (lz & 1023)


def line_blur(value, derivative):
    taps = taps_of(derivative)
    rows, length = value.shape
    wide = jnp.concatenate([value, jnp.zeros((rows, 128), F32)], axis=1)
    total = None if derivative else float(taps[KR]) * value
    for d in range(1, KR + 1):
        up = pltpu.roll(wide, d, 1)[:, :length]
        down = pltpu.roll(wide, length + 128 - d, 1)[:, :length]
        pair = up - down if derivative else up + down
        term = float(taps[KR + d]) * pair
        total = term if total is None else total + term
    return total


def splat_kernel(lines, rb, got_ref, out_ref, acc_ref):
    slots = got_ref.shape[0]
    beads = got_ref.shape[1] // 3
    his = acc_ref.shape[0]
    acc_ref[...] = jnp.zeros_like(acc_ref)
    hi_iota = lax.broadcasted_iota(I32, (his, beads), 0)
    lo_iota = lax.broadcasted_iota(I32, (LO, beads), 0)

    def body(i, carry):
        word = got_ref[pl.ds(i * rb, rb), 0:beads]
        lo = word & (LO - 1)
        hi = (word >> 8) & 255
        weight = (word >> 16).astype(F32) * (1.0 / WEIGHT_SCALE)
        left, right = [], []
        for q in range(rb):
            left.append(jnp.where(hi_iota == hi[q : q + 1], weight[q : q + 1], 0.0).astype(BF16))
            right.append(jnp.where(lo_iota == lo[q : q + 1], 1.0, 0.0).astype(BF16))
        acc_ref[...] += lax.dot_general(
            jnp.concatenate(left, axis=1),
            jnp.concatenate(right, axis=1),
            (((1,), (1,)), ((), ())),
            preferred_element_type=F32,
        )
        return carry

    lax.fori_loop(0, slots // rb, body, 0)
    density = [acc_ref[yh * lines : (yh + 1) * lines, :] for yh in range(his // lines)]
    out_ref[...] = line_blur(jnp.concatenate(density, axis=1), False)


def split(value):
    high = value.astype(BF16)
    low = (value - high.astype(F32)).astype(BF16)
    return high, low


def mix_lines(table_ref, parts):
    value = jnp.concatenate(parts, axis=0)
    high, low = split(value)
    return jnp.dot(
        table_ref[0], jnp.concatenate([high, low, high], axis=0), preferred_element_type=F32
    )


def store_fields(fields, lines, out_ref):
    his = fields[0].shape[1] // LO * lines
    for k, field in enumerate(fields):
        for yh in range(field.shape[1] // LO):
            high, low = split(field[:, yh * LO : (yh + 1) * LO])
            rows = slice(k * his + yh * lines, k * his + (yh + 1) * lines)
            out_ref[rows, 0:LO] = high
            out_ref[rows, LO : 2 * LO] = low


def target_kernel(lines, count, _, table_ref, *refs):
    parts, out_ref = refs[:count], refs[count]
    mixed = mix_lines(table_ref, [ref[...] for ref in parts])
    grad_x = line_blur(mixed[0:lines], False)
    grad_y = line_blur(mixed[lines : 2 * lines], True)
    grad_z = line_blur(mixed[2 * lines : 3 * lines], False)
    store_fields([grad_x, grad_y, grad_z], lines, out_ref)


def model_kernel(lines, count, _, table_ref, target_ref, *refs):
    parts, out_ref, sum_ref = refs[:count], refs[count], refs[count + 1]
    smooth = mix_lines(table_ref, [ref[...] for ref in parts])
    model = smooth[3 * lines :]
    target = target_ref[...]
    sums = [jnp.sum(model * target), jnp.sum(model * model), jnp.sum(target * target)]
    lane = lax.broadcasted_iota(I32, sum_ref.shape, 1)
    total = jnp.zeros(sum_ref.shape, F32)
    for k, value in enumerate(sums):
        total = jnp.where(lane == k, value, total)
    sum_ref[...] = total
    grad_x = line_blur(smooth[0:lines], False)
    grad_y = line_blur(smooth[lines : 2 * lines], True)
    grad_z = line_blur(smooth[2 * lines : 3 * lines], False)
    store_fields([grad_x, grad_y, grad_z], lines, out_ref)


def sample_kernel(his, rb, start, got_ref, field_ref, out_ref, force_ref):
    slots = out_ref.shape[0]
    beads = got_ref.shape[1] // 3
    lo_iota = lax.broadcasted_iota(I32, (LO, beads), 0)
    sub_iota = lax.broadcasted_iota(I32, (8, beads), 0)

    def body(i, carry):
        word = got_ref[pl.ds(start + i * rb, rb), 0:beads]
        lo = word & (LO - 1)
        hi = (word >> 8) & 255
        picks = [
            jnp.where(lo_iota == lo[q : q + 1], 1.0, 0.0).astype(BF16) for q in range(rb)
        ]
        pick = jnp.concatenate(picks, axis=1)
        sampled = jnp.dot(
            field_ref[...], jnp.concatenate([pick, pick], axis=0), preferred_element_type=F32
        )
        for q in range(rb):
            own = jnp.broadcast_to(hi[q : q + 1], (8, beads))
            group, within = own >> 3, (own & 7) == sub_iota
            found = [jnp.zeros((8, beads), F32)] * 3
            for j in range(his // 8):
                here = group == j
                for k in range(3):
                    rows = slice(k * his + 8 * j, k * his + 8 * j + 8)
                    found[k] = jnp.where(
                        here, sampled[rows, q * beads : (q + 1) * beads], found[k]
                    )
            for k in range(3):
                value = jnp.sum(jnp.where(within, found[k], 0.0), axis=0, keepdims=True)
                force_ref[k, pl.ds(i * rb + q, 1), :] = value
        return carry

    lax.fori_loop(0, slots // rb, body, 0)
    rows = slice(start, start + slots)
    first, second = got_ref[rows, beads : 2 * beads], got_ref[rows, 2 * beads : 3 * beads]
    weight = (got_ref[rows, 0:beads] >> 16).astype(F32) * (1.0 / WEIGHT_SCALE)
    lever_z = (((first & 2047) << 10) | (second & 1023)) - LEVER_BIAS
    levers = [
        v.astype(F32) * (1.0 / LEVER_SCALE) for v in (first >> 11, second >> 11, lever_z)
    ]
    force = [force_ref[k] * weight for k in range(3)]
    terms = force + [
        levers[1] * force[2] - levers[2] * force[1],
        levers[2] * force[0] - levers[0] * force[2],
        levers[0] * force[1] - levers[1] * force[0],
    ]
    lane = lax.broadcasted_iota(I32, out_ref.shape, 1)
    total = jnp.zeros(out_ref.shape, F32)
    for k, term in enumerate(terms):
        total = jnp.where(lane == k, jnp.sum(term, axis=1, keepdims=True), total)
    out_ref[...] = total


def join_kernel(most, first_ref, second_ref, model_ref, sum_ref, out_ref):
    bricks = out_ref.shape[0]
    lane = lax.broadcasted_iota(I32, out_ref.shape, 1)
    sums = sum_ref[0:1, :]
    for k in range(1, sum_ref.shape[0] // 8):
        sums = sums + sum_ref[8 * k : 8 * k + 1, :]
    total = jnp.zeros(out_ref.shape, F32)
    for k in range(most):
        rows, half = pl.ds(k, bricks, stride=most), pl.ds(k, bricks // 2, stride=most)
        own = jnp.concatenate([first_ref[half, :], second_ref[half, :]], axis=0)
        own = jnp.where(lane < 6, own, 0.0)
        own = own + pltpu.roll(jnp.where(lane < 6, model_ref[rows, :], 0.0), 6, 1)
        if k == 0:
            own = own + pltpu.roll(jnp.where(lane < 3, sums, 0.0), 12, 1)
        total = total + (pltpu.roll(own, FIELDS * k, 1) if k else own)
    out_ref[...] = total


def finish_kernel(most, voxel_total, brick_ref, back_ref, out_ref):
    frags = out_ref.shape[1]
    bricks = back_ref.shape[0]
    row = brick_ref[...]
    rank, _ = slot_row(row, most)
    place = jnp.where(lax.broadcasted_iota(I32, (bricks, frags), 0) == row, 1.0, 0.0).astype(F32)
    back = back_ref[...]
    sums = jnp.sum(back, axis=0, keepdims=True)
    cross, model_sq, target_sq = sums[:, 12:13], sums[:, 13:14], sums[:, 14:15]
    norm_model = jnp.sqrt(model_sq + EPSILON)
    norm_target = jnp.sqrt(target_sq + EPSILON)
    corr = cross / (norm_model * norm_target)
    scale_target = voxel_total / (norm_model * norm_target)
    scale_model = voxel_total * corr / (norm_model * norm_model)
    found = lax.dot_general(
        back, place, (((0,), (0,)), ((), ())), precision=HIGHEST, preferred_element_type=F32
    )
    mine = jnp.zeros((FIELDS, frags), F32)
    for k in range(most):
        mine = jnp.where(rank == k, found[FIELDS * k : FIELDS * (k + 1)], mine)
    out_ref[...] = scale_target * mine[0:6] - scale_model * mine[6:12]


def cost(macs, nbytes):
    return pl.CostEstimate(flops=2 * macs, bytes_accessed=nbytes, transcendentals=0)


def call(
    kernel, out_shape, *args, scratch=(), name=None, macs=0, in_specs=None, vmem=VMEM_BYTES
):
    kwargs = {} if in_specs is None else {"in_specs": in_specs}
    return pl.pallas_call(
        kernel,
        out_shape=out_shape,
        scratch_shapes=list(scratch),
        compiler_params=pltpu.CompilerParams(vmem_limit_bytes=vmem),
        cost_estimate=cost(macs, 4 * sum(a.size for a in args)),
        name=name,
        **kwargs,
    )(*args)


def call_at(kernel, out_shape, index, table, *args, name=None, macs=0):
    def whole(shape):
        return pl.BlockSpec(shape, lambda i, s: (0,) * len(shape))

    single = not isinstance(out_shape, list)
    outs = [out_shape] if single else out_shape
    specs = [whole(o.shape) for o in outs]
    return pl.pallas_call(
        kernel,
        out_shape=out_shape,
        grid_spec=pltpu.PrefetchScalarGridSpec(
            num_scalar_prefetch=1,
            grid=(1,),
            in_specs=[pl.BlockSpec((1,) + table.shape[1:], lambda i, s: (s[0], 0, 0))]
            + [whole(a.shape) for a in args],
            out_specs=specs[0] if single else specs,
        ),
        compiler_params=pltpu.CompilerParams(vmem_limit_bytes=VMEM_BYTES),
        cost_estimate=cost(macs, 4 * sum(a.size for a in args)),
        name=name,
    )(index, table, *args)


def looked_up(values, position):
    found = jnp.full((), int(values[0]), I32)
    for i in range(1, len(values)):
        step = int(values[i]) - int(values[i - 1])
        if step:
            found = found + step * (position >= i).astype(I32)
    return found


def shifted(value, axis, step):
    size = lax.axis_size(axis)
    pairs = [(i, i + step) for i in range(size) if 0 <= i + step < size]
    return lax.ppermute(value, axis, pairs)


def relay_blocks(value, reach):
    size = lax.axis_size("relay")
    if size == 2:
        return [value, lax.ppermute(value, "relay", [(0, 1), (1, 0)])]
    blocks = [value]
    for step in range(1, min(reach, size - 1) + 1):
        blocks += [shifted(value, "relay", step), shifted(value, "relay", -step)]
    return blocks


def relay_order(size, reach):
    if size == 2:
        return lambda r: [r, 1 - r]
    steps = [0]
    for step in range(1, min(reach, size - 1) + 1):
        steps += [-step, step]
    return lambda r: [r + s for s in steps]


def relay_total(value):
    size = lax.axis_size("relay")
    values, moving = [value], value
    for _ in range(size - 1):
        moving = lax.ppermute(moving, "relay", [(i, (i + 1) % size) for i in range(size)])
        values.append(moving)
    return jnp.concatenate(values, axis=0)


def shards(target, frag_brick, bead_cell, bead_weight, bead_arm, frag_angle):
    brick_count, relay_count = lax.axis_size("brick"), lax.axis_size("relay")
    frags, beads = bead_cell.shape
    planes, columns, rows = target.shape
    lines = planes * columns
    his = lines * (rows // LO)
    assert rows % LO == 0 and his <= 256 and columns >= 2 * KR
    voxel_total = float(brick_count * columns * relay_count * planes * rows)
    most = max(2, 2 * frags // brick_count)
    slots = brick_count * most
    assert most * FIELDS <= 128

    z_total, x_total = relay_count * planes, brick_count * columns
    gz, dz = axis_matrix(z_total, False), axis_matrix(z_total, True)
    gx, dx = axis_matrix(x_total, False), axis_matrix(x_total, True)
    reach_one, reach_two = -(-KR // planes), -(-2 * KR // planes)
    target_table, tz, tx, tn = weight_table(
        [gz, gz, dz], [dx, gx, gx], planes, relay_count, relay_order(relay_count, reach_one),
        columns, brick_count,
        [np.arange(columns), np.arange(-KR, 0), np.arange(columns, columns + KR)],
    )
    model_table, mz, mx, mn = weight_table(
        [gz @ gz, gz @ gz, dz @ gz, gz], [dx @ gx, gx @ gx, gx @ gx, gx],
        planes, relay_count, relay_order(relay_count, reach_two), columns, brick_count,
        [np.arange(columns), np.arange(-columns, 0), np.arange(columns, 2 * columns)],
    )
    r, b = lax.axis_index("relay"), lax.axis_index("brick")
    target_index = (looked_up(tz, r) * tn + looked_up(tx, b)).reshape(1)
    model_index = (looked_up(mz, r) * mn + looked_up(mx, b)).reshape(1)

    target_lines = target.reshape(lines, rows)
    target_blocks = relay_blocks(target, reach_one)
    left_edge = jnp.concatenate([t[:, columns - KR :] for t in target_blocks], axis=0)
    right_edge = jnp.concatenate([t[:, :KR] for t in target_blocks], axis=0)
    from_left = shifted(left_edge.reshape(-1, rows), "brick", 1)
    from_right = shifted(right_edge.reshape(-1, rows), "brick", -1)

    brick_row = frag_brick.reshape(1, frags)
    vmem, hbm = pl.BlockSpec(memory_space=pltpu.VMEM), pl.BlockSpec(memory_space=pltpu.HBM)
    sent = call(
        functools.partial(pack_kernel, most, lines, rows),
        jax.ShapeDtypeStruct((slots, 3 * beads), I32),
        brick_row, frag_angle, bead_cell, bead_weight, bead_arm,
        in_specs=[vmem, vmem, hbm, hbm, hbm],
        scratch=[
            pltpu.VMEM(bead_cell.shape, I32),
            pltpu.VMEM(bead_weight.shape, BF16),
            pltpu.VMEM(bead_arm.shape, F32),
            pltpu.SemaphoreType.DMA((3,)),
        ],
        name="pack",
        vmem=PACK_VMEM_BYTES,
    )
    got = lax.all_to_all(sent, "brick", split_axis=0, concat_axis=0, tiled=True)
    smooth = call(
        functools.partial(splat_kernel, lines, min(32, slots)),
        jax.ShapeDtypeStruct((lines, rows), F32),
        got,
        scratch=[pltpu.VMEM((his, LO), F32)],
        name="splat",
        macs=slots * beads * his * LO,
    )
    smooth, from_left, from_right = lax.optimization_barrier((smooth, from_left, from_right))
    target_parts = [t.reshape(lines, rows) for t in target_blocks] + [from_left, from_right]
    blocks = jnp.concatenate(relay_blocks(smooth, reach_two), axis=0)
    target_field = call_at(
        functools.partial(target_kernel, lines, len(target_parts)),
        jax.ShapeDtypeStruct((3 * his, 2 * LO), BF16),
        target_index, jnp.asarray(target_table), *target_parts,
        name="target_fields",
        macs=9 * lines * rows * 128,
    )

    def sample(field, start, count, name):
        return call(
            functools.partial(sample_kernel, his, min(32, count), start),
            jax.ShapeDtypeStruct((count, 128), F32),
            got, field,
            scratch=[pltpu.VMEM((3, count, beads), F32)],
            name=name,
            macs=6 * count * beads * his * LO,
        )

    half = slots // 2
    target_first = sample(target_field, 0, half, "target_sample_a")
    blocks, target_first, target_field = lax.optimization_barrier(
        (blocks, target_first, target_field)
    )
    model_parts = [blocks, shifted(blocks, "brick", 1), shifted(blocks, "brick", -1)]
    target_second = sample(target_field, half, slots - half, "target_sample_b")
    target_second, *model_parts = lax.optimization_barrier((target_second, *model_parts))
    model_field, partial = call_at(
        functools.partial(model_kernel, lines, len(model_parts)),
        [
            jax.ShapeDtypeStruct((3 * his, 2 * LO), BF16),
            jax.ShapeDtypeStruct((8, 128), F32),
        ],
        model_index, jnp.asarray(model_table), target_lines, *model_parts,
        name="model_fields",
    )
    partials = relay_total(partial)
    model_sums = sample(model_field, 0, slots, "model_sample")
    leaving = call(
        functools.partial(join_kernel, most),
        jax.ShapeDtypeStruct((brick_count, 128), F32),
        target_first, target_second, model_sums, partials,
        name="join",
    )
    back = lax.all_to_all(leaving, "brick", split_axis=0, concat_axis=0, tiled=True)
    return call(
        functools.partial(finish_kernel, most, voxel_total),
        jax.ShapeDtypeStruct((6, frags), F32),
        brick_row, back,
        name="finish",
    )


def solution(mesh):
    placed = (
        P("relay", "brick", None),
        P(("brick", "relay"), None),
        P(("brick", "relay"), None),
        P(("brick", "relay"), None),
        P(None, ("brick", "relay"), None),
        P(None, ("brick", "relay")),
    )
    return jax.shard_map(
        shards, mesh=mesh, in_specs=placed, out_specs=P(None, ("brick", "relay")), check_vma=False
    )
```

```python
import functools

import jax
import jax.numpy as jnp
import numpy as np
from jax import lax
from jax.experimental import pallas as pl
from jax.experimental.pallas import tpu as pltpu
from jax.sharding import PartitionSpec as P

KR = 4
SIGMA = 1.5
EPSILON = 1e-06
HIGHEST = lax.Precision.HIGHEST
LO = 256
FIELDS = 16
WEIGHT_SCALE = 512.0
LEVER_SCALE = 32768.0
LEVER_BIAS = 1 << 20
CODE_TOP = 65535
SCALE_UNIT = 512.0
SCALE_LANES = 128
VMEM_BYTES = 48 << 20
PACK_VMEM_BYTES = 60 << 20
F32 = jnp.float32
BF16 = jnp.bfloat16
I32 = jnp.int32


def taps_of(derivative):
    offsets = np.arange(-KR, KR + 1) * 1.0
    gaussian = np.exp(-(offsets**2) / (2.0 * SIGMA**2))
    gaussian = gaussian / gaussian.sum()
    if derivative:
        return -offsets / SIGMA**2 * gaussian
    return gaussian


def axis_matrix(length, derivative):
    offsets = np.arange(length)[:, None] - np.arange(length)[None, :]
    return np.where(
        np.abs(offsets) <= KR, taps_of(derivative)[np.clip(offsets + KR, 0, 2 * KR)], 0.0
    )


def columns_at(matrix, rows, wanted):
    inside = (wanted >= 0) & (wanted < matrix.shape[1])
    picked = matrix[rows][:, np.clip(wanted, 0, matrix.shape[1] - 1)]
    return np.where(inside[None, :], picked, 0.0)


def unique_tables(tables):
    flat = np.stack([t.reshape(-1) for t in tables])
    kept, inverse = np.unique(np.round(flat, 14), axis=0, return_inverse=True)
    return kept.reshape((-1,) + tables[0].shape), inverse.reshape(-1).astype(np.int32)


def pieces_np(table):
    import ml_dtypes

    high = table.astype(np.float32).astype(ml_dtypes.bfloat16)
    low = (table - high.astype(np.float64)).astype(ml_dtypes.bfloat16)
    return np.concatenate([high, high, low], axis=-1)


def weight_table(z_kinds, x_kinds, z_len, z_count, z_blocks, x_len, x_count, x_parts):
    z_tables = []
    for r in range(z_count):
        wanted = np.concatenate([np.arange(z_len) + z_len * block for block in z_blocks(r)])
        rows = np.arange(z_len) + z_len * r
        z_tables.append(np.stack([columns_at(m, rows, wanted) for m in z_kinds]))
    x_tables = []
    for b in range(x_count):
        wanted = np.concatenate([x_len * b + part for part in x_parts])
        rows = np.arange(x_len) + x_len * b
        x_tables.append(np.stack([columns_at(m, rows, wanted) for m in x_kinds]))
    z_tables, z_inverse = unique_tables(z_tables)
    x_tables, x_inverse = unique_tables(x_tables)
    kinds = len(z_kinds)
    parts, start = [], 0
    for part in x_parts:
        piece = x_tables[:, :, :, start : start + len(part)]
        start += len(part)
        full = np.einsum("rkzi,bkxj->rbkzxij", z_tables, piece)
        parts.append(
            full.reshape(len(z_tables) * len(x_tables), kinds * z_len * x_len, -1)
        )
    table = pieces_np(np.concatenate(parts, axis=-1))
    return table, z_inverse, x_inverse, len(x_tables)


def eye_column(row, eye):
    return jnp.sum(jnp.where(eye, row, jnp.zeros_like(row)), axis=1, keepdims=True)


def slot_row(row, most):
    frags = row.shape[1]
    sub = lax.broadcasted_iota(I32, (frags, frags), 0)
    lane = lax.broadcasted_iota(I32, (frags, frags), 1)
    eye = sub == lane
    earlier = jnp.logical_and(eye_column(row, eye) == row, sub < lane)
    return jnp.sum(jnp.where(earlier, 1, 0), axis=0, keepdims=True), eye


def pack_kernel(most, lines, row_count, *refs):
    inputs, (out_ref, place_ref), held, sems = refs[:5], refs[5:7], refs[7:12], refs[12]
    copies = [
        pltpu.make_async_copy(source, target, sems.at[k])
        for k, (source, target) in enumerate(zip(inputs, held))
    ]
    for copy in copies:
        copy.start()
    brick_ref, angle_ref, cell_ref, weight_ref, arm_ref = held
    for copy in copies[:2]:
        copy.wait()
    frags, beads = cell_ref.shape
    slots = out_ref.shape[0]
    row = brick_ref[...]
    rank, eye = slot_row(row, most)
    slot = row * most + rank
    place = jnp.where(lax.broadcasted_iota(I32, (slots, frags), 0) == slot, 1.0, 0.0).astype(F32)

    angles = angle_ref[...]
    cos, sin = jnp.cos(angles), jnp.sin(angles)
    cos_a, cos_b, cos_c = cos[0:1], cos[1:2], cos[2:3]
    sin_a, sin_b, sin_c = sin[0:1], sin[1:2], sin[2:3]
    turn = [
        [cos_a * cos_b, cos_a * sin_b * sin_c - sin_a * cos_c, cos_a * sin_b * cos_c + sin_a * sin_c],
        [sin_a * cos_b, sin_a * sin_b * sin_c + cos_a * cos_c, sin_a * sin_b * cos_c - cos_a * sin_c],
        [-sin_b, cos_b * sin_c, cos_b * cos_c],
    ]
    turn = [[eye_column(value, eye) for value in values] for values in turn]
    place_ref[0:1, :] = row
    place_ref[1:2, :] = rank
    for copy in copies[2:]:
        copy.wait()
    levers = []
    for i in range(3):
        total = turn[i][0] * arm_ref[0]
        for j in (1, 2):
            total = total + turn[i][j] * arm_ref[j]
        levers.append(jnp.round(total * LEVER_SCALE))

    cell = cell_ref[...]
    line = ((cell.astype(F32) + 0.5) * (1.0 / row_count)).astype(I32)
    y = cell - line * row_count
    code = (((y // LO) * lines + line) * LO + (y % LO)).astype(F32)
    weight = weight_ref[...].astype(F32) * WEIGHT_SCALE
    payload = jnp.concatenate([code, weight] + levers, axis=1)
    placed = jnp.dot(place, payload, precision=HIGHEST, preferred_element_type=F32)
    placed = placed.astype(I32)
    code, weight, lx, ly, lz = [placed[:, k * beads : (k + 1) * beads] for k in range(5)]
    lz = lz + LEVER_BIAS
    out_ref[:, 0:beads] = code | (weight << 16)
    out_ref[:, beads : 2 * beads] = (lx << 11) | (lz >> 10)
    out_ref[:, 2 * beads : 3 * beads] = (ly << 11) | (lz & 1023)


def line_blur(value, derivative):
    taps = taps_of(derivative)
    rows, length = value.shape
    wide = jnp.concatenate([value, jnp.zeros((rows, 128), F32)], axis=1)
    total = None if derivative else float(taps[KR]) * value
    for d in range(1, KR + 1):
        up = pltpu.roll(wide, d, 1)[:, :length]
        down = pltpu.roll(wide, length + 128 - d, 1)[:, :length]
        pair = up - down if derivative else up + down
        term = float(taps[KR + d]) * pair
        total = term if total is None else total + term
    return total


def encode(value, out_ref):
    half, length = value.shape[0] // 2, value.shape[1]
    top = (jnp.max(value) * SCALE_UNIT).astype(I32) + 1
    scale = (SCALE_UNIT * CODE_TOP) / top.astype(F32)
    code = jnp.minimum((value * scale + 0.5).astype(I32), CODE_TOP)
    out_ref[:, :length] = code[:half] | (code[half:] << 16)
    out_ref[:, length:] = jnp.full((half, SCALE_LANES), top, I32)


def decode(words, count):
    half, length = words.shape[0] // count, words.shape[1] - SCALE_LANES
    step = words[:, length : length + 1].astype(F32) * (1.0 / (SCALE_UNIT * CODE_TOP))
    low = (words[:, :length] & CODE_TOP).astype(F32) * step
    high = ((words[:, :length] >> 16) & CODE_TOP).astype(F32) * step
    lines = []
    for k in range(count):
        rows = slice(k * half, (k + 1) * half)
        lines += [low[rows], high[rows]]
    return lines


def encode_kernel(value_ref, out_ref):
    encode(value_ref[...], out_ref)


def splat_kernel(lines, rb, got_ref, out_ref, code_ref, acc_ref):
    slots = got_ref.shape[0]
    beads = got_ref.shape[1] // 3
    his = acc_ref.shape[0]
    acc_ref[...] = jnp.zeros_like(acc_ref)
    hi_iota = lax.broadcasted_iota(I32, (his, beads), 0)
    lo_iota = lax.broadcasted_iota(I32, (LO, beads), 0)

    def body(i, carry):
        word = got_ref[pl.ds(i * rb, rb), 0:beads]
        lo = word & (LO - 1)
        hi = (word >> 8) & 255
        weight = (word >> 16).astype(F32) * (1.0 / WEIGHT_SCALE)
        left, right = [], []
        for q in range(rb):
            left.append(jnp.where(hi_iota == hi[q : q + 1], weight[q : q + 1], 0.0).astype(BF16))
            right.append(jnp.where(lo_iota == lo[q : q + 1], 1.0, 0.0).astype(BF16))
        acc_ref[...] += lax.dot_general(
            jnp.concatenate(left, axis=1),
            jnp.concatenate(right, axis=1),
            (((1,), (1,)), ((), ())),
            preferred_element_type=F32,
        )
        return carry

    lax.fori_loop(0, slots // rb, body, 0)
    density = [acc_ref[yh * lines : (yh + 1) * lines, :] for yh in range(his // lines)]
    smooth = line_blur(jnp.concatenate(density, axis=1), False)
    out_ref[...] = smooth
    encode(smooth, code_ref)


def split(value):
    high = value.astype(BF16)
    low = (value - high.astype(F32)).astype(BF16)
    return high, low


def mix_lines(table_ref, parts):
    value = jnp.concatenate(parts, axis=0)
    high, low = split(value)
    return jnp.dot(
        table_ref[0], jnp.concatenate([high, low, high], axis=0), preferred_element_type=F32
    )


def store_fields(fields, lines, out_ref):
    his = fields[0].shape[1] // LO * lines
    for k, field in enumerate(fields):
        for yh in range(field.shape[1] // LO):
            high, low = split(field[:, yh * LO : (yh + 1) * LO])
            rows = slice(k * his + yh * lines, k * his + (yh + 1) * lines)
            out_ref[rows, 0:LO] = high
            out_ref[rows, LO : 2 * LO] = low


def window_lines(own_ref, near_refs, left_ref, right_ref):
    lines = [own_ref[...]]
    for ref in near_refs:
        lines += decode(ref[...], 1)
    for ref in (left_ref, right_ref):
        lines += decode(ref[...], len(near_refs) + 1)
    return lines


def target_kernel(lines, _, table_ref, own_ref, *refs):
    *near_refs, left_ref, right_ref, out_ref = refs
    mixed = mix_lines(table_ref, window_lines(own_ref, near_refs, left_ref, right_ref))
    grad_x = line_blur(mixed[0:lines], False)
    grad_y = line_blur(mixed[lines : 2 * lines], True)
    grad_z = line_blur(mixed[2 * lines : 3 * lines], False)
    store_fields([grad_x, grad_y, grad_z], lines, out_ref)


def model_kernel(lines, _, table_ref, target_ref, own_ref, *refs):
    *near_refs, left_ref, right_ref, out_ref, sum_ref = refs
    smooth = mix_lines(table_ref, window_lines(own_ref, near_refs, left_ref, right_ref))
    model = smooth[3 * lines :]
    target = target_ref[...]
    sums = [jnp.sum(model * target), jnp.sum(model * model), jnp.sum(target * target)]
    lane = lax.broadcasted_iota(I32, sum_ref.shape, 1)
    total = jnp.zeros(sum_ref.shape, F32)
    for k, value in enumerate(sums):
        total = jnp.where(lane == k, value, total)
    sum_ref[...] = total
    grad_x = line_blur(smooth[0:lines], False)
    grad_y = line_blur(smooth[lines : 2 * lines], True)
    grad_z = line_blur(smooth[2 * lines : 3 * lines], False)
    store_fields([grad_x, grad_y, grad_z], lines, out_ref)


def sample_kernel(his, rb, start, got_ref, field_ref, out_ref, force_ref):
    slots = out_ref.shape[0]
    beads = got_ref.shape[1] // 3
    lo_iota = lax.broadcasted_iota(I32, (LO, beads), 0)
    sub_iota = lax.broadcasted_iota(I32, (8, beads), 0)

    def body(i, carry):
        word = got_ref[pl.ds(start + i * rb, rb), 0:beads]
        lo = word & (LO - 1)
        hi = (word >> 8) & 255
        picks = [
            jnp.where(lo_iota == lo[q : q + 1], 1.0, 0.0).astype(BF16) for q in range(rb)
        ]
        pick = jnp.concatenate(picks, axis=1)
        sampled = jnp.dot(
            field_ref[...], jnp.concatenate([pick, pick], axis=0), preferred_element_type=F32
        )
        for q in range(rb):
            own = jnp.broadcast_to(hi[q : q + 1], (8, beads))
            group, within = own >> 3, (own & 7) == sub_iota
            found = [jnp.zeros((8, beads), F32)] * 3
            for j in range(his // 8):
                here = group == j
                for k in range(3):
                    rows = slice(k * his + 8 * j, k * his + 8 * j + 8)
                    found[k] = jnp.where(
                        here, sampled[rows, q * beads : (q + 1) * beads], found[k]
                    )
            for k in range(3):
                value = jnp.sum(jnp.where(within, found[k], 0.0), axis=0, keepdims=True)
                force_ref[k, pl.ds(i * rb + q, 1), :] = value
        return carry

    lax.fori_loop(0, slots // rb, body, 0)
    rows = slice(start, start + slots)
    first, second = got_ref[rows, beads : 2 * beads], got_ref[rows, 2 * beads : 3 * beads]
    weight = (got_ref[rows, 0:beads] >> 16).astype(F32) * (1.0 / WEIGHT_SCALE)
    lever_z = (((first & 2047) << 10) | (second & 1023)) - LEVER_BIAS
    levers = [
        v.astype(F32) * (1.0 / LEVER_SCALE) for v in (first >> 11, second >> 11, lever_z)
    ]
    force = [force_ref[k] * weight for k in range(3)]
    terms = force + [
        levers[1] * force[2] - levers[2] * force[1],
        levers[2] * force[0] - levers[0] * force[2],
        levers[0] * force[1] - levers[1] * force[0],
    ]
    lane = lax.broadcasted_iota(I32, out_ref.shape, 1)
    total = jnp.zeros(out_ref.shape, F32)
    for k, term in enumerate(terms):
        total = jnp.where(lane == k, jnp.sum(term, axis=1, keepdims=True), total)
    out_ref[...] = total


def join_kernel(most, first_ref, second_ref, model_ref, sum_ref, out_ref):
    bricks = out_ref.shape[0]
    lane = lax.broadcasted_iota(I32, out_ref.shape, 1)
    sums = sum_ref[0:1, :]
    for k in range(1, sum_ref.shape[0] // 8):
        sums = sums + sum_ref[8 * k : 8 * k + 1, :]
    total = jnp.zeros(out_ref.shape, F32)
    for k in range(most):
        rows, half = pl.ds(k, bricks, stride=most), pl.ds(k, bricks // 2, stride=most)
        own = jnp.concatenate([first_ref[half, :], second_ref[half, :]], axis=0)
        own = jnp.where(lane < 6, own, 0.0)
        own = own + pltpu.roll(jnp.where(lane < 6, model_ref[rows, :], 0.0), 6, 1)
        if k == 0:
            own = own + pltpu.roll(jnp.where(lane < 3, sums, 0.0), 12, 1)
        total = total + (pltpu.roll(own, FIELDS * k, 1) if k else own)
    out_ref[...] = total


def finish_kernel(most, voxel_total, place_ref, back_ref, out_ref):
    frags = out_ref.shape[1]
    bricks = back_ref.shape[0]
    row, rank = place_ref[0:1, :], place_ref[1:2, :]
    place = jnp.where(lax.broadcasted_iota(I32, (bricks, frags), 0) == row, 1.0, 0.0).astype(F32)
    back = back_ref[...]
    sums = jnp.sum(back, axis=0, keepdims=True)
    cross, model_sq, target_sq = sums[:, 12:13], sums[:, 13:14], sums[:, 14:15]
    norm_model = jnp.sqrt(model_sq + EPSILON)
    norm_target = jnp.sqrt(target_sq + EPSILON)
    corr = cross / (norm_model * norm_target)
    scale_target = voxel_total / (norm_model * norm_target)
    scale_model = voxel_total * corr / (norm_model * norm_model)
    found = lax.dot_general(
        back, place, (((0,), (0,)), ((), ())), precision=HIGHEST, preferred_element_type=F32
    )
    mine = jnp.zeros((FIELDS, frags), F32)
    for k in range(most):
        mine = jnp.where(rank == k, found[FIELDS * k : FIELDS * (k + 1)], mine)
    out_ref[...] = scale_target * mine[0:6] - scale_model * mine[6:12]


def cost(macs, nbytes):
    return pl.CostEstimate(flops=2 * macs, bytes_accessed=nbytes, transcendentals=0)


def call(
    kernel, out_shape, *args, scratch=(), name=None, macs=0, in_specs=None, vmem=VMEM_BYTES
):
    kwargs = {} if in_specs is None else {"in_specs": in_specs}
    return pl.pallas_call(
        kernel,
        out_shape=out_shape,
        scratch_shapes=list(scratch),
        compiler_params=pltpu.CompilerParams(vmem_limit_bytes=vmem),
        cost_estimate=cost(macs, 4 * sum(a.size for a in args)),
        name=name,
        **kwargs,
    )(*args)


def call_at(kernel, out_shape, index, table, *args, name=None, macs=0):
    def whole(shape):
        return pl.BlockSpec(shape, lambda i, s: (0,) * len(shape))

    single = not isinstance(out_shape, list)
    outs = [out_shape] if single else out_shape
    specs = [whole(o.shape) for o in outs]
    return pl.pallas_call(
        kernel,
        out_shape=out_shape,
        grid_spec=pltpu.PrefetchScalarGridSpec(
            num_scalar_prefetch=1,
            grid=(1,),
            in_specs=[pl.BlockSpec((1,) + table.shape[1:], lambda i, s: (s[0], 0, 0))]
            + [whole(a.shape) for a in args],
            out_specs=specs[0] if single else specs,
        ),
        compiler_params=pltpu.CompilerParams(vmem_limit_bytes=VMEM_BYTES),
        cost_estimate=cost(macs, 4 * sum(a.size for a in args)),
        name=name,
    )(index, table, *args)


def looked_up(values, position):
    found = jnp.full((), int(values[0]), I32)
    for i in range(1, len(values)):
        step = int(values[i]) - int(values[i - 1])
        if step:
            found = found + step * (position >= i).astype(I32)
    return found


def shifted(value, axis, step):
    size = lax.axis_size(axis)
    pairs = [(i, i + step) for i in range(size) if 0 <= i + step < size]
    return lax.ppermute(value, axis, pairs)


def relay_blocks(value, reach):
    size = lax.axis_size("relay")
    if size == 2:
        return [value, lax.ppermute(value, "relay", [(0, 1), (1, 0)])]
    blocks = [value]
    for step in range(1, min(reach, size - 1) + 1):
        blocks += [shifted(value, "relay", step), shifted(value, "relay", -step)]
    return blocks


def relay_order(size, reach):
    if size == 2:
        return lambda r: [r, 1 - r]
    steps = [0]
    for step in range(1, min(reach, size - 1) + 1):
        steps += [-step, step]
    return lambda r: [r + s for s in steps]


def relay_total(value):
    size = lax.axis_size("relay")
    values, moving = [value], value
    for _ in range(size - 1):
        moving = lax.ppermute(moving, "relay", [(i, (i + 1) % size) for i in range(size)])
        values.append(moving)
    return jnp.concatenate(values, axis=0)


def shards(target, frag_brick, bead_cell, bead_weight, bead_arm, frag_angle):
    brick_count, relay_count = lax.axis_size("brick"), lax.axis_size("relay")
    frags, beads = bead_cell.shape
    planes, columns, rows = target.shape
    lines = planes * columns
    his = lines * (rows // LO)
    assert rows % LO == 0 and his <= 256 and columns >= 2 * KR
    voxel_total = float(brick_count * columns * relay_count * planes * rows)
    most = max(2, 2 * frags // brick_count)
    slots = brick_count * most
    assert most * FIELDS <= 128

    z_total, x_total = relay_count * planes, brick_count * columns
    gz, dz = axis_matrix(z_total, False), axis_matrix(z_total, True)
    gx, dx = axis_matrix(x_total, False), axis_matrix(x_total, True)
    reach_one, reach_two = -(-KR // planes), -(-2 * KR // planes)
    target_table, tz, tx, tn = weight_table(
        [gz, gz, dz], [dx, gx, gx], planes, relay_count, relay_order(relay_count, reach_one),
        columns, brick_count,
        [np.arange(columns), np.arange(-KR, 0), np.arange(columns, columns + KR)],
    )
    model_table, mz, mx, mn = weight_table(
        [gz @ gz, gz @ gz, dz @ gz, gz], [dx @ gx, gx @ gx, gx @ gx, gx],
        planes, relay_count, relay_order(relay_count, reach_two), columns, brick_count,
        [np.arange(columns), np.arange(-columns, 0), np.arange(columns, 2 * columns)],
    )
    r, b = lax.axis_index("relay"), lax.axis_index("brick")
    target_index = (looked_up(tz, r) * tn + looked_up(tx, b)).reshape(1)
    model_index = (looked_up(mz, r) * mn + looked_up(mx, b)).reshape(1)

    target_lines = target.reshape(lines, rows)
    words = jax.ShapeDtypeStruct((lines // 2, rows + SCALE_LANES), I32)
    target_blocks = relay_blocks(call(encode_kernel, words, target_lines, name="encode"), reach_one)
    by_column = [t.reshape(-1, columns, rows + SCALE_LANES) for t in target_blocks]
    left_edge = jnp.concatenate([t[:, columns - KR :] for t in by_column], axis=0)
    right_edge = jnp.concatenate([t[:, :KR] for t in by_column], axis=0)
    from_left = shifted(left_edge.reshape(-1, rows + SCALE_LANES), "brick", 1)
    from_right = shifted(right_edge.reshape(-1, rows + SCALE_LANES), "brick", -1)

    hbm = pl.BlockSpec(memory_space=pltpu.HBM)
    packed = [frag_brick.reshape(1, frags), frag_angle, bead_cell, bead_weight, bead_arm]
    sent, place = call(
        functools.partial(pack_kernel, most, lines, rows),
        [
            jax.ShapeDtypeStruct((slots, 3 * beads), I32),
            jax.ShapeDtypeStruct((8, frags), I32),
        ],
        *packed,
        in_specs=[hbm] * len(packed),
        scratch=[pltpu.VMEM(a.shape, a.dtype) for a in packed]
        + [pltpu.SemaphoreType.DMA((len(packed),))],
        name="pack",
        vmem=PACK_VMEM_BYTES,
    )
    got = lax.all_to_all(sent, "brick", split_axis=0, concat_axis=0, tiled=True)
    smooth, coded = call(
        functools.partial(splat_kernel, lines, min(32, slots)),
        [jax.ShapeDtypeStruct((lines, rows), F32), words],
        got,
        scratch=[pltpu.VMEM((his, LO), F32)],
        name="splat",
        macs=slots * beads * his * LO,
    )
    coded, from_left, from_right = lax.optimization_barrier((coded, from_left, from_right))
    target_parts = [target_lines] + target_blocks[1:] + [from_left, from_right]
    blocks = relay_blocks(coded, reach_two)
    target_field = call_at(
        functools.partial(target_kernel, lines),
        jax.ShapeDtypeStruct((3 * his, 2 * LO), BF16),
        target_index, jnp.asarray(target_table), *target_parts,
        name="target_fields",
        macs=9 * lines * rows * 128,
    )

    def sample(field, start, count, name):
        return call(
            functools.partial(sample_kernel, his, min(32, count), start),
            jax.ShapeDtypeStruct((count, 128), F32),
            got, field,
            scratch=[pltpu.VMEM((3, count, beads), F32)],
            name=name,
            macs=6 * count * beads * his * LO,
        )

    half = slots // 2
    target_first = sample(target_field, 0, half, "target_sample_a")
    blocks, target_first, target_field = lax.optimization_barrier(
        (blocks, target_first, target_field)
    )
    beside = jnp.concatenate(blocks, axis=0)
    model_parts = [smooth] + blocks[1:]
    model_parts += [shifted(beside, "brick", 1), shifted(beside, "brick", -1)]
    target_second = sample(target_field, half, slots - half, "target_sample_b")
    target_second, *model_parts = lax.optimization_barrier((target_second, *model_parts))
    model_field, partial = call_at(
        functools.partial(model_kernel, lines),
        [
            jax.ShapeDtypeStruct((3 * his, 2 * LO), BF16),
            jax.ShapeDtypeStruct((8, 128), F32),
        ],
        model_index, jnp.asarray(model_table), target_lines, *model_parts,
        name="model_fields",
    )
    partials = relay_total(partial)
    model_sums = sample(model_field, 0, slots, "model_sample")
    leaving = call(
        functools.partial(join_kernel, most),
        jax.ShapeDtypeStruct((brick_count, 128), F32),
        target_first, target_second, model_sums, partials,
        name="join",
    )
    back = lax.all_to_all(leaving, "brick", split_axis=0, concat_axis=0, tiled=True)
    return call(
        functools.partial(finish_kernel, most, voxel_total),
        jax.ShapeDtypeStruct((6, frags), F32),
        place, back,
        name="finish",
    )


def solution(mesh):
    placed = (
        P("relay", "brick", None),
        P(("brick", "relay"), None),
        P(("brick", "relay"), None),
        P(("brick", "relay"), None),
        P(None, ("brick", "relay"), None),
        P(None, ("brick", "relay")),
    )
    return jax.shard_map(
        shards, mesh=mesh, in_specs=placed, out_specs=P(None, ("brick", "relay")), check_vma=False
    )
```

```python
import functools

import jax
import jax.numpy as jnp
import numpy as np
from jax import lax
from jax.experimental import pallas as pl
from jax.experimental.pallas import tpu as pltpu
from jax.sharding import PartitionSpec as P

KR = 4
SIGMA = 1.5
EPSILON = 1e-06
HIGHEST = lax.Precision.HIGHEST
LO = 256
FIELDS = 16
WEIGHT_SCALE = 512.0
LEVER_SCALE = 32768.0
LEVER_BIAS = 1 << 20
CODE_TOP = 65535
SCALE_UNIT = 512.0
SCALE_LANES = 128
VMEM_BYTES = 48 << 20
PACK_VMEM_BYTES = 60 << 20
F32 = jnp.float32
BF16 = jnp.bfloat16
I32 = jnp.int32


def taps_of(derivative):
    offsets = np.arange(-KR, KR + 1) * 1.0
    gaussian = np.exp(-(offsets**2) / (2.0 * SIGMA**2))
    gaussian = gaussian / gaussian.sum()
    if derivative:
        return -offsets / SIGMA**2 * gaussian
    return gaussian


def axis_matrix(length, derivative):
    offsets = np.arange(length)[:, None] - np.arange(length)[None, :]
    return np.where(
        np.abs(offsets) <= KR, taps_of(derivative)[np.clip(offsets + KR, 0, 2 * KR)], 0.0
    )


def columns_at(matrix, rows, wanted):
    inside = (wanted >= 0) & (wanted < matrix.shape[1])
    picked = matrix[rows][:, np.clip(wanted, 0, matrix.shape[1] - 1)]
    return np.where(inside[None, :], picked, 0.0)


def unique_tables(tables):
    flat = np.stack([t.reshape(-1) for t in tables])
    kept, inverse = np.unique(np.round(flat, 14), axis=0, return_inverse=True)
    return kept.reshape((-1,) + tables[0].shape), inverse.reshape(-1).astype(np.int32)


def pieces_np(table):
    import ml_dtypes

    high = table.astype(np.float32).astype(ml_dtypes.bfloat16)
    low = (table - high.astype(np.float64)).astype(ml_dtypes.bfloat16)
    return np.concatenate([high, high, low], axis=-1)


def weight_table(z_kinds, x_kinds, z_len, z_count, z_blocks, x_len, x_count, x_parts):
    z_tables = []
    for r in range(z_count):
        wanted = np.concatenate([np.arange(z_len) + z_len * block for block in z_blocks(r)])
        rows = np.arange(z_len) + z_len * r
        z_tables.append(np.stack([columns_at(m, rows, wanted) for m in z_kinds]))
    x_tables = []
    for b in range(x_count):
        wanted = np.concatenate([x_len * b + part for part in x_parts])
        rows = np.arange(x_len) + x_len * b
        x_tables.append(np.stack([columns_at(m, rows, wanted) for m in x_kinds]))
    z_tables, z_inverse = unique_tables(z_tables)
    x_tables, x_inverse = unique_tables(x_tables)
    kinds = len(z_kinds)
    parts, start = [], 0
    for part in x_parts:
        piece = x_tables[:, :, :, start : start + len(part)]
        start += len(part)
        full = np.einsum("rkzi,bkxj->rbkzxij", z_tables, piece)
        parts.append(
            full.reshape(len(z_tables) * len(x_tables), kinds * z_len * x_len, -1)
        )
    table = pieces_np(np.concatenate(parts, axis=-1))
    return table, z_inverse, x_inverse, len(x_tables)


def eye_column(row, eye):
    return jnp.sum(jnp.where(eye, row, jnp.zeros_like(row)), axis=1, keepdims=True)


def slot_row(row, most):
    frags = row.shape[1]
    sub = lax.broadcasted_iota(I32, (frags, frags), 0)
    lane = lax.broadcasted_iota(I32, (frags, frags), 1)
    eye = sub == lane
    earlier = jnp.logical_and(eye_column(row, eye) == row, sub < lane)
    return jnp.sum(jnp.where(earlier, 1, 0), axis=0, keepdims=True), eye


def pack_kernel(most, lines, row_count, *refs):
    inputs, (out_ref, place_ref), held, sems = refs[:5], refs[5:7], refs[7:12], refs[12]
    copies = [
        pltpu.make_async_copy(source, target, sems.at[k])
        for k, (source, target) in enumerate(zip(inputs, held))
    ]
    for copy in copies:
        copy.start()
    brick_ref, angle_ref, cell_ref, weight_ref, arm_ref = held
    for copy in copies[:2]:
        copy.wait()
    frags, beads = cell_ref.shape
    slots = out_ref.shape[0]
    row = brick_ref[...]
    rank, eye = slot_row(row, most)
    slot = row * most + rank
    place = jnp.where(lax.broadcasted_iota(I32, (slots, frags), 0) == slot, 1.0, 0.0).astype(F32)

    angles = angle_ref[...]
    cos, sin = jnp.cos(angles), jnp.sin(angles)
    cos_a, cos_b, cos_c = cos[0:1], cos[1:2], cos[2:3]
    sin_a, sin_b, sin_c = sin[0:1], sin[1:2], sin[2:3]
    turn = [
        [cos_a * cos_b, cos_a * sin_b * sin_c - sin_a * cos_c, cos_a * sin_b * cos_c + sin_a * sin_c],
        [sin_a * cos_b, sin_a * sin_b * sin_c + cos_a * cos_c, sin_a * sin_b * cos_c - cos_a * sin_c],
        [-sin_b, cos_b * sin_c, cos_b * cos_c],
    ]
    turn = [[eye_column(value, eye) for value in values] for values in turn]
    place_ref[0:1, :] = row
    place_ref[1:2, :] = rank
    for copy in copies[2:]:
        copy.wait()
    levers = []
    for i in range(3):
        total = turn[i][0] * arm_ref[0]
        for j in (1, 2):
            total = total + turn[i][j] * arm_ref[j]
        levers.append(jnp.round(total * LEVER_SCALE))

    cell = cell_ref[...]
    line = ((cell.astype(F32) + 0.5) * (1.0 / row_count)).astype(I32)
    y = cell - line * row_count
    code = (((y // LO) * lines + line) * LO + (y % LO)).astype(F32)
    weight = weight_ref[...].astype(F32) * WEIGHT_SCALE
    payload = jnp.concatenate([code, weight] + levers, axis=1)
    placed = jnp.dot(place, payload, precision=HIGHEST, preferred_element_type=F32)
    placed = placed.astype(I32)
    code, weight, lx, ly, lz = [placed[:, k * beads : (k + 1) * beads] for k in range(5)]
    lz = lz + LEVER_BIAS
    out_ref[:, 0:beads] = code | (weight << 16)
    out_ref[:, beads : 2 * beads] = (lx << 11) | (lz >> 10)
    out_ref[:, 2 * beads : 3 * beads] = (ly << 11) | (lz & 1023)


def line_blur(value, derivative):
    taps = taps_of(derivative)
    rows, length = value.shape
    wide = jnp.concatenate([value, jnp.zeros((rows, 128), F32)], axis=1)
    total = None if derivative else float(taps[KR]) * value
    for d in range(1, KR + 1):
        up = pltpu.roll(wide, d, 1)[:, :length]
        down = pltpu.roll(wide, length + 128 - d, 1)[:, :length]
        pair = up - down if derivative else up + down
        term = float(taps[KR + d]) * pair
        total = term if total is None else total + term
    return total


def encode(value, out_ref):
    half, length = value.shape[0] // 2, value.shape[1]
    top = (jnp.max(value) * SCALE_UNIT).astype(I32) + 1
    scale = (SCALE_UNIT * CODE_TOP) / top.astype(F32)
    code = jnp.minimum((value * scale + 0.5).astype(I32), CODE_TOP)
    out_ref[:, :length] = code[:half] | (code[half:] << 16)
    out_ref[:, length:] = jnp.full((half, SCALE_LANES), top, I32)


def decode(words, count):
    half, length = words.shape[0] // count, words.shape[1] - SCALE_LANES
    step = words[:, length : length + 1].astype(F32) * (1.0 / (SCALE_UNIT * CODE_TOP))
    low = (words[:, :length] & CODE_TOP).astype(F32) * step
    high = ((words[:, :length] >> 16) & CODE_TOP).astype(F32) * step
    lines = []
    for k in range(count):
        rows = slice(k * half, (k + 1) * half)
        lines += [low[rows], high[rows]]
    return lines


def encode_kernel(value_ref, out_ref):
    encode(value_ref[...], out_ref)


def splat_kernel(lines, rb, got_ref, out_ref, code_ref, acc_ref):
    slots = got_ref.shape[0]
    beads = got_ref.shape[1] // 3
    his = acc_ref.shape[0]
    acc_ref[...] = jnp.zeros_like(acc_ref)
    hi_iota = lax.broadcasted_iota(I32, (his, beads), 0)
    lo_iota = lax.broadcasted_iota(I32, (LO, beads), 0)

    def body(i, carry):
        word = got_ref[pl.ds(i * rb, rb), 0:beads]
        lo = word & (LO - 1)
        hi = (word >> 8) & 255
        weight = (word >> 16).astype(F32) * (1.0 / WEIGHT_SCALE)
        left, right = [], []
        for q in range(rb):
            left.append(jnp.where(hi_iota == hi[q : q + 1], weight[q : q + 1], 0.0).astype(BF16))
            right.append(jnp.where(lo_iota == lo[q : q + 1], 1.0, 0.0).astype(BF16))
        acc_ref[...] += lax.dot_general(
            jnp.concatenate(left, axis=1),
            jnp.concatenate(right, axis=1),
            (((1,), (1,)), ((), ())),
            preferred_element_type=F32,
        )
        return carry

    lax.fori_loop(0, slots // rb, body, 0)
    density = [acc_ref[yh * lines : (yh + 1) * lines, :] for yh in range(his // lines)]
    smooth = line_blur(jnp.concatenate(density, axis=1), False)
    out_ref[...] = smooth
    encode(smooth, code_ref)


def split(value):
    high = value.astype(BF16)
    low = (value - high.astype(F32)).astype(BF16)
    return high, low


def mix_lines(table_ref, parts):
    value = jnp.concatenate(parts, axis=0)
    high, low = split(value)
    return jnp.dot(
        table_ref[0], jnp.concatenate([high, low, high], axis=0), preferred_element_type=F32
    )


def store_fields(fields, lines, out_ref, exact_ref):
    his = fields[0].shape[1] // LO * lines
    for k, field in enumerate(fields):
        exact_ref[k * lines : (k + 1) * lines, :] = field
        for yh in range(field.shape[1] // LO):
            high, low = split(field[:, yh * LO : (yh + 1) * LO])
            rows = slice(k * his + yh * lines, k * his + (yh + 1) * lines)
            out_ref[rows, 0:LO] = high
            out_ref[rows, LO : 2 * LO] = low


def window_lines(own_ref, near_refs, left_ref, right_ref):
    lines = [own_ref[...]]
    for ref in near_refs:
        lines += decode(ref[...], 1)
    for ref in (left_ref, right_ref):
        lines += decode(ref[...], len(near_refs) + 1)
    return lines


def target_kernel(lines, _, table_ref, own_ref, *refs):
    *near_refs, left_ref, right_ref, out_ref, exact_ref = refs
    mixed = mix_lines(table_ref, window_lines(own_ref, near_refs, left_ref, right_ref))
    grad_x = line_blur(mixed[0:lines], False)
    grad_y = line_blur(mixed[lines : 2 * lines], True)
    grad_z = line_blur(mixed[2 * lines : 3 * lines], False)
    store_fields([grad_x, grad_y, grad_z], lines, out_ref, exact_ref)


def model_kernel(lines, _, table_ref, target_ref, own_ref, *refs):
    *near_refs, left_ref, right_ref, out_ref, exact_ref, sum_ref = refs
    smooth = mix_lines(table_ref, window_lines(own_ref, near_refs, left_ref, right_ref))
    model = smooth[3 * lines :]
    target = target_ref[...]
    sums = [jnp.sum(model * target), jnp.sum(model * model), jnp.sum(target * target)]
    lane = lax.broadcasted_iota(I32, sum_ref.shape, 1)
    total = jnp.zeros(sum_ref.shape, F32)
    for k, value in enumerate(sums):
        total = jnp.where(lane == k, value, total)
    sum_ref[...] = total
    grad_x = line_blur(smooth[0:lines], False)
    grad_y = line_blur(smooth[lines : 2 * lines], True)
    grad_z = line_blur(smooth[2 * lines : 3 * lines], False)
    store_fields([grad_x, grad_y, grad_z], lines, out_ref, exact_ref)


def sample_by_matmul(word, field_ref, his, store):
    count, beads = word.shape
    lo, hi = word & (LO - 1), (word >> 8) & 255
    lo_iota = lax.broadcasted_iota(I32, (LO, beads), 0)
    picks = [jnp.where(lo_iota == lo[q : q + 1], 1.0, 0.0).astype(BF16) for q in range(count)]
    pick = jnp.concatenate(picks, axis=1)
    sampled = jnp.dot(
        field_ref[...], jnp.concatenate([pick, pick], axis=0), preferred_element_type=F32
    )

    def finish():
        sub_iota = lax.broadcasted_iota(I32, (8, beads), 0)
        for q in range(count):
            own = jnp.broadcast_to(hi[q : q + 1], (8, beads))
            group, within = own >> 3, (own & 7) == sub_iota
            found = [jnp.zeros((8, beads), F32)] * 3
            for j in range(his // 8):
                here = group == j
                for k in range(3):
                    rows = slice(k * his + 8 * j, k * his + 8 * j + 8)
                    part = sampled[rows, q * beads : (q + 1) * beads]
                    found[k] = jnp.where(here, part, found[k])
            store(q, [jnp.sum(jnp.where(within, v, 0.0), axis=0, keepdims=True) for v in found])

    return finish


def sample_by_lanes(word, exact_ref, lines, store):
    count, beads = word.shape
    tiles = exact_ref.shape[1] // 128
    line_shift, lo_shift = lines.bit_length() - 1, LO.bit_length() - 1
    sub_iota = lax.broadcasted_iota(I32, (8, beads), 0)
    for q in range(count):
        own = jnp.broadcast_to(word[q : q + 1], (8, beads))
        lo, hi = own & (LO - 1), (own >> lo_shift) & 255
        line = hi & (lines - 1)
        group = (line >> 3) * tiles + (hi >> line_shift) * (LO // 128) + (lo >> 7)
        within, lane = (line & 7) == sub_iota, lo & 127
        found = [jnp.zeros((8, beads), F32)] * 3
        for j in range(lines // 8 * tiles):
            here = group == j
            first, tile = j // tiles * 8, j % tiles * 128
            for k in range(3):
                table = exact_ref[k * lines + first : k * lines + first + 8, tile : tile + 128]
                part = jnp.take_along_axis(table, lane, axis=1, mode="promise_in_bounds")
                found[k] = jnp.where(here, part, found[k])
        store(q, [jnp.sum(jnp.where(within, v, 0.0), axis=0, keepdims=True) for v in found])


def sample_kernel(
    lines, his, rb, by_lanes, start, got_ref, field_ref, exact_ref, out_ref, force_ref
):
    slots = out_ref.shape[0]
    beads = got_ref.shape[1] // 3
    by_matmul = rb - by_lanes

    def body(i, carry):
        def store_from(first):
            def store(q, values):
                for k in range(3):
                    force_ref[k, pl.ds(i * rb + first + q, 1), :] = values[k]

            return store

        word = got_ref[pl.ds(start + i * rb, rb), 0:beads]
        finish = sample_by_matmul(word[:by_matmul], field_ref, his, store_from(0))
        sample_by_lanes(word[by_matmul:], exact_ref, lines, store_from(by_matmul))
        finish()
        return carry

    lax.fori_loop(0, slots // rb, body, 0)
    rows = slice(start, start + slots)
    first, second = got_ref[rows, beads : 2 * beads], got_ref[rows, 2 * beads : 3 * beads]
    weight = (got_ref[rows, 0:beads] >> 16).astype(F32) * (1.0 / WEIGHT_SCALE)
    lever_z = (((first & 2047) << 10) | (second & 1023)) - LEVER_BIAS
    levers = [
        v.astype(F32) * (1.0 / LEVER_SCALE) for v in (first >> 11, second >> 11, lever_z)
    ]
    force = [force_ref[k] * weight for k in range(3)]
    terms = force + [
        levers[1] * force[2] - levers[2] * force[1],
        levers[2] * force[0] - levers[0] * force[2],
        levers[0] * force[1] - levers[1] * force[0],
    ]
    lane = lax.broadcasted_iota(I32, out_ref.shape, 1)
    total = jnp.zeros(out_ref.shape, F32)
    for k, term in enumerate(terms):
        total = jnp.where(lane == k, jnp.sum(term, axis=1, keepdims=True), total)
    out_ref[...] = total


def join_kernel(most, first_ref, second_ref, model_ref, sum_ref, out_ref):
    bricks = out_ref.shape[0]
    lane = lax.broadcasted_iota(I32, out_ref.shape, 1)
    sums = sum_ref[0:1, :]
    for k in range(1, sum_ref.shape[0] // 8):
        sums = sums + sum_ref[8 * k : 8 * k + 1, :]
    total = jnp.zeros(out_ref.shape, F32)
    for k in range(most):
        rows, half = pl.ds(k, bricks, stride=most), pl.ds(k, bricks // 2, stride=most)
        own = jnp.concatenate([first_ref[half, :], second_ref[half, :]], axis=0)
        own = jnp.where(lane < 6, own, 0.0)
        own = own + pltpu.roll(jnp.where(lane < 6, model_ref[rows, :], 0.0), 6, 1)
        if k == 0:
            own = own + pltpu.roll(jnp.where(lane < 3, sums, 0.0), 12, 1)
        total = total + (pltpu.roll(own, FIELDS * k, 1) if k else own)
    out_ref[...] = total


def finish_kernel(most, voxel_total, place_ref, back_ref, out_ref):
    frags = out_ref.shape[1]
    bricks = back_ref.shape[0]
    row, rank = place_ref[0:1, :], place_ref[1:2, :]
    place = jnp.where(lax.broadcasted_iota(I32, (bricks, frags), 0) == row, 1.0, 0.0).astype(F32)
    back = back_ref[...]
    sums = jnp.sum(back, axis=0, keepdims=True)
    cross, model_sq, target_sq = sums[:, 12:13], sums[:, 13:14], sums[:, 14:15]
    norm_model = jnp.sqrt(model_sq + EPSILON)
    norm_target = jnp.sqrt(target_sq + EPSILON)
    corr = cross / (norm_model * norm_target)
    scale_target = voxel_total / (norm_model * norm_target)
    scale_model = voxel_total * corr / (norm_model * norm_model)
    found = lax.dot_general(
        back, place, (((0,), (0,)), ((), ())), precision=HIGHEST, preferred_element_type=F32
    )
    mine = jnp.zeros((FIELDS, frags), F32)
    for k in range(most):
        mine = jnp.where(rank == k, found[FIELDS * k : FIELDS * (k + 1)], mine)
    out_ref[...] = scale_target * mine[0:6] - scale_model * mine[6:12]


def cost(macs, nbytes):
    return pl.CostEstimate(flops=2 * macs, bytes_accessed=nbytes, transcendentals=0)


def call(
    kernel, out_shape, *args, scratch=(), name=None, macs=0, in_specs=None, vmem=VMEM_BYTES
):
    kwargs = {} if in_specs is None else {"in_specs": in_specs}
    return pl.pallas_call(
        kernel,
        out_shape=out_shape,
        scratch_shapes=list(scratch),
        compiler_params=pltpu.CompilerParams(vmem_limit_bytes=vmem),
        cost_estimate=cost(macs, 4 * sum(a.size for a in args)),
        name=name,
        **kwargs,
    )(*args)


def call_at(kernel, out_shape, index, table, *args, name=None, macs=0):
    def whole(shape):
        return pl.BlockSpec(shape, lambda i, s: (0,) * len(shape))

    single = not isinstance(out_shape, list)
    outs = [out_shape] if single else out_shape
    specs = [whole(o.shape) for o in outs]
    return pl.pallas_call(
        kernel,
        out_shape=out_shape,
        grid_spec=pltpu.PrefetchScalarGridSpec(
            num_scalar_prefetch=1,
            grid=(1,),
            in_specs=[pl.BlockSpec((1,) + table.shape[1:], lambda i, s: (s[0], 0, 0))]
            + [whole(a.shape) for a in args],
            out_specs=specs[0] if single else specs,
        ),
        compiler_params=pltpu.CompilerParams(vmem_limit_bytes=VMEM_BYTES),
        cost_estimate=cost(macs, 4 * sum(a.size for a in args)),
        name=name,
    )(index, table, *args)


def looked_up(values, position):
    found = jnp.full((), int(values[0]), I32)
    for i in range(1, len(values)):
        step = int(values[i]) - int(values[i - 1])
        if step:
            found = found + step * (position >= i).astype(I32)
    return found


def shifted(value, axis, step):
    size = lax.axis_size(axis)
    pairs = [(i, i + step) for i in range(size) if 0 <= i + step < size]
    return lax.ppermute(value, axis, pairs)


def relay_blocks(value, reach):
    size = lax.axis_size("relay")
    if size == 2:
        return [value, lax.ppermute(value, "relay", [(0, 1), (1, 0)])]
    blocks = [value]
    for step in range(1, min(reach, size - 1) + 1):
        blocks += [shifted(value, "relay", step), shifted(value, "relay", -step)]
    return blocks


def relay_order(size, reach):
    if size == 2:
        return lambda r: [r, 1 - r]
    steps = [0]
    for step in range(1, min(reach, size - 1) + 1):
        steps += [-step, step]
    return lambda r: [r + s for s in steps]


def relay_total(value):
    size = lax.axis_size("relay")
    values, moving = [value], value
    for _ in range(size - 1):
        moving = lax.ppermute(moving, "relay", [(i, (i + 1) % size) for i in range(size)])
        values.append(moving)
    return jnp.concatenate(values, axis=0)


def shards(target, frag_brick, bead_cell, bead_weight, bead_arm, frag_angle):
    brick_count, relay_count = lax.axis_size("brick"), lax.axis_size("relay")
    frags, beads = bead_cell.shape
    planes, columns, rows = target.shape
    lines = planes * columns
    his = lines * (rows // LO)
    assert rows % LO == 0 and his <= 256 and columns >= 2 * KR
    assert beads == 128 and lines & (lines - 1) == 0
    voxel_total = float(brick_count * columns * relay_count * planes * rows)
    most = max(2, 2 * frags // brick_count)
    slots = brick_count * most
    assert most * FIELDS <= 128

    z_total, x_total = relay_count * planes, brick_count * columns
    gz, dz = axis_matrix(z_total, False), axis_matrix(z_total, True)
    gx, dx = axis_matrix(x_total, False), axis_matrix(x_total, True)
    reach_one, reach_two = -(-KR // planes), -(-2 * KR // planes)
    target_table, tz, tx, tn = weight_table(
        [gz, gz, dz], [dx, gx, gx], planes, relay_count, relay_order(relay_count, reach_one),
        columns, brick_count,
        [np.arange(columns), np.arange(-KR, 0), np.arange(columns, columns + KR)],
    )
    model_table, mz, mx, mn = weight_table(
        [gz @ gz, gz @ gz, dz @ gz, gz], [dx @ gx, gx @ gx, gx @ gx, gx],
        planes, relay_count, relay_order(relay_count, reach_two), columns, brick_count,
        [np.arange(columns), np.arange(-columns, 0), np.arange(columns, 2 * columns)],
    )
    r, b = lax.axis_index("relay"), lax.axis_index("brick")
    target_index = (looked_up(tz, r) * tn + looked_up(tx, b)).reshape(1)
    model_index = (looked_up(mz, r) * mn + looked_up(mx, b)).reshape(1)

    target_lines = target.reshape(lines, rows)
    words = jax.ShapeDtypeStruct((lines // 2, rows + SCALE_LANES), I32)
    target_blocks = relay_blocks(call(encode_kernel, words, target_lines, name="encode"), reach_one)
    by_column = [t.reshape(-1, columns, rows + SCALE_LANES) for t in target_blocks]
    left_edge = jnp.concatenate([t[:, columns - KR :] for t in by_column], axis=0)
    right_edge = jnp.concatenate([t[:, :KR] for t in by_column], axis=0)
    from_left = shifted(left_edge.reshape(-1, rows + SCALE_LANES), "brick", 1)
    from_right = shifted(right_edge.reshape(-1, rows + SCALE_LANES), "brick", -1)

    hbm = pl.BlockSpec(memory_space=pltpu.HBM)
    packed = [frag_brick.reshape(1, frags), frag_angle, bead_cell, bead_weight, bead_arm]
    sent, place = call(
        functools.partial(pack_kernel, most, lines, rows),
        [
            jax.ShapeDtypeStruct((slots, 3 * beads), I32),
            jax.ShapeDtypeStruct((8, frags), I32),
        ],
        *packed,
        in_specs=[hbm] * len(packed),
        scratch=[pltpu.VMEM(a.shape, a.dtype) for a in packed]
        + [pltpu.SemaphoreType.DMA((len(packed),))],
        name="pack",
        vmem=PACK_VMEM_BYTES,
    )
    got = lax.all_to_all(sent, "brick", split_axis=0, concat_axis=0, tiled=True)
    smooth, coded = call(
        functools.partial(splat_kernel, lines, min(32, slots)),
        [jax.ShapeDtypeStruct((lines, rows), F32), words],
        got,
        scratch=[pltpu.VMEM((his, LO), F32)],
        name="splat",
        macs=slots * beads * his * LO,
    )
    coded, from_left, from_right = lax.optimization_barrier((coded, from_left, from_right))
    target_parts = [target_lines] + target_blocks[1:] + [from_left, from_right]
    blocks = relay_blocks(coded, reach_two)
    field_shapes = [
        jax.ShapeDtypeStruct((3 * his, 2 * LO), BF16),
        jax.ShapeDtypeStruct((3 * lines, rows), F32),
    ]
    target_field = call_at(
        functools.partial(target_kernel, lines),
        field_shapes,
        target_index, jnp.asarray(target_table), *target_parts,
        name="target_fields",
        macs=9 * lines * rows * 128,
    )

    def sample(field, start, count, name):
        rb = min(32, count)
        return call(
            functools.partial(sample_kernel, lines, his, rb, rb * 5 // 16, start),
            jax.ShapeDtypeStruct((count, 128), F32),
            got, *field,
            scratch=[pltpu.VMEM((3, count, beads), F32)],
            name=name,
            macs=6 * count * beads * his * LO,
        )

    half = slots // 2
    target_first = sample(target_field, 0, half, "target_sample_a")
    blocks, target_first, target_field = lax.optimization_barrier(
        (blocks, target_first, target_field)
    )
    beside = jnp.concatenate(blocks, axis=0)
    model_parts = [smooth] + blocks[1:]
    model_parts += [shifted(beside, "brick", 1), shifted(beside, "brick", -1)]
    target_second = sample(target_field, half, slots - half, "target_sample_b")
    target_second, *model_parts = lax.optimization_barrier((target_second, *model_parts))
    *model_field, partial = call_at(
        functools.partial(model_kernel, lines),
        field_shapes + [jax.ShapeDtypeStruct((8, 128), F32)],
        model_index, jnp.asarray(model_table), target_lines, *model_parts,
        name="model_fields",
    )
    partials = relay_total(partial)
    model_sums = sample(model_field, 0, slots, "model_sample")
    leaving = call(
        functools.partial(join_kernel, most),
        jax.ShapeDtypeStruct((brick_count, 128), F32),
        target_first, target_second, model_sums, partials,
        name="join",
    )
    back = lax.all_to_all(leaving, "brick", split_axis=0, concat_axis=0, tiled=True)
    return call(
        functools.partial(finish_kernel, most, voxel_total),
        jax.ShapeDtypeStruct((6, frags), F32),
        place, back,
        name="finish",
    )


def solution(mesh):
    placed = (
        P("relay", "brick", None),
        P(("brick", "relay"), None),
        P(("brick", "relay"), None),
        P(("brick", "relay"), None),
        P(None, ("brick", "relay"), None),
        P(None, ("brick", "relay")),
    )
    return jax.shard_map(
        shards, mesh=mesh, in_specs=placed, out_specs=P(None, ("brick", "relay")), check_vma=False
    )
```

```python
import functools

import jax
import jax.numpy as jnp
import numpy as np
from jax import lax
from jax.experimental import pallas as pl
from jax.experimental.pallas import tpu as pltpu
from jax.sharding import PartitionSpec as P

KR = 4
SIGMA = 1.5
EPSILON = 1e-06
HIGHEST = lax.Precision.HIGHEST
LO = 256
FIELDS = 16
WEIGHT_SCALE = 512.0
LEVER_SCALE = 32768.0
LEVER_BIAS = 1 << 20
CODE_TOP = 65535
SCALE_UNIT = 512.0
SCALE_LANES = 128
VMEM_BYTES = 48 << 20
PACK_VMEM_BYTES = 60 << 20
F32 = jnp.float32
BF16 = jnp.bfloat16
I32 = jnp.int32


def taps_of(derivative):
    offsets = np.arange(-KR, KR + 1) * 1.0
    gaussian = np.exp(-(offsets**2) / (2.0 * SIGMA**2))
    gaussian = gaussian / gaussian.sum()
    if derivative:
        return -offsets / SIGMA**2 * gaussian
    return gaussian


def axis_matrix(length, derivative):
    offsets = np.arange(length)[:, None] - np.arange(length)[None, :]
    return np.where(
        np.abs(offsets) <= KR, taps_of(derivative)[np.clip(offsets + KR, 0, 2 * KR)], 0.0
    )


def columns_at(matrix, rows, wanted):
    inside = (wanted >= 0) & (wanted < matrix.shape[1])
    picked = matrix[rows][:, np.clip(wanted, 0, matrix.shape[1] - 1)]
    return np.where(inside[None, :], picked, 0.0)


def unique_tables(tables):
    flat = np.stack([t.reshape(-1) for t in tables])
    kept, inverse = np.unique(np.round(flat, 14), axis=0, return_inverse=True)
    return kept.reshape((-1,) + tables[0].shape), inverse.reshape(-1).astype(np.int32)


def pieces_np(table):
    import ml_dtypes

    high = table.astype(np.float32).astype(ml_dtypes.bfloat16)
    low = (table - high.astype(np.float64)).astype(ml_dtypes.bfloat16)
    return np.concatenate([high, high, low], axis=-1)


def weight_table(z_kinds, x_kinds, z_len, z_count, z_blocks, x_len, x_count, x_parts):
    z_tables = []
    for r in range(z_count):
        wanted = np.concatenate([np.arange(z_len) + z_len * block for block in z_blocks(r)])
        rows = np.arange(z_len) + z_len * r
        z_tables.append(np.stack([columns_at(m, rows, wanted) for m in z_kinds]))
    x_tables = []
    for b in range(x_count):
        wanted = np.concatenate([x_len * b + part for part in x_parts])
        rows = np.arange(x_len) + x_len * b
        x_tables.append(np.stack([columns_at(m, rows, wanted) for m in x_kinds]))
    z_tables, z_inverse = unique_tables(z_tables)
    x_tables, x_inverse = unique_tables(x_tables)
    kinds = len(z_kinds)
    parts, start = [], 0
    for part in x_parts:
        piece = x_tables[:, :, :, start : start + len(part)]
        start += len(part)
        full = np.einsum("rkzi,bkxj->rbkzxij", z_tables, piece)
        parts.append(
            full.reshape(len(z_tables) * len(x_tables), kinds * z_len * x_len, -1)
        )
    table = pieces_np(np.concatenate(parts, axis=-1))
    return table, z_inverse, x_inverse, len(x_tables)


def eye_column(row, eye):
    return jnp.sum(jnp.where(eye, row, jnp.zeros_like(row)), axis=1, keepdims=True)


def slot_row(row, most):
    frags = row.shape[1]
    sub = lax.broadcasted_iota(I32, (frags, frags), 0)
    lane = lax.broadcasted_iota(I32, (frags, frags), 1)
    eye = sub == lane
    earlier = jnp.logical_and(eye_column(row, eye) == row, sub < lane)
    return jnp.sum(jnp.where(earlier, 1, 0), axis=0, keepdims=True), eye


def pack_kernel(most, lines, row_count, *refs):
    inputs, (out_ref, place_ref, code_ref) = refs[:6], refs[6:9]
    held, sems = refs[9:15], refs[15]
    copies = [
        pltpu.make_async_copy(source, target, sems.at[k])
        for k, (source, target) in enumerate(zip(inputs, held))
    ]
    for copy in copies:
        copy.start()
    brick_ref, angle_ref, cell_ref, weight_ref, arm_ref, target_ref = held
    for copy in copies[:2]:
        copy.wait()
    frags, beads = cell_ref.shape
    slots = out_ref.shape[0]
    row = brick_ref[...]
    rank, eye = slot_row(row, most)
    slot = row * most + rank
    place = jnp.where(lax.broadcasted_iota(I32, (slots, frags), 0) == slot, 1.0, 0.0).astype(F32)

    angles = angle_ref[...]
    cos, sin = jnp.cos(angles), jnp.sin(angles)
    cos_a, cos_b, cos_c = cos[0:1], cos[1:2], cos[2:3]
    sin_a, sin_b, sin_c = sin[0:1], sin[1:2], sin[2:3]
    turn = [
        [cos_a * cos_b, cos_a * sin_b * sin_c - sin_a * cos_c, cos_a * sin_b * cos_c + sin_a * sin_c],
        [sin_a * cos_b, sin_a * sin_b * sin_c + cos_a * cos_c, sin_a * sin_b * cos_c - cos_a * sin_c],
        [-sin_b, cos_b * sin_c, cos_b * cos_c],
    ]
    turn = [[eye_column(value, eye) for value in values] for values in turn]
    place_ref[0:1, :] = row
    place_ref[1:2, :] = rank
    for copy in copies[2:]:
        copy.wait()
    encode(target_ref[...], code_ref)
    levers = []
    for i in range(3):
        total = turn[i][0] * arm_ref[0]
        for j in (1, 2):
            total = total + turn[i][j] * arm_ref[j]
        levers.append(jnp.round(total * LEVER_SCALE))

    cell = cell_ref[...]
    line = ((cell.astype(F32) + 0.5) * (1.0 / row_count)).astype(I32)
    y = cell - line * row_count
    code = (((y // LO) * lines + line) * LO + (y % LO)).astype(F32)
    weight = weight_ref[...].astype(F32) * WEIGHT_SCALE
    payload = jnp.concatenate([code, weight] + levers, axis=1)
    placed = jnp.dot(place, payload, precision=HIGHEST, preferred_element_type=F32)
    placed = placed.astype(I32)
    code, weight, lx, ly, lz = [placed[:, k * beads : (k + 1) * beads] for k in range(5)]
    lz = lz + LEVER_BIAS
    out_ref[:, 0:beads] = code | (weight << 16)
    out_ref[:, beads : 2 * beads] = (lx << 11) | (lz >> 10)
    out_ref[:, 2 * beads : 3 * beads] = (ly << 11) | (lz & 1023)


def line_blur(value, derivative):
    taps = taps_of(derivative)
    rows, length = value.shape
    wide = jnp.concatenate([value, jnp.zeros((rows, 128), F32)], axis=1)
    total = None if derivative else float(taps[KR]) * value
    for d in range(1, KR + 1):
        up = pltpu.roll(wide, d, 1)[:, :length]
        down = pltpu.roll(wide, length + 128 - d, 1)[:, :length]
        pair = up - down if derivative else up + down
        term = float(taps[KR + d]) * pair
        total = term if total is None else total + term
    return total


def encode(value, out_ref):
    half, length = value.shape[0] // 2, value.shape[1]
    top = (jnp.max(value) * SCALE_UNIT).astype(I32) + 1
    scale = (SCALE_UNIT * CODE_TOP) / top.astype(F32)
    code = jnp.minimum((value * scale + 0.5).astype(I32), CODE_TOP)
    out_ref[:, :length] = code[:half] | (code[half:] << 16)
    out_ref[:, length:] = jnp.full((half, SCALE_LANES), top, I32)


def decode(words, count):
    half, length = words.shape[0] // count, words.shape[1] - SCALE_LANES
    step = words[:, length : length + 1].astype(F32) * (1.0 / (SCALE_UNIT * CODE_TOP))
    low = (words[:, :length] & CODE_TOP).astype(F32) * step
    high = ((words[:, :length] >> 16) & CODE_TOP).astype(F32) * step
    lines = []
    for k in range(count):
        rows = slice(k * half, (k + 1) * half)
        lines += [low[rows], high[rows]]
    return lines


def splat_kernel(lines, rb, got_ref, out_ref, code_ref, acc_ref):
    slots = got_ref.shape[0]
    beads = got_ref.shape[1] // 3
    his = acc_ref.shape[0]
    acc_ref[...] = jnp.zeros_like(acc_ref)
    hi_iota = lax.broadcasted_iota(I32, (his, beads), 0)
    lo_iota = lax.broadcasted_iota(I32, (LO, beads), 0)

    def body(i, carry):
        word = got_ref[pl.ds(i * rb, rb), 0:beads]
        lo = word & (LO - 1)
        hi = (word >> 8) & 255
        weight = (word >> 16).astype(F32) * (1.0 / WEIGHT_SCALE)
        left, right = [], []
        for q in range(rb):
            left.append(jnp.where(hi_iota == hi[q : q + 1], weight[q : q + 1], 0.0).astype(BF16))
            right.append(jnp.where(lo_iota == lo[q : q + 1], 1.0, 0.0).astype(BF16))
        acc_ref[...] += lax.dot_general(
            jnp.concatenate(left, axis=1),
            jnp.concatenate(right, axis=1),
            (((1,), (1,)), ((), ())),
            preferred_element_type=F32,
        )
        return carry

    lax.fori_loop(0, slots // rb, body, 0)
    density = [acc_ref[yh * lines : (yh + 1) * lines, :] for yh in range(his // lines)]
    smooth = line_blur(jnp.concatenate(density, axis=1), False)
    out_ref[...] = smooth
    encode(smooth, code_ref)


def split(value):
    high = value.astype(BF16)
    low = (value - high.astype(F32)).astype(BF16)
    return high, low


def mix_lines(table_ref, parts):
    value = jnp.concatenate(parts, axis=0)
    high, low = split(value)
    return jnp.dot(
        table_ref[0], jnp.concatenate([high, low, high], axis=0), preferred_element_type=F32
    )


def store_fields(fields, lines, out_ref, exact_ref):
    his = fields[0].shape[1] // LO * lines
    for k, field in enumerate(fields):
        exact_ref[k * lines : (k + 1) * lines, :] = field
        for yh in range(field.shape[1] // LO):
            high, low = split(field[:, yh * LO : (yh + 1) * LO])
            rows = slice(k * his + yh * lines, k * his + (yh + 1) * lines)
            out_ref[rows, 0:LO] = high
            out_ref[rows, LO : 2 * LO] = low


def window_lines(own_ref, near_refs, left_ref, right_ref):
    lines = [own_ref[...]]
    for ref in near_refs:
        lines += decode(ref[...], 1)
    for ref in (left_ref, right_ref):
        lines += decode(ref[...], len(near_refs) + 1)
    return lines


def target_kernel(lines, _, table_ref, own_ref, *refs):
    *near_refs, left_ref, right_ref, out_ref, exact_ref = refs
    mixed = mix_lines(table_ref, window_lines(own_ref, near_refs, left_ref, right_ref))
    grad_x = line_blur(mixed[0:lines], False)
    grad_y = line_blur(mixed[lines : 2 * lines], True)
    grad_z = line_blur(mixed[2 * lines : 3 * lines], False)
    store_fields([grad_x, grad_y, grad_z], lines, out_ref, exact_ref)


def model_kernel(lines, _, table_ref, target_ref, own_ref, *refs):
    *near_refs, left_ref, right_ref, out_ref, exact_ref, sum_ref = refs
    smooth = mix_lines(table_ref, window_lines(own_ref, near_refs, left_ref, right_ref))
    model = smooth[3 * lines :]
    target = target_ref[...]
    sums = [jnp.sum(model * target), jnp.sum(model * model), jnp.sum(target * target)]
    lane = lax.broadcasted_iota(I32, sum_ref.shape, 1)
    total = jnp.zeros(sum_ref.shape, F32)
    for k, value in enumerate(sums):
        total = jnp.where(lane == k, value, total)
    sum_ref[...] = total
    grad_x = line_blur(smooth[0:lines], False)
    grad_y = line_blur(smooth[lines : 2 * lines], True)
    grad_z = line_blur(smooth[2 * lines : 3 * lines], False)
    store_fields([grad_x, grad_y, grad_z], lines, out_ref, exact_ref)


def sample_by_matmul(word, field_ref, his, store):
    count, beads = word.shape
    lo, hi = word & (LO - 1), (word >> 8) & 255
    lo_iota = lax.broadcasted_iota(I32, (LO, beads), 0)
    picks = [jnp.where(lo_iota == lo[q : q + 1], 1.0, 0.0).astype(BF16) for q in range(count)]
    pick = jnp.concatenate(picks, axis=1)
    sampled = jnp.dot(
        field_ref[...], jnp.concatenate([pick, pick], axis=0), preferred_element_type=F32
    )

    def finish():
        sub_iota = lax.broadcasted_iota(I32, (8, beads), 0)
        for q in range(count):
            own = jnp.broadcast_to(hi[q : q + 1], (8, beads))
            group, within = own >> 3, (own & 7) == sub_iota
            found = [jnp.zeros((8, beads), F32)] * 3
            for j in range(his // 8):
                here = group == j
                for k in range(3):
                    rows = slice(k * his + 8 * j, k * his + 8 * j + 8)
                    part = sampled[rows, q * beads : (q + 1) * beads]
                    found[k] = jnp.where(here, part, found[k])
            store(q, [jnp.sum(jnp.where(within, v, 0.0), axis=0, keepdims=True) for v in found])

    return finish


def sample_by_lanes(word, exact_ref, lines, store):
    count, beads = word.shape
    tiles = exact_ref.shape[1] // 128
    line_shift, lo_shift = lines.bit_length() - 1, LO.bit_length() - 1
    sub_iota = lax.broadcasted_iota(I32, (8, beads), 0)
    for q in range(count):
        own = jnp.broadcast_to(word[q : q + 1], (8, beads))
        lo, hi = own & (LO - 1), (own >> lo_shift) & 255
        line = hi & (lines - 1)
        group = (line >> 3) * tiles + (hi >> line_shift) * (LO // 128) + (lo >> 7)
        within, lane = (line & 7) == sub_iota, lo & 127
        found = [jnp.zeros((8, beads), F32)] * 3
        for j in range(lines // 8 * tiles):
            here = group == j
            first, tile = j // tiles * 8, j % tiles * 128
            for k in range(3):
                table = exact_ref[k * lines + first : k * lines + first + 8, tile : tile + 128]
                part = jnp.take_along_axis(table, lane, axis=1, mode="promise_in_bounds")
                found[k] = jnp.where(here, part, found[k])
        store(q, [jnp.sum(jnp.where(within, v, 0.0), axis=0, keepdims=True) for v in found])


def sample_kernel(
    lines, his, rb, by_lanes, start, got_ref, field_ref, exact_ref, out_ref, force_ref
):
    slots = out_ref.shape[0]
    beads = got_ref.shape[1] // 3
    by_matmul = rb - by_lanes

    def body(i, carry):
        def store_from(first):
            def store(q, values):
                for k in range(3):
                    force_ref[k, pl.ds(i * rb + first + q, 1), :] = values[k]

            return store

        word = got_ref[pl.ds(start + i * rb, rb), 0:beads]
        finish = sample_by_matmul(word[:by_matmul], field_ref, his, store_from(0))
        sample_by_lanes(word[by_matmul:], exact_ref, lines, store_from(by_matmul))
        finish()
        return carry

    lax.fori_loop(0, slots // rb, body, 0)
    rows = slice(start, start + slots)
    first, second = got_ref[rows, beads : 2 * beads], got_ref[rows, 2 * beads : 3 * beads]
    weight = (got_ref[rows, 0:beads] >> 16).astype(F32) * (1.0 / WEIGHT_SCALE)
    lever_z = (((first & 2047) << 10) | (second & 1023)) - LEVER_BIAS
    levers = [
        v.astype(F32) * (1.0 / LEVER_SCALE) for v in (first >> 11, second >> 11, lever_z)
    ]
    force = [force_ref[k] * weight for k in range(3)]
    terms = force + [
        levers[1] * force[2] - levers[2] * force[1],
        levers[2] * force[0] - levers[0] * force[2],
        levers[0] * force[1] - levers[1] * force[0],
    ]
    lane = lax.broadcasted_iota(I32, out_ref.shape, 1)
    total = jnp.zeros(out_ref.shape, F32)
    for k, term in enumerate(terms):
        total = jnp.where(lane == k, jnp.sum(term, axis=1, keepdims=True), total)
    out_ref[...] = total


def join_kernel(most, *refs):
    *target_refs, model_ref, sum_ref, out_ref = refs
    bricks = out_ref.shape[0]
    lane = lax.broadcasted_iota(I32, out_ref.shape, 1)
    sums = sum_ref[0:1, :]
    for k in range(1, sum_ref.shape[0] // 8):
        sums = sums + sum_ref[8 * k : 8 * k + 1, :]
    total = jnp.zeros(out_ref.shape, F32)
    for k in range(most):
        rows = pl.ds(k, bricks, stride=most)
        parts = [ref[pl.ds(k, ref.shape[0] // most, stride=most), :] for ref in target_refs]
        own = jnp.concatenate(parts, axis=0)
        own = jnp.where(lane < 6, own, 0.0)
        own = own + pltpu.roll(jnp.where(lane < 6, model_ref[rows, :], 0.0), 6, 1)
        if k == 0:
            own = own + pltpu.roll(jnp.where(lane < 3, sums, 0.0), 12, 1)
        total = total + (pltpu.roll(own, FIELDS * k, 1) if k else own)
    out_ref[...] = total


def finish_kernel(most, voxel_total, place_ref, back_ref, out_ref):
    frags = out_ref.shape[1]
    bricks = back_ref.shape[0]
    row, rank = place_ref[0:1, :], place_ref[1:2, :]
    place = jnp.where(lax.broadcasted_iota(I32, (bricks, frags), 0) == row, 1.0, 0.0).astype(F32)
    back = back_ref[...]
    sums = jnp.sum(back, axis=0, keepdims=True)
    cross, model_sq, target_sq = sums[:, 12:13], sums[:, 13:14], sums[:, 14:15]
    norm_model = jnp.sqrt(model_sq + EPSILON)
    norm_target = jnp.sqrt(target_sq + EPSILON)
    corr = cross / (norm_model * norm_target)
    scale_target = voxel_total / (norm_model * norm_target)
    scale_model = voxel_total * corr / (norm_model * norm_model)
    found = lax.dot_general(
        back, place, (((0,), (0,)), ((), ())), precision=HIGHEST, preferred_element_type=F32
    )
    mine = jnp.zeros((FIELDS, frags), F32)
    for k in range(most):
        mine = jnp.where(rank == k, found[FIELDS * k : FIELDS * (k + 1)], mine)
    out_ref[...] = scale_target * mine[0:6] - scale_model * mine[6:12]


def cost(macs, nbytes):
    return pl.CostEstimate(flops=2 * macs, bytes_accessed=nbytes, transcendentals=0)


def call(
    kernel, out_shape, *args, scratch=(), name=None, macs=0, in_specs=None, vmem=VMEM_BYTES
):
    kwargs = {} if in_specs is None else {"in_specs": in_specs}
    return pl.pallas_call(
        kernel,
        out_shape=out_shape,
        scratch_shapes=list(scratch),
        compiler_params=pltpu.CompilerParams(vmem_limit_bytes=vmem),
        cost_estimate=cost(macs, 4 * sum(a.size for a in args)),
        name=name,
        **kwargs,
    )(*args)


def call_at(kernel, out_shape, index, table, *args, name=None, macs=0):
    def whole(shape):
        return pl.BlockSpec(shape, lambda i, s: (0,) * len(shape))

    single = not isinstance(out_shape, list)
    outs = [out_shape] if single else out_shape
    specs = [whole(o.shape) for o in outs]
    return pl.pallas_call(
        kernel,
        out_shape=out_shape,
        grid_spec=pltpu.PrefetchScalarGridSpec(
            num_scalar_prefetch=1,
            grid=(1,),
            in_specs=[pl.BlockSpec((1,) + table.shape[1:], lambda i, s: (s[0], 0, 0))]
            + [whole(a.shape) for a in args],
            out_specs=specs[0] if single else specs,
        ),
        compiler_params=pltpu.CompilerParams(vmem_limit_bytes=VMEM_BYTES),
        cost_estimate=cost(macs, 4 * sum(a.size for a in args)),
        name=name,
    )(index, table, *args)


def looked_up(values, position):
    found = jnp.full((), int(values[0]), I32)
    for i in range(1, len(values)):
        step = int(values[i]) - int(values[i - 1])
        if step:
            found = found + step * (position >= i).astype(I32)
    return found


def shifted(value, axis, step):
    size = lax.axis_size(axis)
    pairs = [(i, i + step) for i in range(size) if 0 <= i + step < size]
    return lax.ppermute(value, axis, pairs)


def relay_blocks(value, reach):
    size = lax.axis_size("relay")
    if size == 2:
        return [value, lax.ppermute(value, "relay", [(0, 1), (1, 0)])]
    blocks = [value]
    for step in range(1, min(reach, size - 1) + 1):
        blocks += [shifted(value, "relay", step), shifted(value, "relay", -step)]
    return blocks


def relay_order(size, reach):
    if size == 2:
        return lambda r: [r, 1 - r]
    steps = [0]
    for step in range(1, min(reach, size - 1) + 1):
        steps += [-step, step]
    return lambda r: [r + s for s in steps]


def relay_total(value):
    size = lax.axis_size("relay")
    values, moving = [value], value
    for _ in range(size - 1):
        moving = lax.ppermute(moving, "relay", [(i, (i + 1) % size) for i in range(size)])
        values.append(moving)
    return jnp.concatenate(values, axis=0)


def shards(target, frag_brick, bead_cell, bead_weight, bead_arm, frag_angle):
    brick_count, relay_count = lax.axis_size("brick"), lax.axis_size("relay")
    frags, beads = bead_cell.shape
    planes, columns, rows = target.shape
    lines = planes * columns
    his = lines * (rows // LO)
    assert rows % LO == 0 and his <= 256 and columns >= 2 * KR
    assert beads == 128 and lines & (lines - 1) == 0
    voxel_total = float(brick_count * columns * relay_count * planes * rows)
    most = max(2, 2 * frags // brick_count)
    slots = brick_count * most
    assert most * FIELDS <= 128

    z_total, x_total = relay_count * planes, brick_count * columns
    gz, dz = axis_matrix(z_total, False), axis_matrix(z_total, True)
    gx, dx = axis_matrix(x_total, False), axis_matrix(x_total, True)
    reach_one, reach_two = -(-KR // planes), -(-2 * KR // planes)
    target_table, tz, tx, tn = weight_table(
        [gz, gz, dz], [dx, gx, gx], planes, relay_count, relay_order(relay_count, reach_one),
        columns, brick_count,
        [np.arange(columns), np.arange(-KR, 0), np.arange(columns, columns + KR)],
    )
    model_table, mz, mx, mn = weight_table(
        [gz @ gz, gz @ gz, dz @ gz, gz], [dx @ gx, gx @ gx, gx @ gx, gx],
        planes, relay_count, relay_order(relay_count, reach_two), columns, brick_count,
        [np.arange(columns), np.arange(-columns, 0), np.arange(columns, 2 * columns)],
    )
    r, b = lax.axis_index("relay"), lax.axis_index("brick")
    target_index = (looked_up(tz, r) * tn + looked_up(tx, b)).reshape(1)
    model_index = (looked_up(mz, r) * mn + looked_up(mx, b)).reshape(1)

    target_lines = target.reshape(lines, rows)
    words = jax.ShapeDtypeStruct((lines // 2, rows + SCALE_LANES), I32)
    hbm = pl.BlockSpec(memory_space=pltpu.HBM)
    packed = [frag_brick.reshape(1, frags), frag_angle, bead_cell, bead_weight, bead_arm]
    packed += [target_lines]
    sent, place, target_code = call(
        functools.partial(pack_kernel, most, lines, rows),
        [
            jax.ShapeDtypeStruct((slots, 3 * beads), I32),
            jax.ShapeDtypeStruct((8, frags), I32),
            words,
        ],
        *packed,
        in_specs=[hbm] * len(packed),
        scratch=[pltpu.VMEM(a.shape, a.dtype) for a in packed]
        + [pltpu.SemaphoreType.DMA((len(packed),))],
        name="pack",
        vmem=PACK_VMEM_BYTES,
    )
    target_blocks = relay_blocks(target_code, reach_one)
    by_column = [t.reshape(-1, columns, rows + SCALE_LANES) for t in target_blocks]
    left_edge = jnp.concatenate([t[:, columns - KR :] for t in by_column], axis=0)
    right_edge = jnp.concatenate([t[:, :KR] for t in by_column], axis=0)
    from_left = shifted(left_edge.reshape(-1, rows + SCALE_LANES), "brick", 1)
    from_right = shifted(right_edge.reshape(-1, rows + SCALE_LANES), "brick", -1)

    got = lax.all_to_all(sent, "brick", split_axis=0, concat_axis=0, tiled=True)
    smooth, coded = call(
        functools.partial(splat_kernel, lines, min(64, slots)),
        [jax.ShapeDtypeStruct((lines, rows), F32), words],
        got,
        scratch=[pltpu.VMEM((his, LO), F32)],
        name="splat",
        macs=slots * beads * his * LO,
    )
    coded, from_left, from_right = lax.optimization_barrier((coded, from_left, from_right))
    target_parts = [target_lines] + target_blocks[1:] + [from_left, from_right]
    blocks = relay_blocks(coded, reach_two)
    field_shapes = [
        jax.ShapeDtypeStruct((3 * his, 2 * LO), BF16),
        jax.ShapeDtypeStruct((3 * lines, rows), F32),
    ]
    target_field = call_at(
        functools.partial(target_kernel, lines),
        field_shapes,
        target_index, jnp.asarray(target_table), *target_parts,
        name="target_fields",
        macs=9 * lines * rows * 128,
    )

    def sample(field, start, count, name):
        rb = min(32, count)
        return call(
            functools.partial(sample_kernel, lines, his, rb, rb * 5 // 16, start),
            jax.ShapeDtypeStruct((count, 128), F32),
            got, *field,
            scratch=[pltpu.VMEM((3, count, beads), F32)],
            name=name,
            macs=6 * count * beads * his * LO,
        )

    part = slots // 4
    target_first = sample(target_field, 0, part, "target_sample_a")
    blocks, target_first, target_field = lax.optimization_barrier(
        (blocks, target_first, target_field)
    )
    beside = jnp.concatenate(blocks, axis=0)
    model_parts = [smooth] + blocks[1:]
    model_parts += [shifted(beside, "brick", 1), shifted(beside, "brick", -1)]
    target_second = sample(target_field, part, slots - part, "target_sample_b")
    target_second, *model_parts = lax.optimization_barrier((target_second, *model_parts))
    *model_field, partial = call_at(
        functools.partial(model_kernel, lines),
        field_shapes + [jax.ShapeDtypeStruct((8, 128), F32)],
        model_index, jnp.asarray(model_table), target_lines, *model_parts,
        name="model_fields",
    )
    partials = relay_total(partial)
    model_sums = sample(model_field, 0, slots, "model_sample")
    leaving = call(
        functools.partial(join_kernel, most),
        jax.ShapeDtypeStruct((brick_count, 128), F32),
        target_first, target_second, model_sums, partials,
        name="join",
    )
    back = lax.all_to_all(leaving, "brick", split_axis=0, concat_axis=0, tiled=True)
    return call(
        functools.partial(finish_kernel, most, voxel_total),
        jax.ShapeDtypeStruct((6, frags), F32),
        place, back,
        name="finish",
    )


def solution(mesh):
    placed = (
        P("relay", "brick", None),
        P(("brick", "relay"), None),
        P(("brick", "relay"), None),
        P(("brick", "relay"), None),
        P(None, ("brick", "relay"), None),
        P(None, ("brick", "relay")),
    )
    return jax.shard_map(
        shards, mesh=mesh, in_specs=placed, out_specs=P(None, ("brick", "relay")), check_vma=False
    )
```

```python
import functools

import jax
import jax.numpy as jnp
import numpy as np
from jax import lax
from jax.experimental import pallas as pl
from jax.experimental.pallas import tpu as pltpu
from jax.sharding import PartitionSpec as P

KR = 4
SIGMA = 1.5
EPSILON = 1e-06
HIGHEST = lax.Precision.HIGHEST
LO = 256
FIELDS = 16
WEIGHT_SCALE = 512.0
LEVER_SCALE = 32768.0
LEVER_BIAS = 1 << 20
CODE_TOP = 65535
SCALE_UNIT = 512.0
SCALE_LANES = 128
VMEM_BYTES = 48 << 20
PACK_VMEM_BYTES = 60 << 20
F32 = jnp.float32
BF16 = jnp.bfloat16
I32 = jnp.int32


def taps_of(derivative):
    offsets = np.arange(-KR, KR + 1) * 1.0
    gaussian = np.exp(-(offsets**2) / (2.0 * SIGMA**2))
    gaussian = gaussian / gaussian.sum()
    if derivative:
        return -offsets / SIGMA**2 * gaussian
    return gaussian


def axis_matrix(length, derivative):
    offsets = np.arange(length)[:, None] - np.arange(length)[None, :]
    return np.where(
        np.abs(offsets) <= KR, taps_of(derivative)[np.clip(offsets + KR, 0, 2 * KR)], 0.0
    )


def columns_at(matrix, rows, wanted):
    inside = (wanted >= 0) & (wanted < matrix.shape[1])
    picked = matrix[rows][:, np.clip(wanted, 0, matrix.shape[1] - 1)]
    return np.where(inside[None, :], picked, 0.0)


def unique_tables(tables):
    flat = np.stack([t.reshape(-1) for t in tables])
    kept, inverse = np.unique(np.round(flat, 14), axis=0, return_inverse=True)
    return kept.reshape((-1,) + tables[0].shape), inverse.reshape(-1).astype(np.int32)


def pieces_np(table):
    import ml_dtypes

    high = table.astype(np.float32).astype(ml_dtypes.bfloat16)
    low = (table - high.astype(np.float64)).astype(ml_dtypes.bfloat16)
    return np.concatenate([high, high, low], axis=-1)


def weight_table(z_kinds, x_kinds, z_len, z_count, z_blocks, x_len, x_count, x_parts):
    z_tables = []
    for r in range(z_count):
        wanted = np.concatenate([np.arange(z_len) + z_len * block for block in z_blocks(r)])
        rows = np.arange(z_len) + z_len * r
        z_tables.append(np.stack([columns_at(m, rows, wanted) for m in z_kinds]))
    x_tables = []
    for b in range(x_count):
        wanted = np.concatenate([x_len * b + part for part in x_parts(b)])
        rows = np.arange(x_len) + x_len * b
        x_tables.append(np.stack([columns_at(m, rows, wanted) for m in x_kinds]))
    z_tables, z_inverse = unique_tables(z_tables)
    x_tables, x_inverse = unique_tables(x_tables)
    kinds = len(z_kinds)
    parts, start = [], 0
    for part in x_parts(0):
        piece = x_tables[:, :, :, start : start + len(part)]
        start += len(part)
        full = np.einsum("rkzi,bkxj->rbkzxij", z_tables, piece)
        parts.append(
            full.reshape(len(z_tables) * len(x_tables), kinds * z_len * x_len, -1)
        )
    table = pieces_np(np.concatenate(parts, axis=-1))
    return table, z_inverse, x_inverse, len(x_tables)


def eye_column(row, eye):
    return jnp.sum(jnp.where(eye, row, jnp.zeros_like(row)), axis=1, keepdims=True)


def slot_row(row, most):
    frags = row.shape[1]
    sub = lax.broadcasted_iota(I32, (frags, frags), 0)
    lane = lax.broadcasted_iota(I32, (frags, frags), 1)
    eye = sub == lane
    earlier = jnp.logical_and(eye_column(row, eye) == row, sub < lane)
    return jnp.sum(jnp.where(earlier, 1, 0), axis=0, keepdims=True), eye


def pack_kernel(most, lines, row_count, *refs):
    inputs, (out_ref, place_ref), held, sems = refs[:5], refs[5:7], refs[7:12], refs[12]
    copies = [
        pltpu.make_async_copy(source, target, sems.at[k])
        for k, (source, target) in enumerate(zip(inputs, held))
    ]
    for copy in copies:
        copy.start()
    brick_ref, angle_ref, cell_ref, weight_ref, arm_ref = held
    for copy in copies[:2]:
        copy.wait()
    frags, beads = cell_ref.shape
    slots = out_ref.shape[0]
    row = brick_ref[...]
    rank, eye = slot_row(row, most)
    slot = row * most + rank
    place = jnp.where(lax.broadcasted_iota(I32, (slots, frags), 0) == slot, 1.0, 0.0).astype(F32)

    angles = angle_ref[...]
    cos, sin = jnp.cos(angles), jnp.sin(angles)
    cos_a, cos_b, cos_c = cos[0:1], cos[1:2], cos[2:3]
    sin_a, sin_b, sin_c = sin[0:1], sin[1:2], sin[2:3]
    turn = [
        [cos_a * cos_b, cos_a * sin_b * sin_c - sin_a * cos_c, cos_a * sin_b * cos_c + sin_a * sin_c],
        [sin_a * cos_b, sin_a * sin_b * sin_c + cos_a * cos_c, sin_a * sin_b * cos_c - cos_a * sin_c],
        [-sin_b, cos_b * sin_c, cos_b * cos_c],
    ]
    turn = [[eye_column(value, eye) for value in values] for values in turn]
    place_ref[0:1, :] = row
    place_ref[1:2, :] = rank
    for copy in copies[2:]:
        copy.wait()
    levers = []
    for i in range(3):
        total = turn[i][0] * arm_ref[0]
        for j in (1, 2):
            total = total + turn[i][j] * arm_ref[j]
        levers.append(jnp.round(total * LEVER_SCALE))

    cell = cell_ref[...]
    line = ((cell.astype(F32) + 0.5) * (1.0 / row_count)).astype(I32)
    y = cell - line * row_count
    code = (((y // LO) * lines + line) * LO + (y % LO)).astype(F32)
    weight = weight_ref[...].astype(F32) * WEIGHT_SCALE
    payload = jnp.concatenate([code, weight] + levers, axis=1)
    placed = jnp.dot(place, payload, precision=HIGHEST, preferred_element_type=F32)
    placed = placed.astype(I32)
    code, weight, lx, ly, lz = [placed[:, k * beads : (k + 1) * beads] for k in range(5)]
    lz = lz + LEVER_BIAS
    out_ref[:, 0:beads] = code | (weight << 16)
    out_ref[:, beads : 2 * beads] = (lx << 11) | (lz >> 10)
    out_ref[:, 2 * beads : 3 * beads] = (ly << 11) | (lz & 1023)


def line_blur(value, derivative):
    taps = taps_of(derivative)
    rows, length = value.shape
    wide = jnp.concatenate([value, jnp.zeros((rows, 128), F32)], axis=1)
    total = None if derivative else float(taps[KR]) * value
    for d in range(1, KR + 1):
        up = pltpu.roll(wide, d, 1)[:, :length]
        down = pltpu.roll(wide, length + 128 - d, 1)[:, :length]
        pair = up - down if derivative else up + down
        term = float(taps[KR + d]) * pair
        total = term if total is None else total + term
    return total


def encode(value, out_ref):
    half, length = value.shape[0] // 2, value.shape[1]
    top = (jnp.max(value) * SCALE_UNIT).astype(I32) + 1
    scale = (SCALE_UNIT * CODE_TOP) / top.astype(F32)
    code = jnp.minimum((value * scale + 0.5).astype(I32), CODE_TOP)
    out_ref[:, :length] = code[:half] | (code[half:] << 16)
    out_ref[:, length:] = jnp.full((half, SCALE_LANES), top, I32)


def decode(words, count):
    half, length = words.shape[0] // count, words.shape[1] - SCALE_LANES
    step = words[:, length : length + 1].astype(F32) * (1.0 / (SCALE_UNIT * CODE_TOP))
    low = (words[:, :length] & CODE_TOP).astype(F32) * step
    high = ((words[:, :length] >> 16) & CODE_TOP).astype(F32) * step
    lines = []
    for k in range(count):
        rows = slice(k * half, (k + 1) * half)
        lines += [low[rows], high[rows]]
    return lines


def encode_kernel(value_ref, out_ref):
    encode(value_ref[...], out_ref)


def splat_kernel(lines, rb, got_ref, out_ref, code_ref, acc_ref):
    slots = got_ref.shape[0]
    beads = got_ref.shape[1] // 3
    his = acc_ref.shape[0]
    acc_ref[...] = jnp.zeros_like(acc_ref)
    hi_iota = lax.broadcasted_iota(I32, (his, beads), 0)
    lo_iota = lax.broadcasted_iota(I32, (LO, beads), 0)

    def body(i, carry):
        word = got_ref[pl.ds(i * rb, rb), 0:beads]
        lo = word & (LO - 1)
        hi = (word >> 8) & 255
        weight = (word >> 16).astype(F32) * (1.0 / WEIGHT_SCALE)
        left, right = [], []
        for q in range(rb):
            left.append(jnp.where(hi_iota == hi[q : q + 1], weight[q : q + 1], 0.0).astype(BF16))
            right.append(jnp.where(lo_iota == lo[q : q + 1], 1.0, 0.0).astype(BF16))
        acc_ref[...] += lax.dot_general(
            jnp.concatenate(left, axis=1),
            jnp.concatenate(right, axis=1),
            (((1,), (1,)), ((), ())),
            preferred_element_type=F32,
        )
        return carry

    lax.fori_loop(0, slots // rb, body, 0)
    density = [acc_ref[yh * lines : (yh + 1) * lines, :] for yh in range(his // lines)]
    smooth = line_blur(jnp.concatenate(density, axis=1), False)
    out_ref[...] = smooth
    encode(smooth, code_ref)


def split(value):
    high = value.astype(BF16)
    low = (value - high.astype(F32)).astype(BF16)
    return high, low


def mix_lines(index_ref, tables_ref, table_ref, sem, lines_of):
    copy = pltpu.make_async_copy(tables_ref.at[index_ref[0]], table_ref, sem)
    copy.start()
    value = jnp.concatenate(lines_of(), axis=0)
    high, low = split(value)
    copy.wait()
    return jnp.dot(
        table_ref[...], jnp.concatenate([high, low, high], axis=0), preferred_element_type=F32
    )


def store_fields(fields, lines, out_ref, exact_ref):
    his = fields[0].shape[1] // LO * lines
    for k, field in enumerate(fields):
        exact_ref[k * lines : (k + 1) * lines, :] = field
        for yh in range(field.shape[1] // LO):
            high, low = split(field[:, yh * LO : (yh + 1) * LO])
            rows = slice(k * his + yh * lines, k * his + (yh + 1) * lines)
            out_ref[rows, 0:LO] = high
            out_ref[rows, LO : 2 * LO] = low


def window_lines(own_ref, near_refs, first_ref, second_ref):
    lines = [own_ref[...]]
    for ref in near_refs:
        lines += decode(ref[...], 1)
    for ref in (first_ref, second_ref):
        lines += decode(ref[...], len(near_refs) + 1)
    return lines


def target_kernel(lines, index_ref, tables_ref, own_ref, *refs):
    *near_refs, first_ref, second_ref, out_ref, exact_ref, table_ref, sem = refs
    window = functools.partial(window_lines, own_ref, near_refs, first_ref, second_ref)
    mixed = mix_lines(index_ref, tables_ref, table_ref, sem, window)
    grad_x = line_blur(mixed[0:lines], False)
    grad_y = line_blur(mixed[lines : 2 * lines], True)
    grad_z = line_blur(mixed[2 * lines : 3 * lines], False)
    store_fields([grad_x, grad_y, grad_z], lines, out_ref, exact_ref)


def model_kernel(lines, index_ref, tables_ref, target_ref, own_ref, *refs):
    *near_refs, first_ref, second_ref, out_ref, exact_ref, sum_ref, table_ref, sem = refs
    window = functools.partial(window_lines, own_ref, near_refs, first_ref, second_ref)
    smooth = mix_lines(index_ref, tables_ref, table_ref, sem, window)
    model = smooth[3 * lines :]
    target = target_ref[...]
    sums = [jnp.sum(model * target), jnp.sum(model * model), jnp.sum(target * target)]
    lane = lax.broadcasted_iota(I32, sum_ref.shape, 1)
    total = jnp.zeros(sum_ref.shape, F32)
    for k, value in enumerate(sums):
        total = jnp.where(lane == k, value, total)
    sum_ref[...] = total
    grad_x = line_blur(smooth[0:lines], False)
    grad_y = line_blur(smooth[lines : 2 * lines], True)
    grad_z = line_blur(smooth[2 * lines : 3 * lines], False)
    store_fields([grad_x, grad_y, grad_z], lines, out_ref, exact_ref)


def sample_by_matmul(word, field_ref, his, store):
    count, beads = word.shape
    lo, hi = word & (LO - 1), (word >> 8) & 255
    lo_iota = lax.broadcasted_iota(I32, (LO, beads), 0)
    picks = [jnp.where(lo_iota == lo[q : q + 1], 1.0, 0.0).astype(BF16) for q in range(count)]
    pick = jnp.concatenate(picks, axis=1)
    sampled = jnp.dot(
        field_ref[...], jnp.concatenate([pick, pick], axis=0), preferred_element_type=F32
    )

    def finish():
        sub_iota = lax.broadcasted_iota(I32, (8, beads), 0)
        for q in range(count):
            own = jnp.broadcast_to(hi[q : q + 1], (8, beads))
            group, within = own >> 3, (own & 7) == sub_iota
            found = [jnp.zeros((8, beads), F32)] * 3
            for j in range(his // 8):
                here = group == j
                for k in range(3):
                    rows = slice(k * his + 8 * j, k * his + 8 * j + 8)
                    part = sampled[rows, q * beads : (q + 1) * beads]
                    found[k] = jnp.where(here, part, found[k])
            store(q, [jnp.sum(jnp.where(within, v, 0.0), axis=0, keepdims=True) for v in found])

    return finish


def sample_by_lanes(word, exact_ref, lines, store):
    count, beads = word.shape
    tiles = exact_ref.shape[1] // 128
    line_shift, lo_shift = lines.bit_length() - 1, LO.bit_length() - 1
    sub_iota = lax.broadcasted_iota(I32, (8, beads), 0)
    for q in range(count):
        own = jnp.broadcast_to(word[q : q + 1], (8, beads))
        lo, hi = own & (LO - 1), (own >> lo_shift) & 255
        line = hi & (lines - 1)
        group = (line >> 3) * tiles + (hi >> line_shift) * (LO // 128) + (lo >> 7)
        within, lane = (line & 7) == sub_iota, lo & 127
        found = [jnp.zeros((8, beads), F32)] * 3
        for j in range(lines // 8 * tiles):
            here = group == j
            first, tile = j // tiles * 8, j % tiles * 128
            for k in range(3):
                table = exact_ref[k * lines + first : k * lines + first + 8, tile : tile + 128]
                part = jnp.take_along_axis(table, lane, axis=1, mode="promise_in_bounds")
                found[k] = jnp.where(here, part, found[k])
        store(q, [jnp.sum(jnp.where(within, v, 0.0), axis=0, keepdims=True) for v in found])


def sample_kernel(
    lines, his, rb, by_lanes, start, got_ref, field_ref, exact_ref, out_ref, force_ref
):
    slots = out_ref.shape[0]
    beads = got_ref.shape[1] // 3
    by_matmul = rb - by_lanes

    def body(i, carry):
        def store_from(first):
            def store(q, values):
                for k in range(3):
                    force_ref[k, pl.ds(i * rb + first + q, 1), :] = values[k]

            return store

        word = got_ref[pl.ds(start + i * rb, rb), 0:beads]
        finish = sample_by_matmul(word[:by_matmul], field_ref, his, store_from(0))
        sample_by_lanes(word[by_matmul:], exact_ref, lines, store_from(by_matmul))
        finish()
        return carry

    lax.fori_loop(0, slots // rb, body, 0)
    rows = slice(start, start + slots)
    first, second = got_ref[rows, beads : 2 * beads], got_ref[rows, 2 * beads : 3 * beads]
    weight = (got_ref[rows, 0:beads] >> 16).astype(F32) * (1.0 / WEIGHT_SCALE)
    lever_z = (((first & 2047) << 10) | (second & 1023)) - LEVER_BIAS
    levers = [
        v.astype(F32) * (1.0 / LEVER_SCALE) for v in (first >> 11, second >> 11, lever_z)
    ]
    force = [force_ref[k] * weight for k in range(3)]
    terms = force + [
        levers[1] * force[2] - levers[2] * force[1],
        levers[2] * force[0] - levers[0] * force[2],
        levers[0] * force[1] - levers[1] * force[0],
    ]
    lane = lax.broadcasted_iota(I32, out_ref.shape, 1)
    total = jnp.zeros(out_ref.shape, F32)
    for k, term in enumerate(terms):
        total = jnp.where(lane == k, jnp.sum(term, axis=1, keepdims=True), total)
    out_ref[...] = total


def join_kernel(most, first_ref, second_ref, model_ref, sum_ref, out_ref):
    bricks = out_ref.shape[0]
    lane = lax.broadcasted_iota(I32, out_ref.shape, 1)
    sums = sum_ref[0:1, :]
    for k in range(1, sum_ref.shape[0] // 8):
        sums = sums + sum_ref[8 * k : 8 * k + 1, :]
    total = jnp.zeros(out_ref.shape, F32)
    for k in range(most):
        rows, half = pl.ds(k, bricks, stride=most), pl.ds(k, bricks // 2, stride=most)
        own = jnp.concatenate([first_ref[half, :], second_ref[half, :]], axis=0)
        own = jnp.where(lane < 6, own, 0.0)
        own = own + pltpu.roll(jnp.where(lane < 6, model_ref[rows, :], 0.0), 6, 1)
        if k == 0:
            own = own + pltpu.roll(jnp.where(lane < 3, sums, 0.0), 12, 1)
        total = total + (pltpu.roll(own, FIELDS * k, 1) if k else own)
    out_ref[...] = total


def finish_kernel(most, voxel_total, place_ref, back_ref, out_ref):
    frags = out_ref.shape[1]
    bricks = back_ref.shape[0]
    row, rank = place_ref[0:1, :], place_ref[1:2, :]
    place = jnp.where(lax.broadcasted_iota(I32, (bricks, frags), 0) == row, 1.0, 0.0).astype(F32)
    back = back_ref[...]
    sums = jnp.sum(back, axis=0, keepdims=True)
    cross, model_sq, target_sq = sums[:, 12:13], sums[:, 13:14], sums[:, 14:15]
    norm_model = jnp.sqrt(model_sq + EPSILON)
    norm_target = jnp.sqrt(target_sq + EPSILON)
    corr = cross / (norm_model * norm_target)
    scale_target = voxel_total / (norm_model * norm_target)
    scale_model = voxel_total * corr / (norm_model * norm_model)
    found = lax.dot_general(
        back, place, (((0,), (0,)), ((), ())), precision=HIGHEST, preferred_element_type=F32
    )
    mine = jnp.zeros((FIELDS, frags), F32)
    for k in range(most):
        mine = jnp.where(rank == k, found[FIELDS * k : FIELDS * (k + 1)], mine)
    out_ref[...] = scale_target * mine[0:6] - scale_model * mine[6:12]


def cost(macs, nbytes):
    return pl.CostEstimate(flops=2 * macs, bytes_accessed=nbytes, transcendentals=0)


def call(
    kernel, out_shape, *args, scratch=(), name=None, macs=0, in_specs=None, vmem=VMEM_BYTES
):
    kwargs = {} if in_specs is None else {"in_specs": in_specs}
    return pl.pallas_call(
        kernel,
        out_shape=out_shape,
        scratch_shapes=list(scratch),
        compiler_params=pltpu.CompilerParams(vmem_limit_bytes=vmem),
        cost_estimate=cost(macs, 4 * sum(a.size for a in args)),
        name=name,
        **kwargs,
    )(*args)


def call_at(kernel, out_shape, index, table, *args, name=None, macs=0):
    vmem = pl.BlockSpec(memory_space=pltpu.VMEM)
    return call(
        kernel,
        out_shape,
        index, table, *args,
        in_specs=[pl.BlockSpec(memory_space=pltpu.SMEM), pl.BlockSpec(memory_space=pl.ANY)]
        + [vmem] * len(args),
        scratch=[pltpu.VMEM(table.shape[1:], table.dtype), pltpu.SemaphoreType.DMA],
        name=name,
        macs=macs,
    )


def looked_up(values, position):
    found = jnp.full((), int(values[0]), I32)
    for i in range(1, len(values)):
        step = int(values[i]) - int(values[i - 1])
        if step:
            found = found + step * (position >= i).astype(I32)
    return found


def shifted(value, axis, step):
    size = lax.axis_size(axis)
    pairs = [(i, i + step) for i in range(size) if 0 <= i + step < size]
    return lax.ppermute(value, axis, pairs)


def paired(own, left, right):
    return lambda b: [own, right, left] if b % 2 == 0 else [own, left, right]


def swapped(first, second):
    size = lax.axis_size("brick")
    found = []
    for value, start in ((first, 0), (second, 1)):
        pairs = [(i, i + 1) for i in range(start, size - 1, 2)]
        found.append(lax.ppermute(value, "brick", pairs + [(j, i) for i, j in pairs]))
    return found


def relay_blocks(value, reach):
    size = lax.axis_size("relay")
    if size == 2:
        return [value, lax.ppermute(value, "relay", [(0, 1), (1, 0)])]
    blocks = [value]
    for step in range(1, min(reach, size - 1) + 1):
        blocks += [shifted(value, "relay", step), shifted(value, "relay", -step)]
    return blocks


def relay_order(size, reach):
    if size == 2:
        return lambda r: [r, 1 - r]
    steps = [0]
    for step in range(1, min(reach, size - 1) + 1):
        steps += [-step, step]
    return lambda r: [r + s for s in steps]


def relay_total(value):
    size = lax.axis_size("relay")
    values, moving = [value], value
    for _ in range(size - 1):
        moving = lax.ppermute(moving, "relay", [(i, (i + 1) % size) for i in range(size)])
        values.append(moving)
    return jnp.concatenate(values, axis=0)


def shards(target, frag_brick, bead_cell, bead_weight, bead_arm, frag_angle):
    brick_count, relay_count = lax.axis_size("brick"), lax.axis_size("relay")
    frags, beads = bead_cell.shape
    planes, columns, rows = target.shape
    lines = planes * columns
    his = lines * (rows // LO)
    assert rows % LO == 0 and his <= 256 and columns >= 2 * KR
    assert beads == 128 and lines & (lines - 1) == 0
    voxel_total = float(brick_count * columns * relay_count * planes * rows)
    most = max(2, 2 * frags // brick_count)
    slots = brick_count * most
    assert most * FIELDS <= 128

    z_total, x_total = relay_count * planes, brick_count * columns
    gz, dz = axis_matrix(z_total, False), axis_matrix(z_total, True)
    gx, dx = axis_matrix(x_total, False), axis_matrix(x_total, True)
    reach_one, reach_two = -(-KR // planes), -(-2 * KR // planes)
    target_table, tz, tx, tn = weight_table(
        [gz, gz, dz], [dx, gx, gx], planes, relay_count, relay_order(relay_count, reach_one),
        columns, brick_count,
        paired(np.arange(columns), np.arange(-KR, 0), np.arange(columns, columns + KR)),
    )
    model_table, mz, mx, mn = weight_table(
        [gz @ gz, gz @ gz, dz @ gz, gz], [dx @ gx, gx @ gx, gx @ gx, gx],
        planes, relay_count, relay_order(relay_count, reach_two), columns, brick_count,
        paired(np.arange(columns), np.arange(-columns, 0), np.arange(columns, 2 * columns)),
    )
    r, b = lax.axis_index("relay"), lax.axis_index("brick")
    target_index = (looked_up(tz, r) * tn + looked_up(tx, b)).reshape(1)
    model_index = (looked_up(mz, r) * mn + looked_up(mx, b)).reshape(1)

    target_lines = target.reshape(lines, rows)
    words = jax.ShapeDtypeStruct((lines // 2, rows + SCALE_LANES), I32)
    target_blocks = relay_blocks(call(encode_kernel, words, target_lines, name="encode"), reach_one)
    by_column = [t.reshape(-1, columns, rows + SCALE_LANES) for t in target_blocks]
    left_edge = jnp.concatenate([t[:, columns - KR :] for t in by_column], axis=0)
    right_edge = jnp.concatenate([t[:, :KR] for t in by_column], axis=0)
    first_edge = jnp.where(b % 2 == 0, left_edge, right_edge)
    second_edge = jnp.where(b % 2 == 0, right_edge, left_edge)
    target_near = swapped(
        first_edge.reshape(-1, rows + SCALE_LANES), second_edge.reshape(-1, rows + SCALE_LANES)
    )

    hbm = pl.BlockSpec(memory_space=pltpu.HBM)
    packed = [frag_brick.reshape(1, frags), frag_angle, bead_cell, bead_weight, bead_arm]
    sent, place = call(
        functools.partial(pack_kernel, most, lines, rows),
        [
            jax.ShapeDtypeStruct((slots, 3 * beads), I32),
            jax.ShapeDtypeStruct((8, frags), I32),
        ],
        *packed,
        in_specs=[hbm] * len(packed),
        scratch=[pltpu.VMEM(a.shape, a.dtype) for a in packed]
        + [pltpu.SemaphoreType.DMA((len(packed),))],
        name="pack",
        vmem=PACK_VMEM_BYTES,
    )
    got = lax.all_to_all(sent, "brick", split_axis=0, concat_axis=0, tiled=True)
    smooth, coded = call(
        functools.partial(splat_kernel, lines, min(64, slots)),
        [jax.ShapeDtypeStruct((lines, rows), F32), words],
        got,
        scratch=[pltpu.VMEM((his, LO), F32)],
        name="splat",
        macs=slots * beads * his * LO,
    )
    coded, *target_near = lax.optimization_barrier((coded, *target_near))
    target_parts = [target_lines] + target_blocks[1:] + target_near
    blocks = relay_blocks(coded, reach_two)
    field_shapes = [
        jax.ShapeDtypeStruct((3 * his, 2 * LO), BF16),
        jax.ShapeDtypeStruct((3 * lines, rows), F32),
    ]
    target_field = call_at(
        functools.partial(target_kernel, lines),
        field_shapes,
        target_index, jnp.asarray(target_table), *target_parts,
        name="target_fields",
        macs=9 * lines * rows * 128,
    )

    def sample(field, start, count, name):
        rb = min(32, count)
        return call(
            functools.partial(sample_kernel, lines, his, rb, rb * 5 // 16, start),
            jax.ShapeDtypeStruct((count, 128), F32),
            got, *field,
            scratch=[pltpu.VMEM((3, count, beads), F32)],
            name=name,
            macs=6 * count * beads * his * LO,
        )

    half = slots // 2
    target_first = sample(target_field, 0, half, "target_sample_a")
    blocks, target_first, target_field = lax.optimization_barrier(
        (blocks, target_first, target_field)
    )
    beside = jnp.concatenate(blocks, axis=0)
    model_parts = [smooth] + blocks[1:]
    model_parts += swapped(beside, beside)
    target_second = sample(target_field, half, slots - half, "target_sample_b")
    target_second, *model_parts = lax.optimization_barrier((target_second, *model_parts))
    *model_field, partial = call_at(
        functools.partial(model_kernel, lines),
        field_shapes + [jax.ShapeDtypeStruct((8, 128), F32)],
        model_index, jnp.asarray(model_table), target_lines, *model_parts,
        name="model_fields",
    )
    partials = relay_total(partial)
    model_sums = sample(model_field, 0, slots, "model_sample")
    leaving = call(
        functools.partial(join_kernel, most),
        jax.ShapeDtypeStruct((brick_count, 128), F32),
        target_first, target_second, model_sums, partials,
        name="join",
    )
    back = lax.all_to_all(leaving, "brick", split_axis=0, concat_axis=0, tiled=True)
    return call(
        functools.partial(finish_kernel, most, voxel_total),
        jax.ShapeDtypeStruct((6, frags), F32),
        place, back,
        name="finish",
    )


def solution(mesh):
    placed = (
        P("relay", "brick", None),
        P(("brick", "relay"), None),
        P(("brick", "relay"), None),
        P(("brick", "relay"), None),
        P(None, ("brick", "relay"), None),
        P(None, ("brick", "relay")),
    )
    return jax.shard_map(
        shards, mesh=mesh, in_specs=placed, out_specs=P(None, ("brick", "relay")), check_vma=False
    )
```

```python
import functools

import jax
import jax.numpy as jnp
import numpy as np
from jax import lax
from jax.experimental import pallas as pl
from jax.experimental.pallas import tpu as pltpu
from jax.sharding import PartitionSpec as P

KR = 4
SIGMA = 1.5
EPSILON = 1e-06
HIGHEST = lax.Precision.HIGHEST
LO = 256
FIELDS = 16
WEIGHT_SCALE = 512.0
LEVER_SCALE = 32768.0
LEVER_BIAS = 1 << 20
CODE_TOP = 65535
SCALE_UNIT = 512.0
SCALE_LANES = 128
VMEM_BYTES = 48 << 20
PACK_VMEM_BYTES = 60 << 20
F32 = jnp.float32
BF16 = jnp.bfloat16
I32 = jnp.int32


def taps_of(derivative):
    offsets = np.arange(-KR, KR + 1) * 1.0
    gaussian = np.exp(-(offsets**2) / (2.0 * SIGMA**2))
    gaussian = gaussian / gaussian.sum()
    if derivative:
        return -offsets / SIGMA**2 * gaussian
    return gaussian


def axis_matrix(length, derivative):
    offsets = np.arange(length)[:, None] - np.arange(length)[None, :]
    return np.where(
        np.abs(offsets) <= KR, taps_of(derivative)[np.clip(offsets + KR, 0, 2 * KR)], 0.0
    )


def columns_at(matrix, rows, wanted):
    inside = (wanted >= 0) & (wanted < matrix.shape[1])
    picked = matrix[rows][:, np.clip(wanted, 0, matrix.shape[1] - 1)]
    return np.where(inside[None, :], picked, 0.0)


def unique_tables(tables):
    flat = np.stack([t.reshape(-1) for t in tables])
    kept, inverse = np.unique(np.round(flat, 14), axis=0, return_inverse=True)
    return kept.reshape((-1,) + tables[0].shape), inverse.reshape(-1).astype(np.int32)


def pieces_np(table):
    import ml_dtypes

    high = table.astype(np.float32).astype(ml_dtypes.bfloat16)
    low = (table - high.astype(np.float64)).astype(ml_dtypes.bfloat16)
    return np.concatenate([high, high, low], axis=-1)


def weight_table(z_kinds, x_kinds, z_len, z_count, z_blocks, x_len, x_count, x_parts):
    z_tables = []
    for r in range(z_count):
        wanted = np.concatenate([np.arange(z_len) + z_len * block for block in z_blocks(r)])
        rows = np.arange(z_len) + z_len * r
        z_tables.append(np.stack([columns_at(m, rows, wanted) for m in z_kinds]))
    x_tables = []
    for b in range(x_count):
        wanted = np.concatenate([x_len * b + part for part in x_parts(b)])
        rows = np.arange(x_len) + x_len * b
        x_tables.append(np.stack([columns_at(m, rows, wanted) for m in x_kinds]))
    z_tables, z_inverse = unique_tables(z_tables)
    x_tables, x_inverse = unique_tables(x_tables)
    kinds = len(z_kinds)
    parts, start = [], 0
    for part in x_parts(0):
        piece = x_tables[:, :, :, start : start + len(part)]
        start += len(part)
        full = np.einsum("rkzi,bkxj->rbkzxij", z_tables, piece)
        parts.append(
            full.reshape(len(z_tables) * len(x_tables), kinds * z_len * x_len, -1)
        )
    table = pieces_np(np.concatenate(parts, axis=-1))
    return table, z_inverse, x_inverse, len(x_tables)


def eye_column(row, eye):
    return jnp.sum(jnp.where(eye, row, jnp.zeros_like(row)), axis=1, keepdims=True)


def slot_row(row, most):
    frags = row.shape[1]
    sub = lax.broadcasted_iota(I32, (frags, frags), 0)
    lane = lax.broadcasted_iota(I32, (frags, frags), 1)
    eye = sub == lane
    earlier = jnp.logical_and(eye_column(row, eye) == row, sub < lane)
    return jnp.sum(jnp.where(earlier, 1, 0), axis=0, keepdims=True), eye


def pack_kernel(most, lines, row_count, *refs):
    inputs, (out_ref, place_ref, code_ref) = refs[:6], refs[6:9]
    held, sems = refs[9:15], refs[15]
    copies = [
        pltpu.make_async_copy(source, target, sems.at[k])
        for k, (source, target) in enumerate(zip(inputs, held))
    ]
    for copy in copies:
        copy.start()
    brick_ref, angle_ref, cell_ref, weight_ref, arm_ref, target_ref = held
    for copy in copies[:2]:
        copy.wait()
    frags, beads = cell_ref.shape
    slots = out_ref.shape[0]
    row = brick_ref[...]
    rank, eye = slot_row(row, most)
    slot = row * most + rank
    place = jnp.where(lax.broadcasted_iota(I32, (slots, frags), 0) == slot, 1.0, 0.0).astype(F32)

    angles = angle_ref[...]
    cos, sin = jnp.cos(angles), jnp.sin(angles)
    cos_a, cos_b, cos_c = cos[0:1], cos[1:2], cos[2:3]
    sin_a, sin_b, sin_c = sin[0:1], sin[1:2], sin[2:3]
    turn = [
        [cos_a * cos_b, cos_a * sin_b * sin_c - sin_a * cos_c, cos_a * sin_b * cos_c + sin_a * sin_c],
        [sin_a * cos_b, sin_a * sin_b * sin_c + cos_a * cos_c, sin_a * sin_b * cos_c - cos_a * sin_c],
        [-sin_b, cos_b * sin_c, cos_b * cos_c],
    ]
    turn = [[eye_column(value, eye) for value in values] for values in turn]
    place_ref[0:1, :] = row
    place_ref[1:2, :] = rank
    for copy in copies[2:]:
        copy.wait()
    encode(target_ref[...], code_ref)
    levers = []
    for i in range(3):
        total = turn[i][0] * arm_ref[0]
        for j in (1, 2):
            total = total + turn[i][j] * arm_ref[j]
        levers.append(jnp.round(total * LEVER_SCALE))

    cell = cell_ref[...]
    line = ((cell.astype(F32) + 0.5) * (1.0 / row_count)).astype(I32)
    y = cell - line * row_count
    code = (((y // LO) * lines + line) * LO + (y % LO)).astype(F32)
    weight = weight_ref[...].astype(F32) * WEIGHT_SCALE
    payload = jnp.concatenate([code, weight] + levers, axis=1)
    placed = jnp.dot(place, payload, precision=HIGHEST, preferred_element_type=F32)
    placed = placed.astype(I32)
    code, weight, lx, ly, lz = [placed[:, k * beads : (k + 1) * beads] for k in range(5)]
    lz = lz + LEVER_BIAS
    out_ref[:, 0:beads] = code | (weight << 16)
    out_ref[:, beads : 2 * beads] = (lx << 11) | (lz >> 10)
    out_ref[:, 2 * beads : 3 * beads] = (ly << 11) | (lz & 1023)


def line_blur(value, derivative):
    taps = taps_of(derivative)
    rows, length = value.shape
    wide = jnp.concatenate([value, jnp.zeros((rows, 128), F32)], axis=1)
    total = None if derivative else float(taps[KR]) * value
    for d in range(1, KR + 1):
        up = pltpu.roll(wide, d, 1)[:, :length]
        down = pltpu.roll(wide, length + 128 - d, 1)[:, :length]
        pair = up - down if derivative else up + down
        term = float(taps[KR + d]) * pair
        total = term if total is None else total + term
    return total


def encode(value, out_ref):
    half, length = value.shape[0] // 2, value.shape[1]
    top = (jnp.max(value) * SCALE_UNIT).astype(I32) + 1
    scale = (SCALE_UNIT * CODE_TOP) / top.astype(F32)
    code = jnp.minimum((value * scale + 0.5).astype(I32), CODE_TOP)
    out_ref[:, :length] = code[:half] | (code[half:] << 16)
    out_ref[:, length:] = jnp.full((half, SCALE_LANES), top, I32)


def decode(words, count):
    half, length = words.shape[0] // count, words.shape[1] - SCALE_LANES
    step = words[:, length : length + 1].astype(F32) * (1.0 / (SCALE_UNIT * CODE_TOP))
    low = (words[:, :length] & CODE_TOP).astype(F32) * step
    high = ((words[:, :length] >> 16) & CODE_TOP).astype(F32) * step
    lines = []
    for k in range(count):
        rows = slice(k * half, (k + 1) * half)
        lines += [low[rows], high[rows]]
    return lines


def splat_kernel(lines, rb, got_ref, out_ref, code_ref, acc_ref):
    slots = got_ref.shape[0]
    beads = got_ref.shape[1] // 3
    his = acc_ref.shape[0]
    acc_ref[...] = jnp.zeros_like(acc_ref)
    hi_iota = lax.broadcasted_iota(I32, (his, beads), 0)
    lo_iota = lax.broadcasted_iota(I32, (LO, beads), 0)

    def body(i, carry):
        word = got_ref[pl.ds(i * rb, rb), 0:beads]
        lo = word & (LO - 1)
        hi = (word >> 8) & 255
        weight = (word >> 16).astype(F32) * (1.0 / WEIGHT_SCALE)
        left, right = [], []
        for q in range(rb):
            left.append(jnp.where(hi_iota == hi[q : q + 1], weight[q : q + 1], 0.0).astype(BF16))
            right.append(jnp.where(lo_iota == lo[q : q + 1], 1.0, 0.0).astype(BF16))
        acc_ref[...] += lax.dot_general(
            jnp.concatenate(left, axis=1),
            jnp.concatenate(right, axis=1),
            (((1,), (1,)), ((), ())),
            preferred_element_type=F32,
        )
        return carry

    lax.fori_loop(0, slots // rb, body, 0)
    density = [acc_ref[yh * lines : (yh + 1) * lines, :] for yh in range(his // lines)]
    smooth = line_blur(jnp.concatenate(density, axis=1), False)
    out_ref[...] = smooth
    encode(smooth, code_ref)


def split(value):
    high = value.astype(BF16)
    low = (value - high.astype(F32)).astype(BF16)
    return high, low


def mix_lines(table_ref, parts):
    value = jnp.concatenate(parts, axis=0)
    high, low = split(value)
    return jnp.dot(
        table_ref[0], jnp.concatenate([high, low, high], axis=0), preferred_element_type=F32
    )


def store_fields(fields, lines, out_ref, exact_ref):
    his = fields[0].shape[1] // LO * lines
    for k, field in enumerate(fields):
        exact_ref[k * lines : (k + 1) * lines, :] = field
        for yh in range(field.shape[1] // LO):
            high, low = split(field[:, yh * LO : (yh + 1) * LO])
            rows = slice(k * his + yh * lines, k * his + (yh + 1) * lines)
            out_ref[rows, 0:LO] = high
            out_ref[rows, LO : 2 * LO] = low


def window_lines(own_ref, near_refs, first_ref, second_ref):
    lines = [own_ref[...]]
    for ref in near_refs:
        lines += decode(ref[...], 1)
    for ref in (first_ref, second_ref):
        lines += decode(ref[...], len(near_refs) + 1)
    return lines


def target_kernel(lines, _, table_ref, own_ref, *refs):
    *near_refs, first_ref, second_ref, out_ref, exact_ref = refs
    mixed = mix_lines(table_ref, window_lines(own_ref, near_refs, first_ref, second_ref))
    grad_x = line_blur(mixed[0:lines], False)
    grad_y = line_blur(mixed[lines : 2 * lines], True)
    grad_z = line_blur(mixed[2 * lines : 3 * lines], False)
    store_fields([grad_x, grad_y, grad_z], lines, out_ref, exact_ref)


def model_kernel(lines, _, table_ref, target_ref, own_ref, *refs):
    *near_refs, first_ref, second_ref, out_ref, exact_ref, sum_ref = refs
    smooth = mix_lines(table_ref, window_lines(own_ref, near_refs, first_ref, second_ref))
    model = smooth[3 * lines :]
    target = target_ref[...]
    sums = [jnp.sum(model * target), jnp.sum(model * model), jnp.sum(target * target)]
    lane = lax.broadcasted_iota(I32, sum_ref.shape, 1)
    total = jnp.zeros(sum_ref.shape, F32)
    for k, value in enumerate(sums):
        total = jnp.where(lane == k, value, total)
    sum_ref[...] = total
    grad_x = line_blur(smooth[0:lines], False)
    grad_y = line_blur(smooth[lines : 2 * lines], True)
    grad_z = line_blur(smooth[2 * lines : 3 * lines], False)
    store_fields([grad_x, grad_y, grad_z], lines, out_ref, exact_ref)


def sample_by_matmul(word, field_ref, his, store):
    count, beads = word.shape
    lo, hi = word & (LO - 1), (word >> 8) & 255
    lo_iota = lax.broadcasted_iota(I32, (LO, beads), 0)
    picks = [jnp.where(lo_iota == lo[q : q + 1], 1.0, 0.0).astype(BF16) for q in range(count)]
    pick = jnp.concatenate(picks, axis=1)
    sampled = jnp.dot(
        field_ref[...], jnp.concatenate([pick, pick], axis=0), preferred_element_type=F32
    )

    def finish():
        sub_iota = lax.broadcasted_iota(I32, (8, beads), 0)
        for q in range(count):
            own = jnp.broadcast_to(hi[q : q + 1], (8, beads))
            group, within = own >> 3, (own & 7) == sub_iota
            found = [jnp.zeros((8, beads), F32)] * 3
            for j in range(his // 8):
                here = group == j
                for k in range(3):
                    rows = slice(k * his + 8 * j, k * his + 8 * j + 8)
                    part = sampled[rows, q * beads : (q + 1) * beads]
                    found[k] = jnp.where(here, part, found[k])
            store(q, [jnp.sum(jnp.where(within, v, 0.0), axis=0, keepdims=True) for v in found])

    return finish


def sample_by_lanes(word, exact_ref, lines, store):
    count, beads = word.shape
    tiles = exact_ref.shape[1] // 128
    line_shift, lo_shift = lines.bit_length() - 1, LO.bit_length() - 1
    sub_iota = lax.broadcasted_iota(I32, (8, beads), 0)
    for q in range(count):
        own = jnp.broadcast_to(word[q : q + 1], (8, beads))
        lo, hi = own & (LO - 1), (own >> lo_shift) & 255
        line = hi & (lines - 1)
        group = (line >> 3) * tiles + (hi >> line_shift) * (LO // 128) + (lo >> 7)
        within, lane = (line & 7) == sub_iota, lo & 127
        found = [jnp.zeros((8, beads), F32)] * 3
        for j in range(lines // 8 * tiles):
            here = group == j
            first, tile = j // tiles * 8, j % tiles * 128
            for k in range(3):
                table = exact_ref[k * lines + first : k * lines + first + 8, tile : tile + 128]
                part = jnp.take_along_axis(table, lane, axis=1, mode="promise_in_bounds")
                found[k] = jnp.where(here, part, found[k])
        store(q, [jnp.sum(jnp.where(within, v, 0.0), axis=0, keepdims=True) for v in found])


def sample_kernel(
    lines, his, rb, by_lanes, start, got_ref, field_ref, exact_ref, out_ref, force_ref
):
    slots = out_ref.shape[0]
    beads = got_ref.shape[1] // 3
    by_matmul = rb - by_lanes

    def body(i, carry):
        def store_from(first):
            def store(q, values):
                for k in range(3):
                    force_ref[k, pl.ds(i * rb + first + q, 1), :] = values[k]

            return store

        word = got_ref[pl.ds(start + i * rb, rb), 0:beads]
        finish = sample_by_matmul(word[:by_matmul], field_ref, his, store_from(0))
        sample_by_lanes(word[by_matmul:], exact_ref, lines, store_from(by_matmul))
        finish()
        return carry

    lax.fori_loop(0, slots // rb, body, 0)
    rows = slice(start, start + slots)
    first, second = got_ref[rows, beads : 2 * beads], got_ref[rows, 2 * beads : 3 * beads]
    weight = (got_ref[rows, 0:beads] >> 16).astype(F32) * (1.0 / WEIGHT_SCALE)
    lever_z = (((first & 2047) << 10) | (second & 1023)) - LEVER_BIAS
    levers = [
        v.astype(F32) * (1.0 / LEVER_SCALE) for v in (first >> 11, second >> 11, lever_z)
    ]
    force = [force_ref[k] * weight for k in range(3)]
    terms = force + [
        levers[1] * force[2] - levers[2] * force[1],
        levers[2] * force[0] - levers[0] * force[2],
        levers[0] * force[1] - levers[1] * force[0],
    ]
    lane = lax.broadcasted_iota(I32, out_ref.shape, 1)
    total = jnp.zeros(out_ref.shape, F32)
    for k, term in enumerate(terms):
        total = jnp.where(lane == k, jnp.sum(term, axis=1, keepdims=True), total)
    out_ref[...] = total


def join_kernel(most, first_ref, second_ref, model_ref, sum_ref, out_ref):
    bricks = out_ref.shape[0]
    lane = lax.broadcasted_iota(I32, out_ref.shape, 1)
    sums = sum_ref[0:1, :]
    for k in range(1, sum_ref.shape[0] // 8):
        sums = sums + sum_ref[8 * k : 8 * k + 1, :]
    total = jnp.zeros(out_ref.shape, F32)
    for k in range(most):
        rows, half = pl.ds(k, bricks, stride=most), pl.ds(k, bricks // 2, stride=most)
        own = jnp.concatenate([first_ref[half, :], second_ref[half, :]], axis=0)
        own = jnp.where(lane < 6, own, 0.0)
        own = own + pltpu.roll(jnp.where(lane < 6, model_ref[rows, :], 0.0), 6, 1)
        if k == 0:
            own = own + pltpu.roll(jnp.where(lane < 3, sums, 0.0), 12, 1)
        total = total + (pltpu.roll(own, FIELDS * k, 1) if k else own)
    out_ref[...] = total


def finish_kernel(most, voxel_total, place_ref, back_ref, out_ref):
    frags = out_ref.shape[1]
    bricks = back_ref.shape[0]
    row, rank = place_ref[0:1, :], place_ref[1:2, :]
    place = jnp.where(lax.broadcasted_iota(I32, (bricks, frags), 0) == row, 1.0, 0.0).astype(F32)
    back = back_ref[...]
    sums = jnp.sum(back, axis=0, keepdims=True)
    cross, model_sq, target_sq = sums[:, 12:13], sums[:, 13:14], sums[:, 14:15]
    norm_model = jnp.sqrt(model_sq + EPSILON)
    norm_target = jnp.sqrt(target_sq + EPSILON)
    corr = cross / (norm_model * norm_target)
    scale_target = voxel_total / (norm_model * norm_target)
    scale_model = voxel_total * corr / (norm_model * norm_model)
    found = lax.dot_general(
        back, place, (((0,), (0,)), ((), ())), precision=HIGHEST, preferred_element_type=F32
    )
    mine = jnp.zeros((FIELDS, frags), F32)
    for k in range(most):
        mine = jnp.where(rank == k, found[FIELDS * k : FIELDS * (k + 1)], mine)
    out_ref[...] = scale_target * mine[0:6] - scale_model * mine[6:12]


def cost(macs, nbytes):
    return pl.CostEstimate(flops=2 * macs, bytes_accessed=nbytes, transcendentals=0)


def call(
    kernel, out_shape, *args, scratch=(), name=None, macs=0, in_specs=None, vmem=VMEM_BYTES
):
    kwargs = {} if in_specs is None else {"in_specs": in_specs}
    return pl.pallas_call(
        kernel,
        out_shape=out_shape,
        scratch_shapes=list(scratch),
        compiler_params=pltpu.CompilerParams(vmem_limit_bytes=vmem),
        cost_estimate=cost(macs, 4 * sum(a.size for a in args)),
        name=name,
        **kwargs,
    )(*args)


def call_at(kernel, out_shape, index, table, *args, name=None, macs=0):
    def whole(shape):
        return pl.BlockSpec(shape, lambda i, s: (0,) * len(shape))

    single = not isinstance(out_shape, list)
    outs = [out_shape] if single else out_shape
    specs = [whole(o.shape) for o in outs]
    return pl.pallas_call(
        kernel,
        out_shape=out_shape,
        grid_spec=pltpu.PrefetchScalarGridSpec(
            num_scalar_prefetch=1,
            grid=(1,),
            in_specs=[pl.BlockSpec((1,) + table.shape[1:], lambda i, s: (s[0], 0, 0))]
            + [whole(a.shape) for a in args],
            out_specs=specs[0] if single else specs,
        ),
        compiler_params=pltpu.CompilerParams(vmem_limit_bytes=VMEM_BYTES),
        cost_estimate=cost(macs, 4 * sum(a.size for a in args)),
        name=name,
    )(index, table, *args)


def looked_up(values, position):
    found = jnp.full((), int(values[0]), I32)
    for i in range(1, len(values)):
        step = int(values[i]) - int(values[i - 1])
        if step:
            found = found + step * (position >= i).astype(I32)
    return found


def shifted(value, axis, step):
    size = lax.axis_size(axis)
    pairs = [(i, i + step) for i in range(size) if 0 <= i + step < size]
    return lax.ppermute(value, axis, pairs)


def paired(own, left, right):
    return lambda b: [own, right, left] if b % 2 == 0 else [own, left, right]


def swapped(first, second):
    size = lax.axis_size("brick")
    found = []
    for value, start in ((first, 0), (second, 1)):
        pairs = [(i, i + 1) for i in range(start, size - 1, 2)]
        found.append(lax.ppermute(value, "brick", pairs + [(j, i) for i, j in pairs]))
    return found


def relay_blocks(value, reach):
    size = lax.axis_size("relay")
    if size == 2:
        return [value, lax.ppermute(value, "relay", [(0, 1), (1, 0)])]
    blocks = [value]
    for step in range(1, min(reach, size - 1) + 1):
        blocks += [shifted(value, "relay", step), shifted(value, "relay", -step)]
    return blocks


def relay_order(size, reach):
    if size == 2:
        return lambda r: [r, 1 - r]
    steps = [0]
    for step in range(1, min(reach, size - 1) + 1):
        steps += [-step, step]
    return lambda r: [r + s for s in steps]


def relay_total(value):
    size = lax.axis_size("relay")
    values, moving = [value], value
    for _ in range(size - 1):
        moving = lax.ppermute(moving, "relay", [(i, (i + 1) % size) for i in range(size)])
        values.append(moving)
    return jnp.concatenate(values, axis=0)


def shards(target, frag_brick, bead_cell, bead_weight, bead_arm, frag_angle):
    brick_count, relay_count = lax.axis_size("brick"), lax.axis_size("relay")
    frags, beads = bead_cell.shape
    planes, columns, rows = target.shape
    lines = planes * columns
    his = lines * (rows // LO)
    assert rows % LO == 0 and his <= 256 and columns >= 2 * KR
    assert beads == 128 and lines & (lines - 1) == 0
    voxel_total = float(brick_count * columns * relay_count * planes * rows)
    most = max(2, 2 * frags // brick_count)
    slots = brick_count * most
    assert most * FIELDS <= 128

    z_total, x_total = relay_count * planes, brick_count * columns
    gz, dz = axis_matrix(z_total, False), axis_matrix(z_total, True)
    gx, dx = axis_matrix(x_total, False), axis_matrix(x_total, True)
    reach_one, reach_two = -(-KR // planes), -(-2 * KR // planes)
    target_table, tz, tx, tn = weight_table(
        [gz, gz, dz], [dx, gx, gx], planes, relay_count, relay_order(relay_count, reach_one),
        columns, brick_count,
        paired(np.arange(columns), np.arange(-KR, 0), np.arange(columns, columns + KR)),
    )
    model_table, mz, mx, mn = weight_table(
        [gz @ gz, gz @ gz, dz @ gz, gz], [dx @ gx, gx @ gx, gx @ gx, gx],
        planes, relay_count, relay_order(relay_count, reach_two), columns, brick_count,
        paired(np.arange(columns), np.arange(-columns, 0), np.arange(columns, 2 * columns)),
    )
    r, b = lax.axis_index("relay"), lax.axis_index("brick")
    target_index = (looked_up(tz, r) * tn + looked_up(tx, b)).reshape(1)
    model_index = (looked_up(mz, r) * mn + looked_up(mx, b)).reshape(1)

    target_lines = target.reshape(lines, rows)
    words = jax.ShapeDtypeStruct((lines // 2, rows + SCALE_LANES), I32)
    hbm = pl.BlockSpec(memory_space=pltpu.HBM)
    packed = [frag_brick.reshape(1, frags), frag_angle, bead_cell, bead_weight, bead_arm]
    packed += [target_lines]
    sent, place, target_code = call(
        functools.partial(pack_kernel, most, lines, rows),
        [
            jax.ShapeDtypeStruct((slots, 3 * beads), I32),
            jax.ShapeDtypeStruct((8, frags), I32),
            words,
        ],
        *packed,
        in_specs=[hbm] * len(packed),
        scratch=[pltpu.VMEM(a.shape, a.dtype) for a in packed]
        + [pltpu.SemaphoreType.DMA((len(packed),))],
        name="pack",
        vmem=PACK_VMEM_BYTES,
    )
    target_blocks = relay_blocks(target_code, reach_one)
    by_column = [t.reshape(-1, columns, rows + SCALE_LANES) for t in target_blocks]
    left_edge = jnp.concatenate([t[:, columns - KR :] for t in by_column], axis=0)
    right_edge = jnp.concatenate([t[:, :KR] for t in by_column], axis=0)
    first_edge = jnp.where(b % 2 == 0, left_edge, right_edge)
    second_edge = jnp.where(b % 2 == 0, right_edge, left_edge)
    target_near = swapped(
        first_edge.reshape(-1, rows + SCALE_LANES), second_edge.reshape(-1, rows + SCALE_LANES)
    )

    got = lax.all_to_all(sent, "brick", split_axis=0, concat_axis=0, tiled=True)
    smooth, coded = call(
        functools.partial(splat_kernel, lines, min(64, slots)),
        [jax.ShapeDtypeStruct((lines, rows), F32), words],
        got,
        scratch=[pltpu.VMEM((his, LO), F32)],
        name="splat",
        macs=slots * beads * his * LO,
    )
    coded, *target_near = lax.optimization_barrier((coded, *target_near))
    target_parts = [target_lines] + target_blocks[1:] + target_near
    blocks = relay_blocks(coded, reach_two)
    field_shapes = [
        jax.ShapeDtypeStruct((3 * his, 2 * LO), BF16),
        jax.ShapeDtypeStruct((3 * lines, rows), F32),
    ]
    target_field = call_at(
        functools.partial(target_kernel, lines),
        field_shapes,
        target_index, jnp.asarray(target_table), *target_parts,
        name="target_fields",
        macs=9 * lines * rows * 128,
    )

    def sample(field, start, count, name):
        rb = min(32, count)
        return call(
            functools.partial(sample_kernel, lines, his, rb, rb * 5 // 16, start),
            jax.ShapeDtypeStruct((count, 128), F32),
            got, *field,
            scratch=[pltpu.VMEM((3, count, beads), F32)],
            name=name,
            macs=6 * count * beads * his * LO,
        )

    half = slots // 2
    target_first = sample(target_field, 0, half, "target_sample_a")
    blocks, target_first, target_field = lax.optimization_barrier(
        (blocks, target_first, target_field)
    )
    beside = jnp.concatenate(blocks, axis=0)
    model_parts = [smooth] + blocks[1:]
    model_parts += swapped(beside, beside)
    target_second = sample(target_field, half, slots - half, "target_sample_b")
    target_second, *model_parts = lax.optimization_barrier((target_second, *model_parts))
    *model_field, partial = call_at(
        functools.partial(model_kernel, lines),
        field_shapes + [jax.ShapeDtypeStruct((8, 128), F32)],
        model_index, jnp.asarray(model_table), target_lines, *model_parts,
        name="model_fields",
    )
    partials = relay_total(partial)
    model_sums = sample(model_field, 0, slots, "model_sample")
    leaving = call(
        functools.partial(join_kernel, most),
        jax.ShapeDtypeStruct((brick_count, 128), F32),
        target_first, target_second, model_sums, partials,
        name="join",
    )
    back = lax.all_to_all(leaving, "brick", split_axis=0, concat_axis=0, tiled=True)
    return call(
        functools.partial(finish_kernel, most, voxel_total),
        jax.ShapeDtypeStruct((6, frags), F32),
        place, back,
        name="finish",
    )


def solution(mesh):
    placed = (
        P("relay", "brick", None),
        P(("brick", "relay"), None),
        P(("brick", "relay"), None),
        P(("brick", "relay"), None),
        P(None, ("brick", "relay"), None),
        P(None, ("brick", "relay")),
    )
    return jax.shard_map(
        shards, mesh=mesh, in_specs=placed, out_specs=P(None, ("brick", "relay")), check_vma=False
    )
```

```python
import functools

import jax
import jax.numpy as jnp
import numpy as np
from jax import lax
from jax.experimental import pallas as pl
from jax.experimental.pallas import tpu as pltpu
from jax.sharding import PartitionSpec as P

KR = 4
SIGMA = 1.5
EPSILON = 1e-06
HIGHEST = lax.Precision.HIGHEST
LO = 256
FIELDS = 16
WEIGHT_SCALE = 512.0
LEVER_SCALE = 32768.0
LEVER_BIAS = 1 << 20
CODE_TOP = 65535
SCALE_UNIT = 512.0
SCALE_LANES = 128
VMEM_BYTES = 48 << 20
PACK_VMEM_BYTES = 60 << 20
F32 = jnp.float32
BF16 = jnp.bfloat16
I32 = jnp.int32


def taps_of(derivative):
    offsets = np.arange(-KR, KR + 1) * 1.0
    gaussian = np.exp(-(offsets**2) / (2.0 * SIGMA**2))
    gaussian = gaussian / gaussian.sum()
    if derivative:
        return -offsets / SIGMA**2 * gaussian
    return gaussian


def axis_matrix(length, derivative):
    offsets = np.arange(length)[:, None] - np.arange(length)[None, :]
    return np.where(
        np.abs(offsets) <= KR, taps_of(derivative)[np.clip(offsets + KR, 0, 2 * KR)], 0.0
    )


def columns_at(matrix, rows, wanted):
    inside = (wanted >= 0) & (wanted < matrix.shape[1])
    picked = matrix[rows][:, np.clip(wanted, 0, matrix.shape[1] - 1)]
    return np.where(inside[None, :], picked, 0.0)


def unique_tables(tables):
    flat = np.stack([t.reshape(-1) for t in tables])
    kept, inverse = np.unique(np.round(flat, 14), axis=0, return_inverse=True)
    return kept.reshape((-1,) + tables[0].shape), inverse.reshape(-1).astype(np.int32)


def pieces_np(table):
    import ml_dtypes

    high = table.astype(np.float32).astype(ml_dtypes.bfloat16)
    low = (table - high.astype(np.float64)).astype(ml_dtypes.bfloat16)
    return np.concatenate([high, high, low], axis=-1)


def weight_table(z_kinds, x_kinds, z_len, z_count, z_blocks, x_len, x_count, x_parts):
    z_tables = []
    for r in range(z_count):
        wanted = np.concatenate([np.arange(z_len) + z_len * block for block in z_blocks(r)])
        rows = np.arange(z_len) + z_len * r
        z_tables.append(np.stack([columns_at(m, rows, wanted) for m in z_kinds]))
    x_tables = []
    for b in range(x_count):
        wanted = np.concatenate([x_len * b + part for part in x_parts(b)])
        rows = np.arange(x_len) + x_len * b
        x_tables.append(np.stack([columns_at(m, rows, wanted) for m in x_kinds]))
    z_tables, z_inverse = unique_tables(z_tables)
    x_tables, x_inverse = unique_tables(x_tables)
    kinds = len(z_kinds)
    parts, start = [], 0
    for part in x_parts(0):
        piece = x_tables[:, :, :, start : start + len(part)]
        start += len(part)
        full = np.einsum("rkzi,bkxj->rbkzxij", z_tables, piece)
        parts.append(
            full.reshape(len(z_tables) * len(x_tables), kinds * z_len * x_len, -1)
        )
    table = pieces_np(np.concatenate(parts, axis=-1))
    return table, z_inverse, x_inverse, len(x_tables)


def eye_column(row, eye):
    return jnp.sum(jnp.where(eye, row, jnp.zeros_like(row)), axis=1, keepdims=True)


def slot_row(row, most):
    frags = row.shape[1]
    sub = lax.broadcasted_iota(I32, (frags, frags), 0)
    lane = lax.broadcasted_iota(I32, (frags, frags), 1)
    eye = sub == lane
    earlier = jnp.logical_and(eye_column(row, eye) == row, sub < lane)
    return jnp.sum(jnp.where(earlier, 1, 0), axis=0, keepdims=True), eye


def pack_kernel(most, lines, row_count, *refs):
    inputs, (out_ref, place_ref, code_ref) = refs[:6], refs[6:9]
    held, sems = refs[9:15], refs[15]
    copies = [
        pltpu.make_async_copy(source, target, sems.at[k])
        for k, (source, target) in enumerate(zip(inputs, held))
    ]
    for copy in copies:
        copy.start()
    brick_ref, angle_ref, cell_ref, weight_ref, arm_ref, target_ref = held
    for copy in copies[:2]:
        copy.wait()
    frags, beads = cell_ref.shape
    slots = out_ref.shape[0]
    row = brick_ref[...]
    rank, eye = slot_row(row, most)
    slot = row * most + rank
    place = jnp.where(lax.broadcasted_iota(I32, (slots, frags), 0) == slot, 1.0, 0.0).astype(F32)

    angles = angle_ref[...]
    cos, sin = jnp.cos(angles), jnp.sin(angles)
    cos_a, cos_b, cos_c = cos[0:1], cos[1:2], cos[2:3]
    sin_a, sin_b, sin_c = sin[0:1], sin[1:2], sin[2:3]
    turn = [
        [cos_a * cos_b, cos_a * sin_b * sin_c - sin_a * cos_c, cos_a * sin_b * cos_c + sin_a * sin_c],
        [sin_a * cos_b, sin_a * sin_b * sin_c + cos_a * cos_c, sin_a * sin_b * cos_c - cos_a * sin_c],
        [-sin_b, cos_b * sin_c, cos_b * cos_c],
    ]
    turn = [[eye_column(value, eye) for value in values] for values in turn]
    place_ref[0:1, :] = row
    place_ref[1:2, :] = rank
    for copy in copies[2:]:
        copy.wait()
    encode(target_ref[...], code_ref)
    levers = []
    for i in range(3):
        total = turn[i][0] * arm_ref[0]
        for j in (1, 2):
            total = total + turn[i][j] * arm_ref[j]
        levers.append(jnp.round(total * LEVER_SCALE))

    cell = cell_ref[...]
    line = ((cell.astype(F32) + 0.5) * (1.0 / row_count)).astype(I32)
    y = cell - line * row_count
    code = (((y // LO) * lines + line) * LO + (y % LO)).astype(F32)
    weight = weight_ref[...].astype(F32) * WEIGHT_SCALE
    payload = jnp.concatenate([code, weight] + levers, axis=1)
    placed = jnp.dot(place, payload, precision=HIGHEST, preferred_element_type=F32)
    placed = placed.astype(I32)
    code, weight, lx, ly, lz = [placed[:, k * beads : (k + 1) * beads] for k in range(5)]
    lz = lz + LEVER_BIAS
    out_ref[:, 0:beads] = code | (weight << 16)
    out_ref[:, beads : 2 * beads] = (lx << 11) | (lz >> 10)
    out_ref[:, 2 * beads : 3 * beads] = (ly << 11) | (lz & 1023)


def line_blur(value, derivative):
    taps = taps_of(derivative)
    rows, length = value.shape
    wide = jnp.concatenate([value, jnp.zeros((rows, 128), F32)], axis=1)
    total = None if derivative else float(taps[KR]) * value
    for d in range(1, KR + 1):
        up = pltpu.roll(wide, d, 1)[:, :length]
        down = pltpu.roll(wide, length + 128 - d, 1)[:, :length]
        pair = up - down if derivative else up + down
        term = float(taps[KR + d]) * pair
        total = term if total is None else total + term
    return total


def encode(value, out_ref):
    half, length = value.shape[0] // 2, value.shape[1]
    top = (jnp.max(value) * SCALE_UNIT).astype(I32) + 1
    scale = (SCALE_UNIT * CODE_TOP) / top.astype(F32)
    code = jnp.minimum((value * scale + 0.5).astype(I32), CODE_TOP)
    out_ref[:, :length] = code[:half] | (code[half:] << 16)
    out_ref[:, length:] = jnp.full((half, SCALE_LANES), top, I32)


def decode(words, count):
    half, length = words.shape[0] // count, words.shape[1] - SCALE_LANES
    step = words[:, length : length + 1].astype(F32) * (1.0 / (SCALE_UNIT * CODE_TOP))
    low = (words[:, :length] & CODE_TOP).astype(F32) * step
    high = ((words[:, :length] >> 16) & CODE_TOP).astype(F32) * step
    lines = []
    for k in range(count):
        rows = slice(k * half, (k + 1) * half)
        lines += [low[rows], high[rows]]
    return lines


def splat_kernel(lines, rb, got_ref, out_ref, code_ref, acc_ref):
    slots = got_ref.shape[0]
    beads = got_ref.shape[1] // 3
    his = acc_ref.shape[0]
    acc_ref[...] = jnp.zeros_like(acc_ref)
    hi_iota = lax.broadcasted_iota(I32, (his, beads), 0)
    lo_iota = lax.broadcasted_iota(I32, (LO, beads), 0)

    def body(i, carry):
        word = got_ref[pl.ds(i * rb, rb), 0:beads]
        lo = word & (LO - 1)
        hi = (word >> 8) & 255
        weight = (word >> 16).astype(F32) * (1.0 / WEIGHT_SCALE)
        left, right = [], []
        for q in range(rb):
            left.append(jnp.where(hi_iota == hi[q : q + 1], weight[q : q + 1], 0.0).astype(BF16))
            right.append(jnp.where(lo_iota == lo[q : q + 1], 1.0, 0.0).astype(BF16))
        acc_ref[...] += lax.dot_general(
            jnp.concatenate(left, axis=1),
            jnp.concatenate(right, axis=1),
            (((1,), (1,)), ((), ())),
            preferred_element_type=F32,
        )
        return carry

    lax.fori_loop(0, slots // rb, body, 0)
    density = [acc_ref[yh * lines : (yh + 1) * lines, :] for yh in range(his // lines)]
    smooth = line_blur(jnp.concatenate(density, axis=1), False)
    out_ref[...] = smooth
    encode(smooth, code_ref)


def split(value):
    high = value.astype(BF16)
    low = (value - high.astype(F32)).astype(BF16)
    return high, low


def mix_lines(table_ref, parts):
    value = jnp.concatenate(parts, axis=0)
    high, low = split(value)
    return jnp.dot(
        table_ref[0], jnp.concatenate([high, low, high], axis=0), preferred_element_type=F32
    )


def store_fields(fields, lines, out_ref, exact_ref):
    his = fields[0].shape[1] // LO * lines
    for k, field in enumerate(fields):
        exact_ref[k * lines : (k + 1) * lines, :] = field
        for yh in range(field.shape[1] // LO):
            high, low = split(field[:, yh * LO : (yh + 1) * LO])
            rows = slice(k * his + yh * lines, k * his + (yh + 1) * lines)
            out_ref[rows, 0:LO] = high
            out_ref[rows, LO : 2 * LO] = low


def window_lines(own_ref, near_refs, first_ref, second_ref):
    lines = [own_ref[...]]
    for ref in near_refs:
        lines += decode(ref[...], 1)
    for ref in (first_ref, second_ref):
        lines += decode(ref[...], len(near_refs) + 1)
    return lines


def target_kernel(lines, _, table_ref, own_ref, *refs):
    *near_refs, first_ref, second_ref, out_ref, exact_ref = refs
    mixed = mix_lines(table_ref, window_lines(own_ref, near_refs, first_ref, second_ref))
    grad_x = line_blur(mixed[0:lines], False)
    grad_y = line_blur(mixed[lines : 2 * lines], True)
    grad_z = line_blur(mixed[2 * lines : 3 * lines], False)
    store_fields([grad_x, grad_y, grad_z], lines, out_ref, exact_ref)


def model_kernel(lines, _, table_ref, target_ref, own_ref, *refs):
    *near_refs, first_ref, second_ref, out_ref, exact_ref, sum_ref = refs
    smooth = mix_lines(table_ref, window_lines(own_ref, near_refs, first_ref, second_ref))
    model = smooth[3 * lines :]
    target = target_ref[...]
    sums = [jnp.sum(model * target), jnp.sum(model * model), jnp.sum(target * target)]
    lane = lax.broadcasted_iota(I32, sum_ref.shape, 1)
    total = jnp.zeros(sum_ref.shape, F32)
    for k, value in enumerate(sums):
        total = jnp.where(lane == k, value, total)
    sum_ref[...] = total
    grad_x = line_blur(smooth[0:lines], False)
    grad_y = line_blur(smooth[lines : 2 * lines], True)
    grad_z = line_blur(smooth[2 * lines : 3 * lines], False)
    store_fields([grad_x, grad_y, grad_z], lines, out_ref, exact_ref)


def sample_by_matmul(word, field_ref, his, store):
    count, beads = word.shape
    lo, hi = word & (LO - 1), (word >> 8) & 255
    lo_iota = lax.broadcasted_iota(I32, (LO, beads), 0)
    picks = [jnp.where(lo_iota == lo[q : q + 1], 1.0, 0.0).astype(BF16) for q in range(count)]
    pick = jnp.concatenate(picks, axis=1)
    sampled = jnp.dot(
        field_ref[...], jnp.concatenate([pick, pick], axis=0), preferred_element_type=F32
    )

    def finish():
        sub_iota = lax.broadcasted_iota(I32, (8, beads), 0)
        for q in range(count):
            own = jnp.broadcast_to(hi[q : q + 1], (8, beads))
            group, within = own >> 3, (own & 7) == sub_iota
            found = [jnp.zeros((8, beads), F32)] * 3
            for j in range(his // 8):
                here = group == j
                for k in range(3):
                    rows = slice(k * his + 8 * j, k * his + 8 * j + 8)
                    part = sampled[rows, q * beads : (q + 1) * beads]
                    found[k] = jnp.where(here, part, found[k])
            store(q, [jnp.sum(jnp.where(within, v, 0.0), axis=0, keepdims=True) for v in found])

    return finish


def sample_by_lanes(word, exact_ref, lines, store):
    count, beads = word.shape
    tiles = exact_ref.shape[1] // 128
    line_shift, lo_shift = lines.bit_length() - 1, LO.bit_length() - 1
    sub_iota = lax.broadcasted_iota(I32, (8, beads), 0)
    for q in range(count):
        own = jnp.broadcast_to(word[q : q + 1], (8, beads))
        lo, hi = own & (LO - 1), (own >> lo_shift) & 255
        line = hi & (lines - 1)
        group = (line >> 3) * tiles + (hi >> line_shift) * (LO // 128) + (lo >> 7)
        within, lane = (line & 7) == sub_iota, lo & 127
        found = [jnp.zeros((8, beads), F32)] * 3
        for j in range(lines // 8 * tiles):
            here = group == j
            first, tile = j // tiles * 8, j % tiles * 128
            for k in range(3):
                table = exact_ref[k * lines + first : k * lines + first + 8, tile : tile + 128]
                part = jnp.take_along_axis(table, lane, axis=1, mode="promise_in_bounds")
                found[k] = jnp.where(here, part, found[k])
        store(q, [jnp.sum(jnp.where(within, v, 0.0), axis=0, keepdims=True) for v in found])


def sample_kernel(
    lines, his, rb, by_lanes, start, got_ref, field_ref, exact_ref, out_ref, force_ref
):
    slots = out_ref.shape[0]
    beads = got_ref.shape[1] // 3
    by_matmul = rb - by_lanes

    def body(i, carry):
        def store_from(first):
            def store(q, values):
                for k in range(3):
                    force_ref[k, pl.ds(i * rb + first + q, 1), :] = values[k]

            return store

        word = got_ref[pl.ds(start + i * rb, rb), 0:beads]
        finish = sample_by_matmul(word[:by_matmul], field_ref, his, store_from(0))
        sample_by_lanes(word[by_matmul:], exact_ref, lines, store_from(by_matmul))
        finish()
        return carry

    lax.fori_loop(0, slots // rb, body, 0)
    rows = slice(start, start + slots)
    first, second = got_ref[rows, beads : 2 * beads], got_ref[rows, 2 * beads : 3 * beads]
    weight = (got_ref[rows, 0:beads] >> 16).astype(F32) * (1.0 / WEIGHT_SCALE)
    lever_z = (((first & 2047) << 10) | (second & 1023)) - LEVER_BIAS
    levers = [
        v.astype(F32) * (1.0 / LEVER_SCALE) for v in (first >> 11, second >> 11, lever_z)
    ]
    force = [force_ref[k] * weight for k in range(3)]
    terms = force + [
        levers[1] * force[2] - levers[2] * force[1],
        levers[2] * force[0] - levers[0] * force[2],
        levers[0] * force[1] - levers[1] * force[0],
    ]
    lane = lax.broadcasted_iota(I32, out_ref.shape, 1)
    total = jnp.zeros(out_ref.shape, F32)
    for k, term in enumerate(terms):
        total = jnp.where(lane == k, jnp.sum(term, axis=1, keepdims=True), total)
    out_ref[...] = total


def join_kernel(most, *refs):
    *target_refs, model_ref, sum_ref, out_ref = refs
    bricks = out_ref.shape[0]
    lane = lax.broadcasted_iota(I32, out_ref.shape, 1)
    sums = sum_ref[0:1, :]
    for k in range(1, sum_ref.shape[0] // 8):
        sums = sums + sum_ref[8 * k : 8 * k + 1, :]
    total = jnp.zeros(out_ref.shape, F32)
    for k in range(most):
        rows = pl.ds(k, bricks, stride=most)
        parts = [ref[pl.ds(k, ref.shape[0] // most, stride=most), :] for ref in target_refs]
        own = jnp.concatenate(parts, axis=0)
        own = jnp.where(lane < 6, own, 0.0)
        own = own + pltpu.roll(jnp.where(lane < 6, model_ref[rows, :], 0.0), 6, 1)
        if k == 0:
            own = own + pltpu.roll(jnp.where(lane < 3, sums, 0.0), 12, 1)
        total = total + (pltpu.roll(own, FIELDS * k, 1) if k else own)
    out_ref[...] = total


def finish_kernel(most, voxel_total, place_ref, back_ref, out_ref):
    frags = out_ref.shape[1]
    bricks = back_ref.shape[0]
    row, rank = place_ref[0:1, :], place_ref[1:2, :]
    place = jnp.where(lax.broadcasted_iota(I32, (bricks, frags), 0) == row, 1.0, 0.0).astype(F32)
    back = back_ref[...]
    sums = jnp.sum(back, axis=0, keepdims=True)
    cross, model_sq, target_sq = sums[:, 12:13], sums[:, 13:14], sums[:, 14:15]
    norm_model = jnp.sqrt(model_sq + EPSILON)
    norm_target = jnp.sqrt(target_sq + EPSILON)
    corr = cross / (norm_model * norm_target)
    scale_target = voxel_total / (norm_model * norm_target)
    scale_model = voxel_total * corr / (norm_model * norm_model)
    found = lax.dot_general(
        back, place, (((0,), (0,)), ((), ())), precision=HIGHEST, preferred_element_type=F32
    )
    mine = jnp.zeros((FIELDS, frags), F32)
    for k in range(most):
        mine = jnp.where(rank == k, found[FIELDS * k : FIELDS * (k + 1)], mine)
    out_ref[...] = scale_target * mine[0:6] - scale_model * mine[6:12]


def cost(macs, nbytes):
    return pl.CostEstimate(flops=2 * macs, bytes_accessed=nbytes, transcendentals=0)


def call(
    kernel, out_shape, *args, scratch=(), name=None, macs=0, in_specs=None, vmem=VMEM_BYTES
):
    kwargs = {} if in_specs is None else {"in_specs": in_specs}
    return pl.pallas_call(
        kernel,
        out_shape=out_shape,
        scratch_shapes=list(scratch),
        compiler_params=pltpu.CompilerParams(vmem_limit_bytes=vmem),
        cost_estimate=cost(macs, 4 * sum(a.size for a in args)),
        name=name,
        **kwargs,
    )(*args)


def call_at(kernel, out_shape, index, table, *args, name=None, macs=0):
    def whole(shape):
        return pl.BlockSpec(shape, lambda i, s: (0,) * len(shape))

    single = not isinstance(out_shape, list)
    outs = [out_shape] if single else out_shape
    specs = [whole(o.shape) for o in outs]
    return pl.pallas_call(
        kernel,
        out_shape=out_shape,
        grid_spec=pltpu.PrefetchScalarGridSpec(
            num_scalar_prefetch=1,
            grid=(1,),
            in_specs=[pl.BlockSpec((1,) + table.shape[1:], lambda i, s: (s[0], 0, 0))]
            + [whole(a.shape) for a in args],
            out_specs=specs[0] if single else specs,
        ),
        compiler_params=pltpu.CompilerParams(vmem_limit_bytes=VMEM_BYTES),
        cost_estimate=cost(macs, 4 * sum(a.size for a in args)),
        name=name,
    )(index, table, *args)


def looked_up(values, position):
    found = jnp.full((), int(values[0]), I32)
    for i in range(1, len(values)):
        step = int(values[i]) - int(values[i - 1])
        if step:
            found = found + step * (position >= i).astype(I32)
    return found


def shifted(value, axis, step):
    size = lax.axis_size(axis)
    pairs = [(i, i + step) for i in range(size) if 0 <= i + step < size]
    return lax.ppermute(value, axis, pairs)


def paired(own, left, right):
    return lambda b: [own, right, left] if b % 2 == 0 else [own, left, right]


def swapped(first, second):
    size = lax.axis_size("brick")
    found = []
    for value, start in ((first, 0), (second, 1)):
        pairs = [(i, i + 1) for i in range(start, size - 1, 2)]
        found.append(lax.ppermute(value, "brick", pairs + [(j, i) for i, j in pairs]))
    return found


def relay_blocks(value, reach):
    size = lax.axis_size("relay")
    if size == 2:
        return [value, lax.ppermute(value, "relay", [(0, 1), (1, 0)])]
    blocks = [value]
    for step in range(1, min(reach, size - 1) + 1):
        blocks += [shifted(value, "relay", step), shifted(value, "relay", -step)]
    return blocks


def relay_order(size, reach):
    if size == 2:
        return lambda r: [r, 1 - r]
    steps = [0]
    for step in range(1, min(reach, size - 1) + 1):
        steps += [-step, step]
    return lambda r: [r + s for s in steps]


def relay_total(value):
    size = lax.axis_size("relay")
    values, moving = [value], value
    for _ in range(size - 1):
        moving = lax.ppermute(moving, "relay", [(i, (i + 1) % size) for i in range(size)])
        values.append(moving)
    return jnp.concatenate(values, axis=0)


def shards(target, frag_brick, bead_cell, bead_weight, bead_arm, frag_angle):
    brick_count, relay_count = lax.axis_size("brick"), lax.axis_size("relay")
    frags, beads = bead_cell.shape
    planes, columns, rows = target.shape
    lines = planes * columns
    his = lines * (rows // LO)
    assert rows % LO == 0 and his <= 256 and columns >= 2 * KR
    assert beads == 128 and lines & (lines - 1) == 0
    voxel_total = float(brick_count * columns * relay_count * planes * rows)
    most = max(2, 2 * frags // brick_count)
    slots = brick_count * most
    assert most * FIELDS <= 128

    z_total, x_total = relay_count * planes, brick_count * columns
    gz, dz = axis_matrix(z_total, False), axis_matrix(z_total, True)
    gx, dx = axis_matrix(x_total, False), axis_matrix(x_total, True)
    reach_one, reach_two = -(-KR // planes), -(-2 * KR // planes)
    target_table, tz, tx, tn = weight_table(
        [gz, gz, dz], [dx, gx, gx], planes, relay_count, relay_order(relay_count, reach_one),
        columns, brick_count,
        paired(np.arange(columns), np.arange(-KR, 0), np.arange(columns, columns + KR)),
    )
    model_table, mz, mx, mn = weight_table(
        [gz @ gz, gz @ gz, dz @ gz, gz], [dx @ gx, gx @ gx, gx @ gx, gx],
        planes, relay_count, relay_order(relay_count, reach_two), columns, brick_count,
        paired(np.arange(columns), np.arange(-columns, 0), np.arange(columns, 2 * columns)),
    )
    r, b = lax.axis_index("relay"), lax.axis_index("brick")
    target_index = (looked_up(tz, r) * tn + looked_up(tx, b)).reshape(1)
    model_index = (looked_up(mz, r) * mn + looked_up(mx, b)).reshape(1)

    target_lines = target.reshape(lines, rows)
    words = jax.ShapeDtypeStruct((lines // 2, rows + SCALE_LANES), I32)
    hbm = pl.BlockSpec(memory_space=pltpu.HBM)
    packed = [frag_brick.reshape(1, frags), frag_angle, bead_cell, bead_weight, bead_arm]
    packed += [target_lines]
    sent, place, target_code = call(
        functools.partial(pack_kernel, most, lines, rows),
        [
            jax.ShapeDtypeStruct((slots, 3 * beads), I32),
            jax.ShapeDtypeStruct((8, frags), I32),
            words,
        ],
        *packed,
        in_specs=[hbm] * len(packed),
        scratch=[pltpu.VMEM(a.shape, a.dtype) for a in packed]
        + [pltpu.SemaphoreType.DMA((len(packed),))],
        name="pack",
        vmem=PACK_VMEM_BYTES,
    )
    target_blocks = relay_blocks(target_code, reach_one)
    by_column = [t.reshape(-1, columns, rows + SCALE_LANES) for t in target_blocks]
    left_edge = jnp.concatenate([t[:, columns - KR :] for t in by_column], axis=0)
    right_edge = jnp.concatenate([t[:, :KR] for t in by_column], axis=0)
    first_edge = jnp.where(b % 2 == 0, left_edge, right_edge)
    second_edge = jnp.where(b % 2 == 0, right_edge, left_edge)
    target_near = swapped(
        first_edge.reshape(-1, rows + SCALE_LANES), second_edge.reshape(-1, rows + SCALE_LANES)
    )

    got = lax.all_to_all(sent, "brick", split_axis=0, concat_axis=0, tiled=True)
    smooth, coded = call(
        functools.partial(splat_kernel, lines, min(64, slots)),
        [jax.ShapeDtypeStruct((lines, rows), F32), words],
        got,
        scratch=[pltpu.VMEM((his, LO), F32)],
        name="splat",
        macs=slots * beads * his * LO,
    )
    coded, *target_near = lax.optimization_barrier((coded, *target_near))
    target_parts = [target_lines] + target_blocks[1:] + target_near
    blocks = relay_blocks(coded, reach_two)
    field_shapes = [
        jax.ShapeDtypeStruct((3 * his, 2 * LO), BF16),
        jax.ShapeDtypeStruct((3 * lines, rows), F32),
    ]
    target_field = call_at(
        functools.partial(target_kernel, lines),
        field_shapes,
        target_index, jnp.asarray(target_table), *target_parts,
        name="target_fields",
        macs=9 * lines * rows * 128,
    )

    def sample(field, start, count, name):
        rb = min(32, count)
        return call(
            functools.partial(sample_kernel, lines, his, rb, rb * 5 // 16, start),
            jax.ShapeDtypeStruct((count, 128), F32),
            got, *field,
            scratch=[pltpu.VMEM((3, count, beads), F32)],
            name=name,
            macs=6 * count * beads * his * LO,
        )

    part = slots // 4
    target_first = sample(target_field, 0, part, "target_sample_a")
    blocks, target_first, target_field = lax.optimization_barrier(
        (blocks, target_first, target_field)
    )
    beside = jnp.concatenate(blocks, axis=0)
    model_parts = [smooth] + blocks[1:]
    model_parts += swapped(beside, beside)
    target_second = sample(target_field, part, slots - part, "target_sample_b")
    target_second, *model_parts = lax.optimization_barrier((target_second, *model_parts))
    *model_field, partial = call_at(
        functools.partial(model_kernel, lines),
        field_shapes + [jax.ShapeDtypeStruct((8, 128), F32)],
        model_index, jnp.asarray(model_table), target_lines, *model_parts,
        name="model_fields",
    )
    partials = relay_total(partial)
    model_sums = sample(model_field, 0, slots, "model_sample")
    leaving = call(
        functools.partial(join_kernel, most),
        jax.ShapeDtypeStruct((brick_count, 128), F32),
        target_first, target_second, model_sums, partials,
        name="join",
    )
    back = lax.all_to_all(leaving, "brick", split_axis=0, concat_axis=0, tiled=True)
    return call(
        functools.partial(finish_kernel, most, voxel_total),
        jax.ShapeDtypeStruct((6, frags), F32),
        place, back,
        name="finish",
    )


def solution(mesh):
    placed = (
        P("relay", "brick", None),
        P(("brick", "relay"), None),
        P(("brick", "relay"), None),
        P(("brick", "relay"), None),
        P(None, ("brick", "relay"), None),
        P(None, ("brick", "relay")),
    )
    return jax.shard_map(
        shards, mesh=mesh, in_specs=placed, out_specs=P(None, ("brick", "relay")), check_vma=False
    )
```

```python
import functools

import jax
import jax.numpy as jnp
import numpy as np
from jax import lax
from jax.experimental import pallas as pl
from jax.experimental.pallas import tpu as pltpu
from jax.sharding import PartitionSpec as P

KR = 4
SIGMA = 1.5
EPSILON = 1e-06
HIGHEST = lax.Precision.HIGHEST
LO = 256
FIELDS = 16
WEIGHT_SCALE = 512.0
LEVER_SCALE = 32768.0
LEVER_BIAS = 1 << 20
CODE_TOP = 65535
SCALE_UNIT = 512.0
SCALE_LANES = 128
VMEM_BYTES = 48 << 20
PACK_VMEM_BYTES = 60 << 20
F32 = jnp.float32
BF16 = jnp.bfloat16
I32 = jnp.int32


def taps_of(derivative):
    offsets = np.arange(-KR, KR + 1) * 1.0
    gaussian = np.exp(-(offsets**2) / (2.0 * SIGMA**2))
    gaussian = gaussian / gaussian.sum()
    if derivative:
        return -offsets / SIGMA**2 * gaussian
    return gaussian


def axis_matrix(length, derivative):
    offsets = np.arange(length)[:, None] - np.arange(length)[None, :]
    return np.where(
        np.abs(offsets) <= KR, taps_of(derivative)[np.clip(offsets + KR, 0, 2 * KR)], 0.0
    )


def columns_at(matrix, rows, wanted):
    inside = (wanted >= 0) & (wanted < matrix.shape[1])
    picked = matrix[rows][:, np.clip(wanted, 0, matrix.shape[1] - 1)]
    return np.where(inside[None, :], picked, 0.0)


def unique_tables(tables):
    flat = np.stack([t.reshape(-1) for t in tables])
    kept, inverse = np.unique(np.round(flat, 14), axis=0, return_inverse=True)
    return kept.reshape((-1,) + tables[0].shape), inverse.reshape(-1).astype(np.int32)


def pieces_np(table):
    import ml_dtypes

    high = table.astype(np.float32).astype(ml_dtypes.bfloat16)
    low = (table - high.astype(np.float64)).astype(ml_dtypes.bfloat16)
    return np.concatenate([high, high, low], axis=-1)


def weight_table(
    z_kinds, x_kinds, z_rows, z_len, z_count, z_blocks, x_len, x_count, x_parts
):
    z_tables = []
    for r in range(z_count):
        wanted = np.concatenate([np.arange(z_len) + z_len * block for block in z_blocks(r)])
        rows = [np.arange(z_len) + z_len * block for block in z_rows(r)]
        z_tables.append(np.stack([columns_at(m, i, wanted) for m, i in zip(z_kinds, rows)]))
    x_tables = []
    for b in range(x_count):
        wanted = np.concatenate([x_len * b + part for part in x_parts(b)])
        rows = np.arange(x_len) + x_len * b
        x_tables.append(np.stack([columns_at(m, rows, wanted) for m in x_kinds]))
    z_tables, z_inverse = unique_tables(z_tables)
    x_tables, x_inverse = unique_tables(x_tables)
    kinds = len(z_kinds)
    parts, start = [], 0
    for part in x_parts(0):
        piece = x_tables[:, :, :, start : start + len(part)]
        start += len(part)
        full = np.einsum("rkzi,bkxj->rbkzxij", z_tables, piece)
        parts.append(
            full.reshape(len(z_tables) * len(x_tables), kinds * z_len * x_len, -1)
        )
    table = pieces_np(np.concatenate(parts, axis=-1))
    return table, z_inverse, x_inverse, len(x_tables)


def eye_column(row, eye):
    return jnp.sum(jnp.where(eye, row, jnp.zeros_like(row)), axis=1, keepdims=True)


def slot_row(row, most):
    frags = row.shape[1]
    sub = lax.broadcasted_iota(I32, (frags, frags), 0)
    lane = lax.broadcasted_iota(I32, (frags, frags), 1)
    eye = sub == lane
    earlier = jnp.logical_and(eye_column(row, eye) == row, sub < lane)
    return jnp.sum(jnp.where(earlier, 1, 0), axis=0, keepdims=True), eye


def pack_kernel(most, lines, row_count, *refs):
    inputs, (out_ref, place_ref, code_ref) = refs[:6], refs[6:9]
    held, sems = refs[9:15], refs[15]
    copies = [
        pltpu.make_async_copy(source, target, sems.at[k])
        for k, (source, target) in enumerate(zip(inputs, held))
    ]
    for copy in copies:
        copy.start()
    brick_ref, angle_ref, cell_ref, weight_ref, arm_ref, target_ref = held
    for copy in copies[:2]:
        copy.wait()
    frags, beads = cell_ref.shape
    slots = out_ref.shape[0]
    row = brick_ref[...]
    rank, eye = slot_row(row, most)
    slot = row * most + rank
    place = jnp.where(lax.broadcasted_iota(I32, (slots, frags), 0) == slot, 1.0, 0.0).astype(F32)

    angles = angle_ref[...]
    cos, sin = jnp.cos(angles), jnp.sin(angles)
    cos_a, cos_b, cos_c = cos[0:1], cos[1:2], cos[2:3]
    sin_a, sin_b, sin_c = sin[0:1], sin[1:2], sin[2:3]
    turn = [
        [cos_a * cos_b, cos_a * sin_b * sin_c - sin_a * cos_c, cos_a * sin_b * cos_c + sin_a * sin_c],
        [sin_a * cos_b, sin_a * sin_b * sin_c + cos_a * cos_c, sin_a * sin_b * cos_c - cos_a * sin_c],
        [-sin_b, cos_b * sin_c, cos_b * cos_c],
    ]
    turn = [[eye_column(value, eye) for value in values] for values in turn]
    place_ref[0:1, :] = row
    place_ref[1:2, :] = rank
    for copy in copies[2:]:
        copy.wait()
    encode(target_ref[...], code_ref)
    levers = []
    for i in range(3):
        total = turn[i][0] * arm_ref[0]
        for j in (1, 2):
            total = total + turn[i][j] * arm_ref[j]
        levers.append(jnp.round(total * LEVER_SCALE))

    cell = cell_ref[...]
    line = ((cell.astype(F32) + 0.5) * (1.0 / row_count)).astype(I32)
    y = cell - line * row_count
    code = (((y // LO) * lines + line) * LO + (y % LO)).astype(F32)
    weight = weight_ref[...].astype(F32) * WEIGHT_SCALE
    payload = jnp.concatenate([code, weight] + levers, axis=1)
    placed = jnp.dot(place, payload, precision=HIGHEST, preferred_element_type=F32)
    placed = placed.astype(I32)
    code, weight, lx, ly, lz = [placed[:, k * beads : (k + 1) * beads] for k in range(5)]
    lz = lz + LEVER_BIAS
    out_ref[:, 0:beads] = code | (weight << 16)
    out_ref[:, beads : 2 * beads] = (lx << 11) | (lz >> 10)
    out_ref[:, 2 * beads : 3 * beads] = (ly << 11) | (lz & 1023)


def line_blur(value, derivative):
    taps = taps_of(derivative)
    rows, length = value.shape
    wide = jnp.concatenate([value, jnp.zeros((rows, 128), F32)], axis=1)
    total = None if derivative else float(taps[KR]) * value
    for d in range(1, KR + 1):
        up = pltpu.roll(wide, d, 1)[:, :length]
        down = pltpu.roll(wide, length + 128 - d, 1)[:, :length]
        pair = up - down if derivative else up + down
        term = float(taps[KR + d]) * pair
        total = term if total is None else total + term
    return total


def encode(value, out_ref):
    half, length = value.shape[0] // 2, value.shape[1]
    top = (jnp.max(value) * SCALE_UNIT).astype(I32) + 1
    scale = (SCALE_UNIT * CODE_TOP) / top.astype(F32)
    code = jnp.minimum((value * scale + 0.5).astype(I32), CODE_TOP)
    out_ref[:, :length] = code[:half] | (code[half:] << 16)
    out_ref[:, length:] = jnp.full((half, SCALE_LANES), top, I32)


def decode(words, count):
    half, length = words.shape[0] // count, words.shape[1] - SCALE_LANES
    step = words[:, length : length + 1].astype(F32) * (1.0 / (SCALE_UNIT * CODE_TOP))
    low = (words[:, :length] & CODE_TOP).astype(F32) * step
    high = ((words[:, :length] >> 16) & CODE_TOP).astype(F32) * step
    lines = []
    for k in range(count):
        rows = slice(k * half, (k + 1) * half)
        lines += [low[rows], high[rows]]
    return lines


def splat_kernel(lines, rb, got_ref, out_ref, code_ref, acc_ref):
    slots = got_ref.shape[0]
    beads = got_ref.shape[1] // 3
    his = acc_ref.shape[0]
    acc_ref[...] = jnp.zeros_like(acc_ref)
    hi_iota = lax.broadcasted_iota(I32, (his, beads), 0)
    lo_iota = lax.broadcasted_iota(I32, (LO, beads), 0)

    def body(i, carry):
        word = got_ref[pl.ds(i * rb, rb), 0:beads]
        lo = word & (LO - 1)
        hi = (word >> 8) & 255
        weight = (word >> 16).astype(F32) * (1.0 / WEIGHT_SCALE)
        left, right = [], []
        for q in range(rb):
            left.append(jnp.where(hi_iota == hi[q : q + 1], weight[q : q + 1], 0.0).astype(BF16))
            right.append(jnp.where(lo_iota == lo[q : q + 1], 1.0, 0.0).astype(BF16))
        acc_ref[...] += lax.dot_general(
            jnp.concatenate(left, axis=1),
            jnp.concatenate(right, axis=1),
            (((1,), (1,)), ((), ())),
            preferred_element_type=F32,
        )
        return carry

    lax.fori_loop(0, slots // rb, body, 0)
    density = [acc_ref[yh * lines : (yh + 1) * lines, :] for yh in range(his // lines)]
    smooth = line_blur(jnp.concatenate(density, axis=1), False)
    out_ref[...] = smooth
    encode(smooth, code_ref)


def split(value):
    high = value.astype(BF16)
    low = (value - high.astype(F32)).astype(BF16)
    return high, low


def mix_lines(index_ref, tables_ref, parts):
    value = jnp.concatenate(parts, axis=0)
    high, low = split(value)
    return jnp.dot(
        tables_ref[index_ref[0]], jnp.concatenate([high, low, high], axis=0), preferred_element_type=F32
    )


def store_fields(fields, lines, out_ref, exact_ref):
    his = fields[0].shape[1] // LO * lines
    for k, field in enumerate(fields):
        exact_ref[k * lines : (k + 1) * lines, :] = field
        for yh in range(field.shape[1] // LO):
            high, low = split(field[:, yh * LO : (yh + 1) * LO])
            rows = slice(k * his + yh * lines, k * his + (yh + 1) * lines)
            out_ref[rows, 0:LO] = high
            out_ref[rows, LO : 2 * LO] = low


def window_lines(own_ref, near_refs, first_ref, second_ref):
    lines = [own_ref[...]]
    for ref in near_refs:
        lines += decode(ref[...], 1)
    for ref in (first_ref, second_ref):
        lines += decode(ref[...], len(near_refs) + 1)
    return lines


def target_kernel(lines, index_ref, tables_ref, own_ref, *refs):
    *near_refs, first_ref, second_ref, out_ref, exact_ref = refs
    window = window_lines(own_ref, near_refs, first_ref, second_ref)
    mixed = mix_lines(index_ref, tables_ref, window)
    grad_x = line_blur(mixed[0:lines], False)
    grad_y = line_blur(mixed[lines : 2 * lines], True)
    grad_z = line_blur(mixed[2 * lines : 3 * lines], False)
    store_fields([grad_x, grad_y, grad_z], lines, out_ref, exact_ref)


def model_kernel(lines, near, index_ref, tables_ref, target_ref, *refs):
    target = [target_ref[...]]
    for ref in refs[: near - 1]:
        target += decode(ref[...], 1)
    target = jnp.concatenate(target, axis=0)
    own_ref, *near_refs, first_ref, second_ref, out_ref, exact_ref, sum_ref = refs[near - 1 :]
    window = window_lines(own_ref, near_refs, first_ref, second_ref)
    smooth = mix_lines(index_ref, tables_ref, window)
    model = smooth[3 * lines :]
    sums = [jnp.sum(model * target), jnp.sum(model * model), jnp.sum(target * target)]
    lane = lax.broadcasted_iota(I32, sum_ref.shape, 1)
    total = jnp.zeros(sum_ref.shape, F32)
    for k, value in enumerate(sums):
        total = jnp.where(lane == k, value, total)
    sum_ref[...] = total
    grad_x = line_blur(smooth[0:lines], False)
    grad_y = line_blur(smooth[lines : 2 * lines], True)
    grad_z = line_blur(smooth[2 * lines : 3 * lines], False)
    store_fields([grad_x, grad_y, grad_z], lines, out_ref, exact_ref)


def sample_by_matmul(word, field_ref, his, store):
    count, beads = word.shape
    lo, hi = word & (LO - 1), (word >> 8) & 255
    lo_iota = lax.broadcasted_iota(I32, (LO, beads), 0)
    picks = [jnp.where(lo_iota == lo[q : q + 1], 1.0, 0.0).astype(BF16) for q in range(count)]
    pick = jnp.concatenate(picks, axis=1)
    sampled = jnp.dot(
        field_ref[...], jnp.concatenate([pick, pick], axis=0), preferred_element_type=F32
    )

    def finish():
        sub_iota = lax.broadcasted_iota(I32, (8, beads), 0)
        for q in range(count):
            own = jnp.broadcast_to(hi[q : q + 1], (8, beads))
            group, within = own >> 3, (own & 7) == sub_iota
            found = [jnp.zeros((8, beads), F32)] * 3
            for j in range(his // 8):
                here = group == j
                for k in range(3):
                    rows = slice(k * his + 8 * j, k * his + 8 * j + 8)
                    part = sampled[rows, q * beads : (q + 1) * beads]
                    found[k] = jnp.where(here, part, found[k])
            store(q, [jnp.sum(jnp.where(within, v, 0.0), axis=0, keepdims=True) for v in found])

    return finish


def sample_by_lanes(word, exact_ref, lines, store):
    count, beads = word.shape
    tiles = exact_ref.shape[1] // 128
    line_shift, lo_shift = lines.bit_length() - 1, LO.bit_length() - 1
    sub_iota = lax.broadcasted_iota(I32, (8, beads), 0)
    for q in range(count):
        own = jnp.broadcast_to(word[q : q + 1], (8, beads))
        lo, hi = own & (LO - 1), (own >> lo_shift) & 255
        line = hi & (lines - 1)
        group = (line >> 3) * tiles + (hi >> line_shift) * (LO // 128) + (lo >> 7)
        within, lane = (line & 7) == sub_iota, lo & 127
        found = [jnp.zeros((8, beads), F32)] * 3
        for j in range(lines // 8 * tiles):
            here = group == j
            first, tile = j // tiles * 8, j % tiles * 128
            for k in range(3):
                table = exact_ref[k * lines + first : k * lines + first + 8, tile : tile + 128]
                part = jnp.take_along_axis(table, lane, axis=1, mode="promise_in_bounds")
                found[k] = jnp.where(here, part, found[k])
        store(q, [jnp.sum(jnp.where(within, v, 0.0), axis=0, keepdims=True) for v in found])


def sample_kernel(
    lines, his, rb, by_lanes, start, got_ref, field_ref, exact_ref, out_ref, force_ref
):
    slots = out_ref.shape[0]
    beads = got_ref.shape[1] // 3
    by_matmul = rb - by_lanes

    def body(i, carry):
        def store_from(first):
            def store(q, values):
                for k in range(3):
                    force_ref[k, pl.ds(i * rb + first + q, 1), :] = values[k]

            return store

        word = got_ref[pl.ds(start + i * rb, rb), 0:beads]
        finish = sample_by_matmul(word[:by_matmul], field_ref, his, store_from(0))
        sample_by_lanes(word[by_matmul:], exact_ref, lines, store_from(by_matmul))
        finish()
        return carry

    lax.fori_loop(0, slots // rb, body, 0)
    rows = slice(start, start + slots)
    first, second = got_ref[rows, beads : 2 * beads], got_ref[rows, 2 * beads : 3 * beads]
    weight = (got_ref[rows, 0:beads] >> 16).astype(F32) * (1.0 / WEIGHT_SCALE)
    lever_z = (((first & 2047) << 10) | (second & 1023)) - LEVER_BIAS
    levers = [
        v.astype(F32) * (1.0 / LEVER_SCALE) for v in (first >> 11, second >> 11, lever_z)
    ]
    force = [force_ref[k] * weight for k in range(3)]
    terms = force + [
        levers[1] * force[2] - levers[2] * force[1],
        levers[2] * force[0] - levers[0] * force[2],
        levers[0] * force[1] - levers[1] * force[0],
    ]
    lane = lax.broadcasted_iota(I32, out_ref.shape, 1)
    total = jnp.zeros(out_ref.shape, F32)
    for k, term in enumerate(terms):
        total = jnp.where(lane == k, jnp.sum(term, axis=1, keepdims=True), total)
    out_ref[...] = total


def join_kernel(most, *refs):
    *target_refs, model_ref, sum_ref, out_ref = refs
    bricks = out_ref.shape[0]
    lane = lax.broadcasted_iota(I32, out_ref.shape, 1)
    sums = sum_ref[0:1, :]
    for k in range(1, sum_ref.shape[0] // 8):
        sums = sums + sum_ref[8 * k : 8 * k + 1, :]
    total = jnp.zeros(out_ref.shape, F32)
    for k in range(most):
        rows = pl.ds(k, bricks, stride=most)
        parts = [ref[pl.ds(k, ref.shape[0] // most, stride=most), :] for ref in target_refs]
        own = jnp.concatenate(parts, axis=0)
        own = jnp.where(lane < 6, own, 0.0)
        own = own + pltpu.roll(jnp.where(lane < 6, model_ref[rows, :], 0.0), 6, 1)
        if k == 0:
            own = own + pltpu.roll(jnp.where(lane < 3, sums, 0.0), 12, 1)
        total = total + (pltpu.roll(own, FIELDS * k, 1) if k else own)
    out_ref[...] = total


def finish_kernel(most, voxel_total, place_ref, back_ref, out_ref):
    frags = out_ref.shape[1]
    bricks = back_ref.shape[0]
    row, rank = place_ref[0:1, :], place_ref[1:2, :]
    place = jnp.where(lax.broadcasted_iota(I32, (bricks, frags), 0) == row, 1.0, 0.0).astype(F32)
    back = back_ref[...]
    sums = jnp.sum(back, axis=0, keepdims=True)
    cross, model_sq, target_sq = sums[:, 12:13], sums[:, 13:14], sums[:, 14:15]
    norm_model = jnp.sqrt(model_sq + EPSILON)
    norm_target = jnp.sqrt(target_sq + EPSILON)
    corr = cross / (norm_model * norm_target)
    scale_target = voxel_total / (norm_model * norm_target)
    scale_model = voxel_total * corr / (norm_model * norm_model)
    found = lax.dot_general(
        back, place, (((0,), (0,)), ((), ())), precision=HIGHEST, preferred_element_type=F32
    )
    mine = jnp.zeros((FIELDS, frags), F32)
    for k in range(most):
        mine = jnp.where(rank == k, found[FIELDS * k : FIELDS * (k + 1)], mine)
    out_ref[...] = scale_target * mine[0:6] - scale_model * mine[6:12]


def cost(macs, nbytes):
    return pl.CostEstimate(flops=2 * macs, bytes_accessed=nbytes, transcendentals=0)


def call(
    kernel, out_shape, *args, scratch=(), name=None, macs=0, in_specs=None, vmem=VMEM_BYTES
):
    kwargs = {} if in_specs is None else {"in_specs": in_specs}
    return pl.pallas_call(
        kernel,
        out_shape=out_shape,
        scratch_shapes=list(scratch),
        compiler_params=pltpu.CompilerParams(vmem_limit_bytes=vmem),
        cost_estimate=cost(macs, 4 * sum(a.size for a in args)),
        name=name,
        **kwargs,
    )(*args)


def call_at(kernel, out_shape, index, table, *args, name=None, macs=0):
    vmem = pl.BlockSpec(memory_space=pltpu.VMEM)
    return call(
        kernel,
        out_shape,
        index, table, *args,
        in_specs=[pl.BlockSpec(memory_space=pltpu.SMEM)] + [vmem] * (1 + len(args)),
        name=name,
        macs=macs,
    )


def looked_up(values, position):
    found = jnp.full((), int(values[0]), I32)
    for i in range(1, len(values)):
        step = int(values[i]) - int(values[i - 1])
        if step:
            found = found + step * (position >= i).astype(I32)
    return found


def shifted(value, axis, step):
    size = lax.axis_size(axis)
    pairs = [(i, i + step) for i in range(size) if 0 <= i + step < size]
    return lax.ppermute(value, axis, pairs)


def paired(own, left, right):
    return lambda b: [own, right, left] if b % 2 == 0 else [own, left, right]


def swapped(first, second):
    size = lax.axis_size("brick")
    found = []
    for value, start in ((first, 0), (second, 1)):
        pairs = [(i, i + 1) for i in range(start, size - 1, 2)]
        found.append(lax.ppermute(value, "brick", pairs + [(j, i) for i, j in pairs]))
    return found


def relay_blocks(value, reach):
    size = lax.axis_size("relay")
    if size == 2:
        return [value, lax.ppermute(value, "relay", [(0, 1), (1, 0)])]
    blocks = [value]
    for step in range(1, min(reach, size - 1) + 1):
        blocks += [shifted(value, "relay", step), shifted(value, "relay", -step)]
    return blocks


def relay_order(size, reach):
    if size == 2:
        return lambda r: [r, 1 - r]
    steps = [0]
    for step in range(1, min(reach, size - 1) + 1):
        steps += [-step, step]
    return lambda r: [r + s for s in steps]


def relay_total(value):
    size = lax.axis_size("relay")
    values, moving = [value], value
    for _ in range(size - 1):
        moving = lax.ppermute(moving, "relay", [(i, (i + 1) % size) for i in range(size)])
        values.append(moving)
    return jnp.concatenate(values, axis=0)


def shards(target, frag_brick, bead_cell, bead_weight, bead_arm, frag_angle):
    brick_count, relay_count = lax.axis_size("brick"), lax.axis_size("relay")
    frags, beads = bead_cell.shape
    planes, columns, rows = target.shape
    lines = planes * columns
    his = lines * (rows // LO)
    assert rows % LO == 0 and his <= 256 and columns >= 2 * KR
    assert beads == 128 and lines & (lines - 1) == 0
    voxel_total = float(brick_count * columns * relay_count * planes * rows)
    most = max(2, 2 * frags // brick_count)
    slots = brick_count * most
    assert most * FIELDS <= 128

    z_total, x_total = relay_count * planes, brick_count * columns
    gz, dz = axis_matrix(z_total, False), axis_matrix(z_total, True)
    gx, dx = axis_matrix(x_total, False), axis_matrix(x_total, True)
    near = 2 if relay_count == 2 else 1
    reach_one, reach_two = -(-KR // planes), -(-2 * KR // planes)
    target_table, tz, tx, tn = weight_table(
        [gz, gz, dz], [dx, gx, gx], lambda r: [r] * 3, planes, relay_count, relay_order(relay_count, reach_one),
        columns, brick_count,
        paired(np.arange(columns), np.arange(-KR, 0), np.arange(columns, columns + KR)),
    )
    model_table, mz, mx, mn = weight_table(
        [gz @ gz, gz @ gz, dz @ gz] + [gz] * near, [dx @ gx, gx @ gx, gx @ gx] + [gx] * near,
        lambda r: [r] * 4 + [1 - r] * (near - 1),
        planes, relay_count, relay_order(relay_count, reach_two), columns, brick_count,
        paired(np.arange(columns), np.arange(-columns, 0), np.arange(columns, 2 * columns)),
    )
    r, b = lax.axis_index("relay"), lax.axis_index("brick")
    target_index = (looked_up(tz, r) * tn + looked_up(tx, b)).reshape(1)
    model_index = (looked_up(mz, r) * mn + looked_up(mx, b)).reshape(1)

    target_lines = target.reshape(lines, rows)
    words = jax.ShapeDtypeStruct((lines // 2, rows + SCALE_LANES), I32)
    hbm = pl.BlockSpec(memory_space=pltpu.HBM)
    packed = [frag_brick.reshape(1, frags), frag_angle, bead_cell, bead_weight, bead_arm]
    packed += [target_lines]
    sent, place, target_code = call(
        functools.partial(pack_kernel, most, lines, rows),
        [
            jax.ShapeDtypeStruct((slots, 3 * beads), I32),
            jax.ShapeDtypeStruct((8, frags), I32),
            words,
        ],
        *packed,
        in_specs=[hbm] * len(packed),
        scratch=[pltpu.VMEM(a.shape, a.dtype) for a in packed]
        + [pltpu.SemaphoreType.DMA((len(packed),))],
        name="pack",
        vmem=PACK_VMEM_BYTES,
    )
    target_blocks = relay_blocks(target_code, reach_one)
    by_column = [t.reshape(-1, columns, rows + SCALE_LANES) for t in target_blocks]
    left_edge = jnp.concatenate([t[:, columns - KR :] for t in by_column], axis=0)
    right_edge = jnp.concatenate([t[:, :KR] for t in by_column], axis=0)
    first_edge = jnp.where(b % 2 == 0, left_edge, right_edge)
    second_edge = jnp.where(b % 2 == 0, right_edge, left_edge)
    target_near = swapped(
        first_edge.reshape(-1, rows + SCALE_LANES), second_edge.reshape(-1, rows + SCALE_LANES)
    )

    got = lax.all_to_all(sent, "brick", split_axis=0, concat_axis=0, tiled=True)
    smooth, coded = call(
        functools.partial(splat_kernel, lines, min(64, slots)),
        [jax.ShapeDtypeStruct((lines, rows), F32), words],
        got,
        scratch=[pltpu.VMEM((his, LO), F32)],
        name="splat",
        macs=slots * beads * his * LO,
    )
    coded, *target_near = lax.optimization_barrier((coded, *target_near))
    target_parts = [target_lines] + target_blocks[1:] + target_near
    blocks = relay_blocks(coded, reach_two)
    field_shapes = [
        jax.ShapeDtypeStruct((3 * his, 2 * LO), BF16),
        jax.ShapeDtypeStruct((3 * lines, rows), F32),
    ]
    target_field = call_at(
        functools.partial(target_kernel, lines),
        field_shapes,
        target_index, jnp.asarray(target_table), *target_parts,
        name="target_fields",
        macs=9 * lines * rows * 128,
    )

    def sample(field, start, count, name):
        rb = min(32, count)
        return call(
            functools.partial(sample_kernel, lines, his, rb, rb * 5 // 16, start),
            jax.ShapeDtypeStruct((count, 128), F32),
            got, *field,
            scratch=[pltpu.VMEM((3, count, beads), F32)],
            name=name,
            macs=6 * count * beads * his * LO,
        )

    part = slots // 4
    target_first = sample(target_field, 0, part, "target_sample_a")
    blocks, target_first, target_field = lax.optimization_barrier(
        (blocks, target_first, target_field)
    )
    beside = jnp.concatenate(blocks, axis=0)
    model_parts = [smooth] + blocks[1:]
    model_parts += swapped(beside, beside)
    target_second = sample(target_field, part, slots - part, "target_sample_b")
    target_second, *model_parts = lax.optimization_barrier((target_second, *model_parts))
    *model_field, partial = call_at(
        functools.partial(model_kernel, lines, near),
        field_shapes + [jax.ShapeDtypeStruct((8, 128), F32)],
        model_index, jnp.asarray(model_table), target_lines, *target_blocks[1:near], *model_parts,
        name="model_fields",
    )
    partials = partial if near == relay_count else relay_total(partial)
    model_sums = sample(model_field, 0, slots, "model_sample")
    leaving = call(
        functools.partial(join_kernel, most),
        jax.ShapeDtypeStruct((brick_count, 128), F32),
        target_first, target_second, model_sums, partials,
        name="join",
    )
    back = lax.all_to_all(leaving, "brick", split_axis=0, concat_axis=0, tiled=True)
    return call(
        functools.partial(finish_kernel, most, voxel_total),
        jax.ShapeDtypeStruct((6, frags), F32),
        place, back,
        name="finish",
    )


def solution(mesh):
    placed = (
        P("relay", "brick", None),
        P(("brick", "relay"), None),
        P(("brick", "relay"), None),
        P(("brick", "relay"), None),
        P(None, ("brick", "relay"), None),
        P(None, ("brick", "relay")),
    )
    return jax.shard_map(
        shards, mesh=mesh, in_specs=placed, out_specs=P(None, ("brick", "relay")), check_vma=False
    )
```

```python
import functools

import jax
import jax.numpy as jnp
import numpy as np
from jax import lax
from jax.experimental import pallas as pl
from jax.experimental.pallas import tpu as pltpu
from jax.sharding import PartitionSpec as P

KR = 4
SIGMA = 1.5
EPSILON = 1e-06
HIGHEST = lax.Precision.HIGHEST
LO = 256
BY_LANES = 14
FIELDS = 16
WEIGHT_SCALE = 512.0
LEVER_SCALE = 32768.0
LEVER_BIAS = 1 << 20
FIELD_TOP = 1048575.0
TINY = 1e-30
CODE_TOP = 65535
SCALE_UNIT = 512.0
SCALE_LANES = 128
VMEM_BYTES = 48 << 20
PACK_VMEM_BYTES = 60 << 20
F32 = jnp.float32
BF16 = jnp.bfloat16
I32 = jnp.int32


def taps_of(derivative):
    offsets = np.arange(-KR, KR + 1) * 1.0
    gaussian = np.exp(-(offsets**2) / (2.0 * SIGMA**2))
    gaussian = gaussian / gaussian.sum()
    if derivative:
        return -offsets / SIGMA**2 * gaussian
    return gaussian


def axis_matrix(length, derivative):
    offsets = np.arange(length)[:, None] - np.arange(length)[None, :]
    return np.where(
        np.abs(offsets) <= KR, taps_of(derivative)[np.clip(offsets + KR, 0, 2 * KR)], 0.0
    )


def columns_at(matrix, rows, wanted):
    inside = (wanted >= 0) & (wanted < matrix.shape[1])
    picked = matrix[rows][:, np.clip(wanted, 0, matrix.shape[1] - 1)]
    return np.where(inside[None, :], picked, 0.0)


def unique_tables(tables):
    flat = np.stack([t.reshape(-1) for t in tables])
    kept, inverse = np.unique(np.round(flat, 14), axis=0, return_inverse=True)
    return kept.reshape((-1,) + tables[0].shape), inverse.reshape(-1).astype(np.int32)


def pieces_np(table):
    import ml_dtypes

    high = table.astype(np.float32).astype(ml_dtypes.bfloat16)
    low = (table - high.astype(np.float64)).astype(ml_dtypes.bfloat16)
    return np.concatenate([high, high, low], axis=-1)


def weight_table(
    z_kinds, x_kinds, z_rows, z_len, z_count, z_blocks, x_len, x_count, x_parts
):
    z_tables = []
    for r in range(z_count):
        wanted = np.concatenate([np.arange(z_len) + z_len * block for block in z_blocks(r)])
        rows = [np.arange(z_len) + z_len * block for block in z_rows(r)]
        z_tables.append(np.stack([columns_at(m, i, wanted) for m, i in zip(z_kinds, rows)]))
    x_tables = []
    for b in range(x_count):
        wanted = np.concatenate([x_len * b + part for part in x_parts(b)])
        rows = np.arange(x_len) + x_len * b
        x_tables.append(np.stack([columns_at(m, rows, wanted) for m in x_kinds]))
    z_tables, z_inverse = unique_tables(z_tables)
    x_tables, x_inverse = unique_tables(x_tables)
    kinds = len(z_kinds)
    parts, start = [], 0
    for part in x_parts(0):
        piece = x_tables[:, :, :, start : start + len(part)]
        start += len(part)
        full = np.einsum("rkzi,bkxj->rbkzxij", z_tables, piece)
        parts.append(
            full.reshape(len(z_tables) * len(x_tables), kinds * z_len * x_len, -1)
        )
    table = pieces_np(np.concatenate(parts, axis=-1))
    return table, z_inverse, x_inverse, len(x_tables)


def eye_column(row, eye):
    return jnp.sum(jnp.where(eye, row, jnp.zeros_like(row)), axis=1, keepdims=True)


def slot_row(row, most):
    frags = row.shape[1]
    sub = lax.broadcasted_iota(I32, (frags, frags), 0)
    lane = lax.broadcasted_iota(I32, (frags, frags), 1)
    eye = sub == lane
    earlier = jnp.logical_and(eye_column(row, eye) == row, sub < lane)
    return jnp.sum(jnp.where(earlier, 1, 0), axis=0, keepdims=True), eye


def pack_kernel(most, lines, row_count, *refs):
    inputs, (out_ref, place_ref, code_ref) = refs[:6], refs[6:9]
    held, sems = refs[9:15], refs[15]
    copies = [
        pltpu.make_async_copy(source, target, sems.at[k])
        for k, (source, target) in enumerate(zip(inputs, held))
    ]
    for copy in copies:
        copy.start()
    brick_ref, angle_ref, cell_ref, weight_ref, arm_ref, target_ref = held
    for copy in copies[:2]:
        copy.wait()
    frags, beads = cell_ref.shape
    slots = out_ref.shape[0]
    row = brick_ref[...]
    rank, eye = slot_row(row, most)
    slot = row * most + rank
    place = jnp.where(lax.broadcasted_iota(I32, (slots, frags), 0) == slot, 1.0, 0.0).astype(F32)

    angles = angle_ref[...]
    cos, sin = jnp.cos(angles), jnp.sin(angles)
    cos_a, cos_b, cos_c = cos[0:1], cos[1:2], cos[2:3]
    sin_a, sin_b, sin_c = sin[0:1], sin[1:2], sin[2:3]
    turn = [
        [cos_a * cos_b, cos_a * sin_b * sin_c - sin_a * cos_c, cos_a * sin_b * cos_c + sin_a * sin_c],
        [sin_a * cos_b, sin_a * sin_b * sin_c + cos_a * cos_c, sin_a * sin_b * cos_c - cos_a * sin_c],
        [-sin_b, cos_b * sin_c, cos_b * cos_c],
    ]
    turn = [[eye_column(value, eye) for value in values] for values in turn]
    place_ref[0:1, :] = row
    place_ref[1:2, :] = rank
    for copy in copies[2:]:
        copy.wait()
    encode(target_ref[...], code_ref)
    levers = []
    for i in range(3):
        total = turn[i][0] * arm_ref[0]
        for j in (1, 2):
            total = total + turn[i][j] * arm_ref[j]
        levers.append(jnp.round(total * LEVER_SCALE))

    cell = cell_ref[...]
    line = ((cell.astype(F32) + 0.5) * (1.0 / row_count)).astype(I32)
    y = cell - line * row_count
    code = (((y // LO) * lines + line) * LO + (y % LO)).astype(F32)
    weight = weight_ref[...].astype(F32) * WEIGHT_SCALE
    payload = jnp.concatenate([code, weight] + levers, axis=1)
    placed = jnp.dot(place, payload, precision=HIGHEST, preferred_element_type=F32)
    placed = placed.astype(I32)
    code, weight, lx, ly, lz = [placed[:, k * beads : (k + 1) * beads] for k in range(5)]
    one, two = pack_three(lx, ly, lz)
    out_ref[:, 0:beads] = code | (weight << 16)
    out_ref[:, beads : 2 * beads] = one
    out_ref[:, 2 * beads : 3 * beads] = two


def line_blur(value, derivative):
    taps = taps_of(derivative)
    rows, length = value.shape
    wide = jnp.concatenate([value, jnp.zeros((rows, 128), F32)], axis=1)
    total = None if derivative else float(taps[KR]) * value
    for d in range(1, KR + 1):
        up = pltpu.roll(wide, d, 1)[:, :length]
        down = pltpu.roll(wide, length + 128 - d, 1)[:, :length]
        pair = up - down if derivative else up + down
        term = float(taps[KR + d]) * pair
        total = term if total is None else total + term
    return total


def encode(value, out_ref):
    half, length = value.shape[0] // 2, value.shape[1]
    top = (jnp.max(value) * SCALE_UNIT).astype(I32) + 1
    scale = (SCALE_UNIT * CODE_TOP) / top.astype(F32)
    code = jnp.minimum((value * scale + 0.5).astype(I32), CODE_TOP)
    out_ref[:, :length] = code[:half] | (code[half:] << 16)
    out_ref[:, length:] = jnp.full((half, SCALE_LANES), top, I32)


def decode(words, count):
    half, length = words.shape[0] // count, words.shape[1] - SCALE_LANES
    step = words[:, length : length + 1].astype(F32) * (1.0 / (SCALE_UNIT * CODE_TOP))
    low = (words[:, :length] & CODE_TOP).astype(F32) * step
    high = ((words[:, :length] >> 16) & CODE_TOP).astype(F32) * step
    lines = []
    for k in range(count):
        rows = slice(k * half, (k + 1) * half)
        lines += [low[rows], high[rows]]
    return lines


def splat_kernel(lines, rb, got_ref, out_ref, code_ref, acc_ref):
    slots = got_ref.shape[0]
    beads = got_ref.shape[1] // 3
    his = acc_ref.shape[0]
    acc_ref[...] = jnp.zeros_like(acc_ref)
    hi_iota = lax.broadcasted_iota(I32, (his, beads), 0)
    lo_iota = lax.broadcasted_iota(I32, (LO, beads), 0)

    def body(i, carry):
        word = got_ref[pl.ds(i * rb, rb), 0:beads]
        lo = word & (LO - 1)
        hi = (word >> 8) & 255
        weight = (word >> 16).astype(F32) * (1.0 / WEIGHT_SCALE)
        left, right = [], []
        for q in range(rb):
            left.append(jnp.where(hi_iota == hi[q : q + 1], weight[q : q + 1], 0.0).astype(BF16))
            right.append(jnp.where(lo_iota == lo[q : q + 1], 1.0, 0.0).astype(BF16))
        acc_ref[...] += lax.dot_general(
            jnp.concatenate(left, axis=1),
            jnp.concatenate(right, axis=1),
            (((1,), (1,)), ((), ())),
            preferred_element_type=F32,
        )
        return carry

    lax.fori_loop(0, slots // rb, body, 0)
    density = [acc_ref[yh * lines : (yh + 1) * lines, :] for yh in range(his // lines)]
    smooth = line_blur(jnp.concatenate(density, axis=1), False)
    out_ref[...] = smooth
    encode(smooth, code_ref)


def split(value):
    high = value.astype(BF16)
    low = (value - high.astype(F32)).astype(BF16)
    return high, low


def mix_lines(index_ref, tables_ref, parts):
    value = jnp.concatenate(parts, axis=0)
    high, low = split(value)
    return jnp.dot(
        tables_ref[index_ref[0]], jnp.concatenate([high, low, high], axis=0), preferred_element_type=F32
    )


def pack_three(first, second, third):
    third = third + LEVER_BIAS
    return (first << 11) | (third >> 10), (second << 11) | (third & 1023)


def unpack_three(one, two):
    return one >> 11, two >> 11, (((one & 2047) << 10) | (two & 1023)) - LEVER_BIAS


def store_fields(fields, lines, out_ref, word_ref, scale_ref):
    top = jnp.maximum(jnp.max(jnp.abs(jnp.concatenate(fields, axis=0))), TINY)
    scale_ref[...] = jnp.full(scale_ref.shape, top * (1.0 / FIELD_TOP), F32)
    up = FIELD_TOP / jnp.full((1, fields[0].shape[1]), top, F32)
    one, two = pack_three(*[jnp.round(field * up).astype(I32) for field in fields])
    word_ref[:lines, :] = one
    word_ref[lines:, :] = two
    his = fields[0].shape[1] // LO * lines
    for k, field in enumerate(fields):
        for yh in range(field.shape[1] // LO):
            high, low = split(field[:, yh * LO : (yh + 1) * LO])
            rows = slice(k * his + yh * lines, k * his + (yh + 1) * lines)
            out_ref[rows, 0:LO] = high
            out_ref[rows, LO : 2 * LO] = low


def window_lines(own_ref, near_refs, first_ref, second_ref):
    lines = [own_ref[...]]
    for ref in near_refs:
        lines += decode(ref[...], 1)
    for ref in (first_ref, second_ref):
        lines += decode(ref[...], len(near_refs) + 1)
    return lines


def target_kernel(lines, index_ref, tables_ref, own_ref, *refs):
    *near_refs, first_ref, second_ref, out_ref, word_ref, scale_ref = refs
    window = window_lines(own_ref, near_refs, first_ref, second_ref)
    mixed = mix_lines(index_ref, tables_ref, window)
    grad_x = line_blur(mixed[0:lines], False)
    grad_y = line_blur(mixed[lines : 2 * lines], True)
    grad_z = line_blur(mixed[2 * lines : 3 * lines], False)
    store_fields([grad_x, grad_y, grad_z], lines, out_ref, word_ref, scale_ref)


def model_kernel(lines, near, index_ref, tables_ref, target_ref, *refs):
    target = [target_ref[...]]
    for ref in refs[: near - 1]:
        target += decode(ref[...], 1)
    target = jnp.concatenate(target, axis=0)
    own_ref, *near_refs, first_ref, second_ref, out_ref, word_ref, scale_ref, sum_ref = refs[near - 1 :]
    window = window_lines(own_ref, near_refs, first_ref, second_ref)
    smooth = mix_lines(index_ref, tables_ref, window)
    model = smooth[3 * lines :]
    sums = [jnp.sum(model * target), jnp.sum(model * model), jnp.sum(target * target)]
    lane = lax.broadcasted_iota(I32, sum_ref.shape, 1)
    total = jnp.zeros(sum_ref.shape, F32)
    for k, value in enumerate(sums):
        total = jnp.where(lane == k, value, total)
    sum_ref[...] = total
    grad_x = line_blur(smooth[0:lines], False)
    grad_y = line_blur(smooth[lines : 2 * lines], True)
    grad_z = line_blur(smooth[2 * lines : 3 * lines], False)
    store_fields([grad_x, grad_y, grad_z], lines, out_ref, word_ref, scale_ref)


def sample_by_matmul(word, field_ref, his, store):
    count, beads = word.shape
    lo, hi = word & (LO - 1), (word >> 8) & 255
    lo_iota = lax.broadcasted_iota(I32, (LO, beads), 0)
    picks = [jnp.where(lo_iota == lo[q : q + 1], 1.0, 0.0).astype(BF16) for q in range(count)]
    pick = jnp.concatenate(picks, axis=1)
    sampled = jnp.dot(
        field_ref[...], jnp.concatenate([pick, pick], axis=0), preferred_element_type=F32
    )

    def finish():
        sub_iota = lax.broadcasted_iota(I32, (8, beads), 0)
        for q in range(count):
            own = jnp.broadcast_to(hi[q : q + 1], (8, beads))
            group, within = own >> 3, (own & 7) == sub_iota
            found = [jnp.zeros((8, beads), F32)] * 3
            for j in range(his // 8):
                here = group == j
                for k in range(3):
                    rows = slice(k * his + 8 * j, k * his + 8 * j + 8)
                    part = sampled[rows, q * beads : (q + 1) * beads]
                    found[k] = jnp.where(here, part, found[k])
            store(q, [jnp.sum(jnp.where(within, v, 0.0), axis=0, keepdims=True) for v in found])

    return finish


def sample_by_lanes(word, word_ref, scale_ref, lines, store):
    count, beads = word.shape
    tiles = word_ref.shape[1] // 128
    line_shift, lo_shift = lines.bit_length() - 1, LO.bit_length() - 1
    sub_iota = lax.broadcasted_iota(I32, (8, beads), 0)
    scale = scale_ref[0:1, :]
    for q in range(count):
        own = jnp.broadcast_to(word[q : q + 1], (8, beads))
        lo, hi = own & (LO - 1), (own >> lo_shift) & 255
        line = hi & (lines - 1)
        group = (line >> 3) * tiles + (hi >> line_shift) * (LO // 128) + (lo >> 7)
        within, lane = (line & 7) == sub_iota, lo & 127
        found = [jnp.zeros((8, beads), I32)] * 2
        for j in range(lines // 8 * tiles):
            here = group == j
            first, tile = j // tiles * 8, j % tiles * 128
            for k in range(2):
                table = word_ref[k * lines + first : k * lines + first + 8, tile : tile + 128]
                part = jnp.take_along_axis(table, lane, axis=1, mode="promise_in_bounds")
                found[k] = jnp.where(here, part, found[k])
        one, two = [jnp.sum(jnp.where(within, v, 0), axis=0, keepdims=True) for v in found]
        store(q, [v.astype(F32) * scale for v in unpack_three(one, two)])


def sample_kernel(
    lines, his, rb, by_lanes, start, got_ref, field_ref, word_ref, scale_ref, out_ref, force_ref
):
    slots = out_ref.shape[0]
    beads = got_ref.shape[1] // 3
    by_matmul = rb - by_lanes

    def body(i, carry):
        def store_from(first):
            def store(q, values):
                for k in range(3):
                    force_ref[k, pl.ds(i * rb + first + q, 1), :] = values[k]

            return store

        word = got_ref[pl.ds(start + i * rb, rb), 0:beads]
        finish = sample_by_matmul(word[:by_matmul], field_ref, his, store_from(0))
        rest = word[by_matmul:]
        sample_by_lanes(rest, word_ref, scale_ref, lines, store_from(by_matmul))
        finish()
        return carry

    lax.fori_loop(0, slots // rb, body, 0)
    rows = slice(start, start + slots)
    first, second = got_ref[rows, beads : 2 * beads], got_ref[rows, 2 * beads : 3 * beads]
    weight = (got_ref[rows, 0:beads] >> 16).astype(F32) * (1.0 / WEIGHT_SCALE)
    levers = [v.astype(F32) * (1.0 / LEVER_SCALE) for v in unpack_three(first, second)]
    force = [force_ref[k] * weight for k in range(3)]
    terms = force + [
        levers[1] * force[2] - levers[2] * force[1],
        levers[2] * force[0] - levers[0] * force[2],
        levers[0] * force[1] - levers[1] * force[0],
    ]
    lane = lax.broadcasted_iota(I32, out_ref.shape, 1)
    total = jnp.zeros(out_ref.shape, F32)
    for k, term in enumerate(terms):
        total = jnp.where(lane == k, jnp.sum(term, axis=1, keepdims=True), total)
    out_ref[...] = total


def join_kernel(most, *refs):
    *target_refs, model_ref, sum_ref, out_ref = refs
    bricks = out_ref.shape[0]
    lane = lax.broadcasted_iota(I32, out_ref.shape, 1)
    sums = sum_ref[0:1, :]
    for k in range(1, sum_ref.shape[0] // 8):
        sums = sums + sum_ref[8 * k : 8 * k + 1, :]
    total = jnp.zeros(out_ref.shape, F32)
    for k in range(most):
        rows = pl.ds(k, bricks, stride=most)
        parts = [ref[pl.ds(k, ref.shape[0] // most, stride=most), :] for ref in target_refs]
        own = jnp.concatenate(parts, axis=0)
        own = jnp.where(lane < 6, own, 0.0)
        own = own + pltpu.roll(jnp.where(lane < 6, model_ref[rows, :], 0.0), 6, 1)
        if k == 0:
            own = own + pltpu.roll(jnp.where(lane < 3, sums, 0.0), 12, 1)
        total = total + (pltpu.roll(own, FIELDS * k, 1) if k else own)
    out_ref[...] = total


def finish_kernel(most, voxel_total, place_ref, back_ref, out_ref):
    frags = out_ref.shape[1]
    bricks = back_ref.shape[0]
    row, rank = place_ref[0:1, :], place_ref[1:2, :]
    place = jnp.where(lax.broadcasted_iota(I32, (bricks, frags), 0) == row, 1.0, 0.0).astype(F32)
    back = back_ref[...]
    sums = jnp.sum(back, axis=0, keepdims=True)
    cross, model_sq, target_sq = sums[:, 12:13], sums[:, 13:14], sums[:, 14:15]
    norm_model = jnp.sqrt(model_sq + EPSILON)
    norm_target = jnp.sqrt(target_sq + EPSILON)
    corr = cross / (norm_model * norm_target)
    scale_target = voxel_total / (norm_model * norm_target)
    scale_model = voxel_total * corr / (norm_model * norm_model)
    found = lax.dot_general(
        back, place, (((0,), (0,)), ((), ())), precision=HIGHEST, preferred_element_type=F32
    )
    mine = jnp.zeros((FIELDS, frags), F32)
    for k in range(most):
        mine = jnp.where(rank == k, found[FIELDS * k : FIELDS * (k + 1)], mine)
    out_ref[...] = scale_target * mine[0:6] - scale_model * mine[6:12]


def cost(macs, nbytes):
    return pl.CostEstimate(flops=2 * macs, bytes_accessed=nbytes, transcendentals=0)


def call(
    kernel, out_shape, *args, scratch=(), name=None, macs=0, in_specs=None, vmem=VMEM_BYTES
):
    kwargs = {} if in_specs is None else {"in_specs": in_specs}
    return pl.pallas_call(
        kernel,
        out_shape=out_shape,
        scratch_shapes=list(scratch),
        compiler_params=pltpu.CompilerParams(vmem_limit_bytes=vmem),
        cost_estimate=cost(macs, 4 * sum(a.size for a in args)),
        name=name,
        **kwargs,
    )(*args)


def call_at(kernel, out_shape, index, table, *args, name=None, macs=0):
    vmem = pl.BlockSpec(memory_space=pltpu.VMEM)
    return call(
        kernel,
        out_shape,
        index, table, *args,
        in_specs=[pl.BlockSpec(memory_space=pltpu.SMEM)] + [vmem] * (1 + len(args)),
        name=name,
        macs=macs,
    )


def looked_up(values, position):
    found = jnp.full((), int(values[0]), I32)
    for i in range(1, len(values)):
        step = int(values[i]) - int(values[i - 1])
        if step:
            found = found + step * (position >= i).astype(I32)
    return found


def shifted(value, axis, step):
    size = lax.axis_size(axis)
    pairs = [(i, i + step) for i in range(size) if 0 <= i + step < size]
    return lax.ppermute(value, axis, pairs)


def paired(own, left, right):
    return lambda b: [own, right, left] if b % 2 == 0 else [own, left, right]


def swapped(first, second):
    size = lax.axis_size("brick")
    found = []
    for value, start in ((first, 0), (second, 1)):
        pairs = [(i, i + 1) for i in range(start, size - 1, 2)]
        found.append(lax.ppermute(value, "brick", pairs + [(j, i) for i, j in pairs]))
    return found


def relay_blocks(value, reach):
    size = lax.axis_size("relay")
    if size == 2:
        return [value, lax.ppermute(value, "relay", [(0, 1), (1, 0)])]
    blocks = [value]
    for step in range(1, min(reach, size - 1) + 1):
        blocks += [shifted(value, "relay", step), shifted(value, "relay", -step)]
    return blocks


def relay_order(size, reach):
    if size == 2:
        return lambda r: [r, 1 - r]
    steps = [0]
    for step in range(1, min(reach, size - 1) + 1):
        steps += [-step, step]
    return lambda r: [r + s for s in steps]


def relay_total(value):
    size = lax.axis_size("relay")
    values, moving = [value], value
    for _ in range(size - 1):
        moving = lax.ppermute(moving, "relay", [(i, (i + 1) % size) for i in range(size)])
        values.append(moving)
    return jnp.concatenate(values, axis=0)


def shards(target, frag_brick, bead_cell, bead_weight, bead_arm, frag_angle):
    brick_count, relay_count = lax.axis_size("brick"), lax.axis_size("relay")
    frags, beads = bead_cell.shape
    planes, columns, rows = target.shape
    lines = planes * columns
    his = lines * (rows // LO)
    assert rows % LO == 0 and his <= 256 and columns >= 2 * KR
    assert beads == 128 and lines & (lines - 1) == 0
    voxel_total = float(brick_count * columns * relay_count * planes * rows)
    most = max(2, 2 * frags // brick_count)
    slots = brick_count * most
    assert most * FIELDS <= 128

    z_total, x_total = relay_count * planes, brick_count * columns
    gz, dz = axis_matrix(z_total, False), axis_matrix(z_total, True)
    gx, dx = axis_matrix(x_total, False), axis_matrix(x_total, True)
    near = 2 if relay_count == 2 else 1
    reach_one, reach_two = -(-KR // planes), -(-2 * KR // planes)
    target_table, tz, tx, tn = weight_table(
        [gz, gz, dz], [dx, gx, gx], lambda r: [r] * 3, planes, relay_count, relay_order(relay_count, reach_one),
        columns, brick_count,
        paired(np.arange(columns), np.arange(-KR, 0), np.arange(columns, columns + KR)),
    )
    model_table, mz, mx, mn = weight_table(
        [gz @ gz, gz @ gz, dz @ gz] + [gz] * near, [dx @ gx, gx @ gx, gx @ gx] + [gx] * near,
        lambda r: [r] * 4 + [1 - r] * (near - 1),
        planes, relay_count, relay_order(relay_count, reach_two), columns, brick_count,
        paired(np.arange(columns), np.arange(-columns, 0), np.arange(columns, 2 * columns)),
    )
    r, b = lax.axis_index("relay"), lax.axis_index("brick")
    target_index = (looked_up(tz, r) * tn + looked_up(tx, b)).reshape(1)
    model_index = (looked_up(mz, r) * mn + looked_up(mx, b)).reshape(1)

    target_lines = target.reshape(lines, rows)
    words = jax.ShapeDtypeStruct((lines // 2, rows + SCALE_LANES), I32)
    hbm = pl.BlockSpec(memory_space=pltpu.HBM)
    packed = [frag_brick.reshape(1, frags), frag_angle, bead_cell, bead_weight, bead_arm]
    packed += [target_lines]
    sent, place, target_code = call(
        functools.partial(pack_kernel, most, lines, rows),
        [
            jax.ShapeDtypeStruct((slots, 3 * beads), I32),
            jax.ShapeDtypeStruct((8, frags), I32),
            words,
        ],
        *packed,
        in_specs=[hbm] * len(packed),
        scratch=[pltpu.VMEM(a.shape, a.dtype) for a in packed]
        + [pltpu.SemaphoreType.DMA((len(packed),))],
        name="pack",
        vmem=PACK_VMEM_BYTES,
    )
    target_blocks = relay_blocks(target_code, reach_one)
    by_column = [t.reshape(-1, columns, rows + SCALE_LANES) for t in target_blocks]
    left_edge = jnp.concatenate([t[:, columns - KR :] for t in by_column], axis=0)
    right_edge = jnp.concatenate([t[:, :KR] for t in by_column], axis=0)
    first_edge = jnp.where(b % 2 == 0, left_edge, right_edge)
    second_edge = jnp.where(b % 2 == 0, right_edge, left_edge)
    target_near = swapped(
        first_edge.reshape(-1, rows + SCALE_LANES), second_edge.reshape(-1, rows + SCALE_LANES)
    )

    got = lax.all_to_all(sent, "brick", split_axis=0, concat_axis=0, tiled=True)
    smooth, coded = call(
        functools.partial(splat_kernel, lines, min(64, slots)),
        [jax.ShapeDtypeStruct((lines, rows), F32), words],
        got,
        scratch=[pltpu.VMEM((his, LO), F32)],
        name="splat",
        macs=slots * beads * his * LO,
    )
    coded, *target_near = lax.optimization_barrier((coded, *target_near))
    target_parts = [target_lines] + target_blocks[1:] + target_near
    blocks = relay_blocks(coded, reach_two)
    field_shapes = [
        jax.ShapeDtypeStruct((3 * his, 2 * LO), BF16),
        jax.ShapeDtypeStruct((2 * lines, rows), I32),
        jax.ShapeDtypeStruct((8, 128), F32),
    ]
    target_field = call_at(
        functools.partial(target_kernel, lines),
        field_shapes,
        target_index, jnp.asarray(target_table), *target_parts,
        name="target_fields",
        macs=9 * lines * rows * 128,
    )

    def sample(field, start, count, name):
        rb = min(32, count)
        return call(
            functools.partial(sample_kernel, lines, his, rb, rb * BY_LANES // 32, start),
            jax.ShapeDtypeStruct((count, 128), F32),
            got, *field,
            scratch=[pltpu.VMEM((3, count, beads), F32)],
            name=name,
            macs=6 * count * beads * his * LO,
        )

    part = slots // 4
    target_first = sample(target_field, 0, part, "target_sample_a")
    blocks, target_first, target_field = lax.optimization_barrier(
        (blocks, target_first, target_field)
    )
    beside = jnp.concatenate(blocks, axis=0)
    model_parts = [smooth] + blocks[1:]
    model_parts += swapped(beside, beside)
    target_second = sample(target_field, part, slots - part, "target_sample_b")
    target_second, *model_parts = lax.optimization_barrier((target_second, *model_parts))
    *model_field, partial = call_at(
        functools.partial(model_kernel, lines, near),
        field_shapes + [jax.ShapeDtypeStruct((8, 128), F32)],
        model_index, jnp.asarray(model_table), target_lines, *target_blocks[1:near], *model_parts,
        name="model_fields",
    )
    partials = partial if near == relay_count else relay_total(partial)
    model_sums = sample(model_field, 0, slots, "model_sample")
    leaving = call(
        functools.partial(join_kernel, most),
        jax.ShapeDtypeStruct((brick_count, 128), F32),
        target_first, target_second, model_sums, partials,
        name="join",
    )
    back = lax.all_to_all(leaving, "brick", split_axis=0, concat_axis=0, tiled=True)
    return call(
        functools.partial(finish_kernel, most, voxel_total),
        jax.ShapeDtypeStruct((6, frags), F32),
        place, back,
        name="finish",
    )


def solution(mesh):
    placed = (
        P("relay", "brick", None),
        P(("brick", "relay"), None),
        P(("brick", "relay"), None),
        P(("brick", "relay"), None),
        P(None, ("brick", "relay"), None),
        P(None, ("brick", "relay")),
    )
    return jax.shard_map(
        shards, mesh=mesh, in_specs=placed, out_specs=P(None, ("brick", "relay")), check_vma=False
    )
```

```python
import functools

import jax
import jax.numpy as jnp
import numpy as np
from jax import lax
from jax.experimental import pallas as pl
from jax.experimental.pallas import tpu as pltpu
from jax.sharding import PartitionSpec as P

KR = 4
SIGMA = 1.5
EPSILON = 1e-06
HIGHEST = lax.Precision.HIGHEST
LO = 256
BY_LANES = 14
FIELDS = 16
WEIGHT_SCALE = 512.0
LEVER_SCALE = 32768.0
LEVER_BIAS = 1 << 20
FIELD_TOP = 1048575.0
TINY = 1e-30
CODE_TOP = 65535
SCALE_UNIT = 512.0
SCALE_LANES = 128
VMEM_BYTES = 48 << 20
PACK_VMEM_BYTES = 60 << 20
F32 = jnp.float32
BF16 = jnp.bfloat16
I32 = jnp.int32


def taps_of(derivative):
    offsets = np.arange(-KR, KR + 1) * 1.0
    gaussian = np.exp(-(offsets**2) / (2.0 * SIGMA**2))
    gaussian = gaussian / gaussian.sum()
    if derivative:
        return -offsets / SIGMA**2 * gaussian
    return gaussian


def axis_matrix(length, derivative):
    offsets = np.arange(length)[:, None] - np.arange(length)[None, :]
    return np.where(
        np.abs(offsets) <= KR, taps_of(derivative)[np.clip(offsets + KR, 0, 2 * KR)], 0.0
    )


def columns_at(matrix, rows, wanted):
    inside = (wanted >= 0) & (wanted < matrix.shape[1])
    picked = matrix[rows][:, np.clip(wanted, 0, matrix.shape[1] - 1)]
    return np.where(inside[None, :], picked, 0.0)


def unique_tables(tables):
    flat = np.stack([t.reshape(-1) for t in tables])
    kept, inverse = np.unique(np.round(flat, 14), axis=0, return_inverse=True)
    return kept.reshape((-1,) + tables[0].shape), inverse.reshape(-1).astype(np.int32)


def pieces_np(table):
    import ml_dtypes

    high = table.astype(np.float32).astype(ml_dtypes.bfloat16)
    low = (table - high.astype(np.float64)).astype(ml_dtypes.bfloat16)
    return np.concatenate([high, high, low], axis=-1)


def weight_table(
    z_kinds, x_kinds, z_rows, z_len, z_count, z_blocks, x_len, x_count, x_parts
):
    z_tables = []
    for r in range(z_count):
        wanted = np.concatenate([np.arange(z_len) + z_len * block for block in z_blocks(r)])
        rows = [np.arange(z_len) + z_len * block for block in z_rows(r)]
        z_tables.append(np.stack([columns_at(m, i, wanted) for m, i in zip(z_kinds, rows)]))
    x_tables = []
    for b in range(x_count):
        wanted = np.concatenate([x_len * b + part for part in x_parts(b)])
        rows = np.arange(x_len) + x_len * b
        x_tables.append(np.stack([columns_at(m, rows, wanted) for m in x_kinds]))
    z_tables, z_inverse = unique_tables(z_tables)
    x_tables, x_inverse = unique_tables(x_tables)
    kinds = len(z_kinds)
    parts, start = [], 0
    for part in x_parts(0):
        piece = x_tables[:, :, :, start : start + len(part)]
        start += len(part)
        full = np.einsum("rkzi,bkxj->rbkzxij", z_tables, piece)
        parts.append(
            full.reshape(len(z_tables) * len(x_tables), kinds * z_len * x_len, -1)
        )
    table = pieces_np(np.concatenate(parts, axis=-1))
    return table, z_inverse, x_inverse, len(x_tables)


def eye_column(row, eye):
    return jnp.sum(jnp.where(eye, row, jnp.zeros_like(row)), axis=1, keepdims=True)


def slot_row(row, most):
    frags = row.shape[1]
    sub = lax.broadcasted_iota(I32, (frags, frags), 0)
    lane = lax.broadcasted_iota(I32, (frags, frags), 1)
    eye = sub == lane
    earlier = jnp.logical_and(eye_column(row, eye) == row, sub < lane)
    return jnp.sum(jnp.where(earlier, 1, 0), axis=0, keepdims=True), eye


def pack_kernel(most, lines, row_count, *refs):
    inputs, (out_ref, place_ref, code_ref) = refs[:6], refs[6:9]
    held, sems = refs[9:15], refs[15]
    copies = [
        pltpu.make_async_copy(source, target, sems.at[k])
        for k, (source, target) in enumerate(zip(inputs, held))
    ]
    for copy in copies:
        copy.start()
    brick_ref, angle_ref, cell_ref, weight_ref, arm_ref, target_ref = held
    for copy in copies[:2]:
        copy.wait()
    frags, beads = cell_ref.shape
    slots = out_ref.shape[0]
    row = brick_ref[...]
    rank, eye = slot_row(row, most)
    slot = row * most + rank
    place = jnp.where(lax.broadcasted_iota(I32, (slots, frags), 0) == slot, 1.0, 0.0).astype(BF16)

    angles = angle_ref[...]
    cos, sin = jnp.cos(angles), jnp.sin(angles)
    cos_a, cos_b, cos_c = cos[0:1], cos[1:2], cos[2:3]
    sin_a, sin_b, sin_c = sin[0:1], sin[1:2], sin[2:3]
    turn = [
        [cos_a * cos_b, cos_a * sin_b * sin_c - sin_a * cos_c, cos_a * sin_b * cos_c + sin_a * sin_c],
        [sin_a * cos_b, sin_a * sin_b * sin_c + cos_a * cos_c, sin_a * sin_b * cos_c - cos_a * sin_c],
        [-sin_b, cos_b * sin_c, cos_b * cos_c],
    ]
    turn = [[eye_column(value, eye) for value in values] for values in turn]
    place_ref[0:1, :] = row
    place_ref[1:2, :] = rank
    for copy in copies[2:]:
        copy.wait()
    encode(target_ref[...], code_ref)
    levers = []
    for i in range(3):
        total = turn[i][0] * arm_ref[0]
        for j in (1, 2):
            total = total + turn[i][j] * arm_ref[j]
        lever = jnp.round(total * LEVER_SCALE).astype(I32)
        levers += [lever >> 14, (lever >> 7) & 127, lever & 127]

    cell = cell_ref[...]
    line = ((cell.astype(F32) + 0.5) * (1.0 / row_count)).astype(I32)
    y = cell - line * row_count
    weight = weight_ref[...].astype(F32) * WEIGHT_SCALE
    pieces = [(y // LO) * lines + line, y % LO] + levers
    pieces = [weight.astype(BF16)] + [v.astype(F32).astype(BF16) for v in pieces]
    payload = jnp.concatenate(pieces, axis=1)
    placed = jnp.dot(place, payload, preferred_element_type=F32).astype(I32)
    weight, hi, lo, *levers = [
        placed[:, k * beads : (k + 1) * beads] for k in range(len(pieces))
    ]
    code = (hi << 8) | lo
    lx, ly, lz = [
        (levers[k] << 14) + (levers[k + 1] << 7) + levers[k + 2] for k in (0, 3, 6)
    ]
    one, two = pack_three(lx, ly, lz)
    out_ref[:, 0:beads] = code | (weight << 16)
    out_ref[:, beads : 2 * beads] = one
    out_ref[:, 2 * beads : 3 * beads] = two


def line_blur(value, derivative):
    taps = taps_of(derivative)
    rows, length = value.shape
    wide = jnp.concatenate([value, jnp.zeros((rows, 128), F32)], axis=1)
    total = None if derivative else float(taps[KR]) * value
    for d in range(1, KR + 1):
        up = pltpu.roll(wide, d, 1)[:, :length]
        down = pltpu.roll(wide, length + 128 - d, 1)[:, :length]
        pair = up - down if derivative else up + down
        term = float(taps[KR + d]) * pair
        total = term if total is None else total + term
    return total


def encode(value, out_ref):
    half, length = value.shape[0] // 2, value.shape[1]
    top = (jnp.max(value) * SCALE_UNIT).astype(I32) + 1
    scale = (SCALE_UNIT * CODE_TOP) / top.astype(F32)
    code = jnp.minimum((value * scale + 0.5).astype(I32), CODE_TOP)
    out_ref[:, :length] = code[:half] | (code[half:] << 16)
    out_ref[:, length:] = jnp.full((half, SCALE_LANES), top, I32)


def decode(words, count):
    half, length = words.shape[0] // count, words.shape[1] - SCALE_LANES
    step = words[:, length : length + 1].astype(F32) * (1.0 / (SCALE_UNIT * CODE_TOP))
    low = (words[:, :length] & CODE_TOP).astype(F32) * step
    high = ((words[:, :length] >> 16) & CODE_TOP).astype(F32) * step
    lines = []
    for k in range(count):
        rows = slice(k * half, (k + 1) * half)
        lines += [low[rows], high[rows]]
    return lines


def splat_kernel(lines, rb, got_ref, out_ref, code_ref, acc_ref):
    slots = got_ref.shape[0]
    beads = got_ref.shape[1] // 3
    his = acc_ref.shape[0]
    acc_ref[...] = jnp.zeros_like(acc_ref)
    hi_iota = lax.broadcasted_iota(I32, (his, beads), 0)
    lo_iota = lax.broadcasted_iota(I32, (LO, beads), 0)

    def body(i, carry):
        word = got_ref[pl.ds(i * rb, rb), 0:beads]
        lo = word & (LO - 1)
        hi = (word >> 8) & 255
        weight = (word >> 16).astype(F32) * (1.0 / WEIGHT_SCALE)
        left, right = [], []
        for q in range(rb):
            left.append(jnp.where(hi_iota == hi[q : q + 1], weight[q : q + 1], 0.0).astype(BF16))
            right.append(jnp.where(lo_iota == lo[q : q + 1], 1.0, 0.0).astype(BF16))
        acc_ref[...] += lax.dot_general(
            jnp.concatenate(left, axis=1),
            jnp.concatenate(right, axis=1),
            (((1,), (1,)), ((), ())),
            preferred_element_type=F32,
        )
        return carry

    lax.fori_loop(0, slots // rb, body, 0)
    density = [acc_ref[yh * lines : (yh + 1) * lines, :] for yh in range(his // lines)]
    smooth = line_blur(jnp.concatenate(density, axis=1), False)
    out_ref[...] = smooth
    encode(smooth, code_ref)


def split(value):
    high = value.astype(BF16)
    low = (value - high.astype(F32)).astype(BF16)
    return high, low


def mix_lines(index_ref, tables_ref, parts):
    value = jnp.concatenate(parts, axis=0)
    high, low = split(value)
    return jnp.dot(
        tables_ref[index_ref[0]], jnp.concatenate([high, low, high], axis=0), preferred_element_type=F32
    )


def pack_three(first, second, third):
    third = third + LEVER_BIAS
    return (first << 11) | (third >> 10), (second << 11) | (third & 1023)


def unpack_three(one, two):
    return one >> 11, two >> 11, (((one & 2047) << 10) | (two & 1023)) - LEVER_BIAS


def store_fields(fields, lines, out_ref, word_ref, scale_ref):
    top = jnp.maximum(jnp.max(jnp.abs(jnp.concatenate(fields, axis=0))), TINY)
    scale_ref[...] = jnp.full(scale_ref.shape, top * (1.0 / FIELD_TOP), F32)
    up = FIELD_TOP / jnp.full((1, fields[0].shape[1]), top, F32)
    one, two = pack_three(*[jnp.round(field * up).astype(I32) for field in fields])
    word_ref[:lines, :] = one
    word_ref[lines:, :] = two
    his = fields[0].shape[1] // LO * lines
    for k, field in enumerate(fields):
        for yh in range(field.shape[1] // LO):
            high, low = split(field[:, yh * LO : (yh + 1) * LO])
            rows = slice(k * his + yh * lines, k * his + (yh + 1) * lines)
            out_ref[rows, 0:LO] = high
            out_ref[rows, LO : 2 * LO] = low


def window_lines(own_ref, near_refs, first_ref, second_ref):
    lines = [own_ref[...]]
    for ref in near_refs:
        lines += decode(ref[...], 1)
    for ref in (first_ref, second_ref):
        lines += decode(ref[...], len(near_refs) + 1)
    return lines


def target_kernel(lines, index_ref, tables_ref, own_ref, *refs):
    *near_refs, first_ref, second_ref, out_ref, word_ref, scale_ref = refs
    window = window_lines(own_ref, near_refs, first_ref, second_ref)
    mixed = mix_lines(index_ref, tables_ref, window)
    grad_x = line_blur(mixed[0:lines], False)
    grad_y = line_blur(mixed[lines : 2 * lines], True)
    grad_z = line_blur(mixed[2 * lines : 3 * lines], False)
    store_fields([grad_x, grad_y, grad_z], lines, out_ref, word_ref, scale_ref)


def model_kernel(lines, near, index_ref, tables_ref, target_ref, *refs):
    target = [target_ref[...]]
    for ref in refs[: near - 1]:
        target += decode(ref[...], 1)
    target = jnp.concatenate(target, axis=0)
    own_ref, *near_refs, first_ref, second_ref, out_ref, word_ref, scale_ref, sum_ref = refs[near - 1 :]
    window = window_lines(own_ref, near_refs, first_ref, second_ref)
    smooth = mix_lines(index_ref, tables_ref, window)
    model = smooth[3 * lines :]
    sums = [jnp.sum(model * target), jnp.sum(model * model), jnp.sum(target * target)]
    lane = lax.broadcasted_iota(I32, sum_ref.shape, 1)
    total = jnp.zeros(sum_ref.shape, F32)
    for k, value in enumerate(sums):
        total = jnp.where(lane == k, value, total)
    sum_ref[...] = total
    grad_x = line_blur(smooth[0:lines], False)
    grad_y = line_blur(smooth[lines : 2 * lines], True)
    grad_z = line_blur(smooth[2 * lines : 3 * lines], False)
    store_fields([grad_x, grad_y, grad_z], lines, out_ref, word_ref, scale_ref)


def sample_by_matmul(word, field_ref, his, store):
    count, beads = word.shape
    lo, hi = word & (LO - 1), (word >> 8) & 255
    lo_iota = lax.broadcasted_iota(I32, (LO, beads), 0)
    picks = [jnp.where(lo_iota == lo[q : q + 1], 1.0, 0.0).astype(BF16) for q in range(count)]
    pick = jnp.concatenate(picks, axis=1)
    sampled = jnp.dot(
        field_ref[...], jnp.concatenate([pick, pick], axis=0), preferred_element_type=F32
    )

    def finish():
        sub_iota = lax.broadcasted_iota(I32, (8, beads), 0)
        for q in range(count):
            own = jnp.broadcast_to(hi[q : q + 1], (8, beads))
            group, within = own >> 3, (own & 7) == sub_iota
            found = [jnp.zeros((8, beads), F32)] * 3
            for j in range(his // 8):
                here = group == j
                for k in range(3):
                    rows = slice(k * his + 8 * j, k * his + 8 * j + 8)
                    part = sampled[rows, q * beads : (q + 1) * beads]
                    found[k] = jnp.where(here, part, found[k])
            store(q, [jnp.sum(jnp.where(within, v, 0.0), axis=0, keepdims=True) for v in found])

    return finish


def sample_by_lanes(word, word_ref, scale_ref, lines, store):
    count, beads = word.shape
    tiles = word_ref.shape[1] // 128
    line_shift, lo_shift = lines.bit_length() - 1, LO.bit_length() - 1
    sub_iota = lax.broadcasted_iota(I32, (8, beads), 0)
    scale = scale_ref[0:1, :]
    for q in range(count):
        own = jnp.broadcast_to(word[q : q + 1], (8, beads))
        lo, hi = own & (LO - 1), (own >> lo_shift) & 255
        line = hi & (lines - 1)
        group = (line >> 3) * tiles + (hi >> line_shift) * (LO // 128) + (lo >> 7)
        within, lane = (line & 7) == sub_iota, lo & 127
        found = [jnp.zeros((8, beads), I32)] * 2
        for j in range(lines // 8 * tiles):
            here = group == j
            first, tile = j // tiles * 8, j % tiles * 128
            for k in range(2):
                table = word_ref[k * lines + first : k * lines + first + 8, tile : tile + 128]
                part = jnp.take_along_axis(table, lane, axis=1, mode="promise_in_bounds")
                found[k] = jnp.where(here, part, found[k])
        one, two = [jnp.sum(jnp.where(within, v, 0), axis=0, keepdims=True) for v in found]
        store(q, [v.astype(F32) * scale for v in unpack_three(one, two)])


def sample_kernel(
    lines, his, rb, by_lanes, start, got_ref, field_ref, word_ref, scale_ref, out_ref, force_ref
):
    slots = out_ref.shape[0]
    beads = got_ref.shape[1] // 3
    by_matmul = rb - by_lanes

    def body(i, carry):
        def store_from(first):
            def store(q, values):
                for k in range(3):
                    force_ref[k, pl.ds(i * rb + first + q, 1), :] = values[k]

            return store

        word = got_ref[pl.ds(start + i * rb, rb), 0:beads]
        finish = sample_by_matmul(word[:by_matmul], field_ref, his, store_from(0))
        rest = word[by_matmul:]
        sample_by_lanes(rest, word_ref, scale_ref, lines, store_from(by_matmul))
        finish()
        return carry

    lax.fori_loop(0, slots // rb, body, 0)
    rows = slice(start, start + slots)
    first, second = got_ref[rows, beads : 2 * beads], got_ref[rows, 2 * beads : 3 * beads]
    weight = (got_ref[rows, 0:beads] >> 16).astype(F32) * (1.0 / WEIGHT_SCALE)
    levers = [v.astype(F32) * (1.0 / LEVER_SCALE) for v in unpack_three(first, second)]
    force = [force_ref[k] * weight for k in range(3)]
    terms = force + [
        levers[1] * force[2] - levers[2] * force[1],
        levers[2] * force[0] - levers[0] * force[2],
        levers[0] * force[1] - levers[1] * force[0],
    ]
    lane = lax.broadcasted_iota(I32, out_ref.shape, 1)
    total = jnp.zeros(out_ref.shape, F32)
    for k, term in enumerate(terms):
        total = jnp.where(lane == k, jnp.sum(term, axis=1, keepdims=True), total)
    out_ref[...] = total


def join_kernel(most, *refs):
    *target_refs, model_ref, sum_ref, out_ref = refs
    bricks = out_ref.shape[0]
    lane = lax.broadcasted_iota(I32, out_ref.shape, 1)
    sums = sum_ref[0:1, :]
    for k in range(1, sum_ref.shape[0] // 8):
        sums = sums + sum_ref[8 * k : 8 * k + 1, :]
    total = jnp.zeros(out_ref.shape, F32)
    for k in range(most):
        rows = pl.ds(k, bricks, stride=most)
        parts = [ref[pl.ds(k, ref.shape[0] // most, stride=most), :] for ref in target_refs]
        own = jnp.concatenate(parts, axis=0)
        own = jnp.where(lane < 6, own, 0.0)
        own = own + pltpu.roll(jnp.where(lane < 6, model_ref[rows, :], 0.0), 6, 1)
        if k == 0:
            own = own + pltpu.roll(jnp.where(lane < 3, sums, 0.0), 12, 1)
        total = total + (pltpu.roll(own, FIELDS * k, 1) if k else own)
    out_ref[...] = total


def finish_kernel(most, voxel_total, place_ref, back_ref, out_ref):
    frags = out_ref.shape[1]
    bricks = back_ref.shape[0]
    row, rank = place_ref[0:1, :], place_ref[1:2, :]
    place = jnp.where(lax.broadcasted_iota(I32, (bricks, frags), 0) == row, 1.0, 0.0).astype(F32)
    back = back_ref[...]
    sums = jnp.sum(back, axis=0, keepdims=True)
    cross, model_sq, target_sq = sums[:, 12:13], sums[:, 13:14], sums[:, 14:15]
    norm_model = jnp.sqrt(model_sq + EPSILON)
    norm_target = jnp.sqrt(target_sq + EPSILON)
    corr = cross / (norm_model * norm_target)
    scale_target = voxel_total / (norm_model * norm_target)
    scale_model = voxel_total * corr / (norm_model * norm_model)
    found = lax.dot_general(
        back, place, (((0,), (0,)), ((), ())), precision=HIGHEST, preferred_element_type=F32
    )
    mine = jnp.zeros((FIELDS, frags), F32)
    for k in range(most):
        mine = jnp.where(rank == k, found[FIELDS * k : FIELDS * (k + 1)], mine)
    out_ref[...] = scale_target * mine[0:6] - scale_model * mine[6:12]


def cost(macs, nbytes):
    return pl.CostEstimate(flops=2 * macs, bytes_accessed=nbytes, transcendentals=0)


def call(
    kernel, out_shape, *args, scratch=(), name=None, macs=0, in_specs=None, vmem=VMEM_BYTES
):
    kwargs = {} if in_specs is None else {"in_specs": in_specs}
    return pl.pallas_call(
        kernel,
        out_shape=out_shape,
        scratch_shapes=list(scratch),
        compiler_params=pltpu.CompilerParams(vmem_limit_bytes=vmem),
        cost_estimate=cost(macs, 4 * sum(a.size for a in args)),
        name=name,
        **kwargs,
    )(*args)


def call_at(kernel, out_shape, index, table, *args, name=None, macs=0):
    vmem = pl.BlockSpec(memory_space=pltpu.VMEM)
    return call(
        kernel,
        out_shape,
        index, table, *args,
        in_specs=[pl.BlockSpec(memory_space=pltpu.SMEM)] + [vmem] * (1 + len(args)),
        name=name,
        macs=macs,
    )


def looked_up(values, position):
    found = jnp.full((), int(values[0]), I32)
    for i in range(1, len(values)):
        step = int(values[i]) - int(values[i - 1])
        if step:
            found = found + step * (position >= i).astype(I32)
    return found


def shifted(value, axis, step):
    size = lax.axis_size(axis)
    pairs = [(i, i + step) for i in range(size) if 0 <= i + step < size]
    return lax.ppermute(value, axis, pairs)


def paired(own, left, right):
    return lambda b: [own, right, left] if b % 2 == 0 else [own, left, right]


def swapped(first, second):
    size = lax.axis_size("brick")
    found = []
    for value, start in ((first, 0), (second, 1)):
        pairs = [(i, i + 1) for i in range(start, size - 1, 2)]
        found.append(lax.ppermute(value, "brick", pairs + [(j, i) for i, j in pairs]))
    return found


def relay_blocks(value, reach):
    size = lax.axis_size("relay")
    if size == 2:
        return [value, lax.ppermute(value, "relay", [(0, 1), (1, 0)])]
    blocks = [value]
    for step in range(1, min(reach, size - 1) + 1):
        blocks += [shifted(value, "relay", step), shifted(value, "relay", -step)]
    return blocks


def relay_order(size, reach):
    if size == 2:
        return lambda r: [r, 1 - r]
    steps = [0]
    for step in range(1, min(reach, size - 1) + 1):
        steps += [-step, step]
    return lambda r: [r + s for s in steps]


def relay_total(value):
    size = lax.axis_size("relay")
    values, moving = [value], value
    for _ in range(size - 1):
        moving = lax.ppermute(moving, "relay", [(i, (i + 1) % size) for i in range(size)])
        values.append(moving)
    return jnp.concatenate(values, axis=0)


def shards(target, frag_brick, bead_cell, bead_weight, bead_arm, frag_angle):
    brick_count, relay_count = lax.axis_size("brick"), lax.axis_size("relay")
    frags, beads = bead_cell.shape
    planes, columns, rows = target.shape
    lines = planes * columns
    his = lines * (rows // LO)
    assert rows % LO == 0 and his <= 256 and columns >= 2 * KR
    assert beads == 128 and lines & (lines - 1) == 0
    voxel_total = float(brick_count * columns * relay_count * planes * rows)
    most = max(2, 2 * frags // brick_count)
    slots = brick_count * most
    assert most * FIELDS <= 128

    z_total, x_total = relay_count * planes, brick_count * columns
    gz, dz = axis_matrix(z_total, False), axis_matrix(z_total, True)
    gx, dx = axis_matrix(x_total, False), axis_matrix(x_total, True)
    near = 2 if relay_count == 2 else 1
    reach_one, reach_two = -(-KR // planes), -(-2 * KR // planes)
    target_table, tz, tx, tn = weight_table(
        [gz, gz, dz], [dx, gx, gx], lambda r: [r] * 3, planes, relay_count, relay_order(relay_count, reach_one),
        columns, brick_count,
        paired(np.arange(columns), np.arange(-KR, 0), np.arange(columns, columns + KR)),
    )
    model_table, mz, mx, mn = weight_table(
        [gz @ gz, gz @ gz, dz @ gz] + [gz] * near, [dx @ gx, gx @ gx, gx @ gx] + [gx] * near,
        lambda r: [r] * 4 + [1 - r] * (near - 1),
        planes, relay_count, relay_order(relay_count, reach_two), columns, brick_count,
        paired(np.arange(columns), np.arange(-columns, 0), np.arange(columns, 2 * columns)),
    )
    r, b = lax.axis_index("relay"), lax.axis_index("brick")
    target_index = (looked_up(tz, r) * tn + looked_up(tx, b)).reshape(1)
    model_index = (looked_up(mz, r) * mn + looked_up(mx, b)).reshape(1)

    target_lines = target.reshape(lines, rows)
    words = jax.ShapeDtypeStruct((lines // 2, rows + SCALE_LANES), I32)
    hbm = pl.BlockSpec(memory_space=pltpu.HBM)
    packed = [frag_brick.reshape(1, frags), frag_angle, bead_cell, bead_weight, bead_arm]
    packed += [target_lines]
    sent, place, target_code = call(
        functools.partial(pack_kernel, most, lines, rows),
        [
            jax.ShapeDtypeStruct((slots, 3 * beads), I32),
            jax.ShapeDtypeStruct((8, frags), I32),
            words,
        ],
        *packed,
        in_specs=[hbm] * len(packed),
        scratch=[pltpu.VMEM(a.shape, a.dtype) for a in packed]
        + [pltpu.SemaphoreType.DMA((len(packed),))],
        name="pack",
        vmem=PACK_VMEM_BYTES,
    )
    target_blocks = relay_blocks(target_code, reach_one)
    by_column = [t.reshape(-1, columns, rows + SCALE_LANES) for t in target_blocks]
    left_edge = jnp.concatenate([t[:, columns - KR :] for t in by_column], axis=0)
    right_edge = jnp.concatenate([t[:, :KR] for t in by_column], axis=0)
    first_edge = jnp.where(b % 2 == 0, left_edge, right_edge)
    second_edge = jnp.where(b % 2 == 0, right_edge, left_edge)
    target_near = swapped(
        first_edge.reshape(-1, rows + SCALE_LANES), second_edge.reshape(-1, rows + SCALE_LANES)
    )

    got = lax.all_to_all(sent, "brick", split_axis=0, concat_axis=0, tiled=True)
    smooth, coded = call(
        functools.partial(splat_kernel, lines, min(64, slots)),
        [jax.ShapeDtypeStruct((lines, rows), F32), words],
        got,
        scratch=[pltpu.VMEM((his, LO), F32)],
        name="splat",
        macs=slots * beads * his * LO,
    )
    coded, *target_near = lax.optimization_barrier((coded, *target_near))
    target_parts = [target_lines] + target_blocks[1:] + target_near
    blocks = relay_blocks(coded, reach_two)
    field_shapes = [
        jax.ShapeDtypeStruct((3 * his, 2 * LO), BF16),
        jax.ShapeDtypeStruct((2 * lines, rows), I32),
        jax.ShapeDtypeStruct((8, 128), F32),
    ]
    target_field = call_at(
        functools.partial(target_kernel, lines),
        field_shapes,
        target_index, jnp.asarray(target_table), *target_parts,
        name="target_fields",
        macs=9 * lines * rows * 128,
    )

    def sample(field, start, count, name):
        rb = min(32, count)
        return call(
            functools.partial(sample_kernel, lines, his, rb, rb * BY_LANES // 32, start),
            jax.ShapeDtypeStruct((count, 128), F32),
            got, *field,
            scratch=[pltpu.VMEM((3, count, beads), F32)],
            name=name,
            macs=6 * count * beads * his * LO,
        )

    part = slots // 4
    target_first = sample(target_field, 0, part, "target_sample_a")
    blocks, target_first, target_field = lax.optimization_barrier(
        (blocks, target_first, target_field)
    )
    beside = jnp.concatenate(blocks, axis=0)
    model_parts = [smooth] + blocks[1:]
    model_parts += swapped(beside, beside)
    target_second = sample(target_field, part, slots - part, "target_sample_b")
    target_second, *model_parts = lax.optimization_barrier((target_second, *model_parts))
    *model_field, partial = call_at(
        functools.partial(model_kernel, lines, near),
        field_shapes + [jax.ShapeDtypeStruct((8, 128), F32)],
        model_index, jnp.asarray(model_table), target_lines, *target_blocks[1:near], *model_parts,
        name="model_fields",
    )
    partials = partial if near == relay_count else relay_total(partial)
    model_sums = sample(model_field, 0, slots, "model_sample")
    leaving = call(
        functools.partial(join_kernel, most),
        jax.ShapeDtypeStruct((brick_count, 128), F32),
        target_first, target_second, model_sums, partials,
        name="join",
    )
    back = lax.all_to_all(leaving, "brick", split_axis=0, concat_axis=0, tiled=True)
    return call(
        functools.partial(finish_kernel, most, voxel_total),
        jax.ShapeDtypeStruct((6, frags), F32),
        place, back,
        name="finish",
    )


def solution(mesh):
    placed = (
        P("relay", "brick", None),
        P(("brick", "relay"), None),
        P(("brick", "relay"), None),
        P(("brick", "relay"), None),
        P(None, ("brick", "relay"), None),
        P(None, ("brick", "relay")),
    )
    return jax.shard_map(
        shards, mesh=mesh, in_specs=placed, out_specs=P(None, ("brick", "relay")), check_vma=False
    )
```

```python
import functools

import jax
import jax.numpy as jnp
import numpy as np
from jax import lax
from jax.experimental import pallas as pl
from jax.experimental.pallas import tpu as pltpu
from jax.sharding import PartitionSpec as P

KR = 4
SIGMA = 1.5
EPSILON = 1e-06
HIGHEST = lax.Precision.HIGHEST
LO = 256
BY_LANES = 14
FIELDS = 16
WEIGHT_SCALE = 512.0
LEVER_SCALE = 32768.0
LEVER_BIAS = 1 << 20
FIELD_TOP = 1048575.0
TINY = 1e-30
CODE_TOP = 65535
SCALE_UNIT = 512.0
SCALE_LANES = 128
VMEM_BYTES = 48 << 20
PACK_VMEM_BYTES = 60 << 20
F32 = jnp.float32
BF16 = jnp.bfloat16
I32 = jnp.int32


def taps_of(derivative):
    offsets = np.arange(-KR, KR + 1) * 1.0
    gaussian = np.exp(-(offsets**2) / (2.0 * SIGMA**2))
    gaussian = gaussian / gaussian.sum()
    if derivative:
        return -offsets / SIGMA**2 * gaussian
    return gaussian


def axis_matrix(length, derivative):
    offsets = np.arange(length)[:, None] - np.arange(length)[None, :]
    return np.where(
        np.abs(offsets) <= KR, taps_of(derivative)[np.clip(offsets + KR, 0, 2 * KR)], 0.0
    )


def columns_at(matrix, rows, wanted):
    inside = (wanted >= 0) & (wanted < matrix.shape[1])
    picked = matrix[rows][:, np.clip(wanted, 0, matrix.shape[1] - 1)]
    return np.where(inside[None, :], picked, 0.0)


def unique_tables(tables):
    flat = np.stack([t.reshape(-1) for t in tables])
    kept, inverse = np.unique(np.round(flat, 14), axis=0, return_inverse=True)
    return kept.reshape((-1,) + tables[0].shape), inverse.reshape(-1).astype(np.int32)


def pieces_np(table):
    import ml_dtypes

    high = table.astype(np.float32).astype(ml_dtypes.bfloat16)
    low = (table - high.astype(np.float64)).astype(ml_dtypes.bfloat16)
    return np.concatenate([high, high, low], axis=-1)


def weight_table(
    z_kinds, x_kinds, z_rows, z_len, z_count, z_blocks, x_len, x_count, x_parts
):
    z_tables = []
    for r in range(z_count):
        wanted = np.concatenate([np.arange(z_len) + z_len * block for block in z_blocks(r)])
        rows = [np.arange(z_len) + z_len * block for block in z_rows(r)]
        z_tables.append(np.stack([columns_at(m, i, wanted) for m, i in zip(z_kinds, rows)]))
    x_tables = []
    for b in range(x_count):
        wanted = np.concatenate([x_len * b + part for part in x_parts(b)])
        rows = np.arange(x_len) + x_len * b
        x_tables.append(np.stack([columns_at(m, rows, wanted) for m in x_kinds]))
    z_tables, z_inverse = unique_tables(z_tables)
    x_tables, x_inverse = unique_tables(x_tables)
    kinds = len(z_kinds)
    parts, start = [], 0
    for part in x_parts(0):
        piece = x_tables[:, :, :, start : start + len(part)]
        start += len(part)
        full = np.einsum("rkzi,bkxj->rbkzxij", z_tables, piece)
        parts.append(
            full.reshape(len(z_tables) * len(x_tables), kinds * z_len * x_len, -1)
        )
    table = pieces_np(np.concatenate(parts, axis=-1))
    return table, z_inverse, x_inverse, len(x_tables)


def eye_column(row, eye):
    return jnp.sum(jnp.where(eye, row, jnp.zeros_like(row)), axis=1, keepdims=True)


def slot_row(row, most):
    frags = row.shape[1]
    sub = lax.broadcasted_iota(I32, (frags, frags), 0)
    lane = lax.broadcasted_iota(I32, (frags, frags), 1)
    eye = sub == lane
    earlier = jnp.logical_and(eye_column(row, eye) == row, sub < lane)
    return jnp.sum(jnp.where(earlier, 1, 0), axis=0, keepdims=True), eye


def pack_kernel(most, lines, row_count, *refs):
    inputs, (out_ref, place_ref, code_ref) = refs[:6], refs[6:9]
    held, sems = refs[9:15], refs[15]
    copies = [
        pltpu.make_async_copy(source, target, sems.at[k])
        for k, (source, target) in enumerate(zip(inputs, held))
    ]
    for copy in copies:
        copy.start()
    brick_ref, angle_ref, cell_ref, weight_ref, arm_ref, target_ref = held
    for copy in copies[:2]:
        copy.wait()
    frags, beads = cell_ref.shape
    slots = out_ref.shape[0]
    row = brick_ref[...]
    rank, eye = slot_row(row, most)
    slot = row * most + rank
    place = jnp.where(lax.broadcasted_iota(I32, (slots, frags), 0) == slot, 1.0, 0.0).astype(BF16)

    angles = angle_ref[...]
    cos, sin = jnp.cos(angles), jnp.sin(angles)
    cos_a, cos_b, cos_c = cos[0:1], cos[1:2], cos[2:3]
    sin_a, sin_b, sin_c = sin[0:1], sin[1:2], sin[2:3]
    turn = [
        [cos_a * cos_b, cos_a * sin_b * sin_c - sin_a * cos_c, cos_a * sin_b * cos_c + sin_a * sin_c],
        [sin_a * cos_b, sin_a * sin_b * sin_c + cos_a * cos_c, sin_a * sin_b * cos_c - cos_a * sin_c],
        [-sin_b, cos_b * sin_c, cos_b * cos_c],
    ]
    turn = [[eye_column(value, eye) for value in values] for values in turn]
    place_ref[0:1, :] = row
    place_ref[1:2, :] = rank
    for copy in copies[2:5]:
        copy.wait()
    levers = []
    for i in range(3):
        total = turn[i][0] * arm_ref[0]
        for j in (1, 2):
            total = total + turn[i][j] * arm_ref[j]
        lever = jnp.round(total * LEVER_SCALE).astype(I32)
        levers += [lever >> 14, (lever >> 7) & 127, lever & 127]

    cell = cell_ref[...]
    line = ((cell.astype(F32) + 0.5) * (1.0 / row_count)).astype(I32)
    y = cell - line * row_count
    weight = weight_ref[...].astype(F32) * WEIGHT_SCALE
    pieces = [(y // LO) * lines + line, y % LO] + levers
    pieces = [weight.astype(BF16)] + [v.astype(F32).astype(BF16) for v in pieces]
    payload = jnp.concatenate(pieces, axis=1)
    placed = jnp.dot(place, payload, preferred_element_type=F32).astype(I32)
    weight, hi, lo, *levers = [
        placed[:, k * beads : (k + 1) * beads] for k in range(len(pieces))
    ]
    code = (hi << 8) | lo
    lx, ly, lz = [
        (levers[k] << 14) + (levers[k + 1] << 7) + levers[k + 2] for k in (0, 3, 6)
    ]
    one, two = pack_three(lx, ly, lz)
    out_ref[:, 0:beads] = code | (weight << 16)
    out_ref[:, beads : 2 * beads] = one
    out_ref[:, 2 * beads : 3 * beads] = two
    copies[5].wait()
    encode(target_ref[...], code_ref)


def line_blur(value, derivative):
    taps = taps_of(derivative)
    rows, length = value.shape
    wide = jnp.concatenate([value, jnp.zeros((rows, 128), F32)], axis=1)
    total = None if derivative else float(taps[KR]) * value
    for d in range(1, KR + 1):
        up = pltpu.roll(wide, d, 1)[:, :length]
        down = pltpu.roll(wide, length + 128 - d, 1)[:, :length]
        pair = up - down if derivative else up + down
        term = float(taps[KR + d]) * pair
        total = term if total is None else total + term
    return total


def encode(value, out_ref):
    half, length = value.shape[0] // 2, value.shape[1]
    top = (jnp.max(value) * SCALE_UNIT).astype(I32) + 1
    scale = (SCALE_UNIT * CODE_TOP) / top.astype(F32)
    code = jnp.minimum((value * scale + 0.5).astype(I32), CODE_TOP)
    out_ref[:, :length] = code[:half] | (code[half:] << 16)
    out_ref[:, length:] = jnp.full((half, SCALE_LANES), top, I32)


def decode(words, count):
    half, length = words.shape[0] // count, words.shape[1] - SCALE_LANES
    step = words[:, length : length + 1].astype(F32) * (1.0 / (SCALE_UNIT * CODE_TOP))
    low = (words[:, :length] & CODE_TOP).astype(F32) * step
    high = ((words[:, :length] >> 16) & CODE_TOP).astype(F32) * step
    lines = []
    for k in range(count):
        rows = slice(k * half, (k + 1) * half)
        lines += [low[rows], high[rows]]
    return lines


def splat_kernel(lines, rb, got_ref, out_ref, code_ref, acc_ref):
    slots = got_ref.shape[0]
    beads = got_ref.shape[1] // 3
    his = acc_ref.shape[0]
    acc_ref[...] = jnp.zeros_like(acc_ref)
    hi_iota = lax.broadcasted_iota(I32, (his, beads), 0)
    lo_iota = lax.broadcasted_iota(I32, (LO, beads), 0)

    def body(i, carry):
        word = got_ref[pl.ds(i * rb, rb), 0:beads]
        lo = word & (LO - 1)
        hi = (word >> 8) & 255
        weight = (word >> 16).astype(F32) * (1.0 / WEIGHT_SCALE)
        left, right = [], []
        for q in range(rb):
            left.append(jnp.where(hi_iota == hi[q : q + 1], weight[q : q + 1], 0.0).astype(BF16))
            right.append(jnp.where(lo_iota == lo[q : q + 1], 1.0, 0.0).astype(BF16))
        acc_ref[...] += lax.dot_general(
            jnp.concatenate(left, axis=1),
            jnp.concatenate(right, axis=1),
            (((1,), (1,)), ((), ())),
            preferred_element_type=F32,
        )
        return carry

    lax.fori_loop(0, slots // rb, body, 0)
    density = [acc_ref[yh * lines : (yh + 1) * lines, :] for yh in range(his // lines)]
    smooth = line_blur(jnp.concatenate(density, axis=1), False)
    out_ref[...] = smooth
    encode(smooth, code_ref)


def split(value):
    high = value.astype(BF16)
    low = (value - high.astype(F32)).astype(BF16)
    return high, low


def mix_lines(index_ref, tables_ref, parts):
    value = jnp.concatenate(parts, axis=0)
    high, low = split(value)
    return jnp.dot(
        tables_ref[index_ref[0]], jnp.concatenate([high, low, high], axis=0), preferred_element_type=F32
    )


def pack_three(first, second, third):
    third = third + LEVER_BIAS
    return (first << 11) | (third >> 10), (second << 11) | (third & 1023)


def unpack_three(one, two):
    return one >> 11, two >> 11, (((one & 2047) << 10) | (two & 1023)) - LEVER_BIAS


def store_fields(fields, lines, out_ref, word_ref, scale_ref):
    top = jnp.maximum(jnp.max(jnp.abs(jnp.concatenate(fields, axis=0))), TINY)
    scale_ref[...] = jnp.full(scale_ref.shape, top * (1.0 / FIELD_TOP), F32)
    up = FIELD_TOP / jnp.full((1, fields[0].shape[1]), top, F32)
    one, two = pack_three(*[jnp.round(field * up).astype(I32) for field in fields])
    word_ref[:lines, :] = one
    word_ref[lines:, :] = two
    his = fields[0].shape[1] // LO * lines
    for k, field in enumerate(fields):
        for yh in range(field.shape[1] // LO):
            high, low = split(field[:, yh * LO : (yh + 1) * LO])
            rows = slice(k * his + yh * lines, k * his + (yh + 1) * lines)
            out_ref[rows, 0:LO] = high
            out_ref[rows, LO : 2 * LO] = low


def window_lines(own_ref, near_refs, first_ref, second_ref):
    lines = [own_ref[...]]
    for ref in near_refs:
        lines += decode(ref[...], 1)
    for ref in (first_ref, second_ref):
        lines += decode(ref[...], len(near_refs) + 1)
    return lines


def target_kernel(lines, index_ref, tables_ref, own_ref, *refs):
    *near_refs, first_ref, second_ref, out_ref, word_ref, scale_ref = refs
    window = window_lines(own_ref, near_refs, first_ref, second_ref)
    mixed = mix_lines(index_ref, tables_ref, window)
    grad_x = line_blur(mixed[0:lines], False)
    grad_y = line_blur(mixed[lines : 2 * lines], True)
    grad_z = line_blur(mixed[2 * lines : 3 * lines], False)
    store_fields([grad_x, grad_y, grad_z], lines, out_ref, word_ref, scale_ref)


def model_kernel(lines, near, index_ref, tables_ref, target_ref, *refs):
    target = [target_ref[...]]
    for ref in refs[: near - 1]:
        target += decode(ref[...], 1)
    target = jnp.concatenate(target, axis=0)
    own_ref, *near_refs, first_ref, second_ref, out_ref, word_ref, scale_ref, sum_ref = refs[near - 1 :]
    window = window_lines(own_ref, near_refs, first_ref, second_ref)
    smooth = mix_lines(index_ref, tables_ref, window)
    model = smooth[3 * lines :]
    sums = [jnp.sum(model * target), jnp.sum(model * model), jnp.sum(target * target)]
    lane = lax.broadcasted_iota(I32, sum_ref.shape, 1)
    total = jnp.zeros(sum_ref.shape, F32)
    for k, value in enumerate(sums):
        total = jnp.where(lane == k, value, total)
    sum_ref[...] = total
    grad_x = line_blur(smooth[0:lines], False)
    grad_y = line_blur(smooth[lines : 2 * lines], True)
    grad_z = line_blur(smooth[2 * lines : 3 * lines], False)
    store_fields([grad_x, grad_y, grad_z], lines, out_ref, word_ref, scale_ref)


def sample_by_matmul(word, field_ref, his, store):
    count, beads = word.shape
    lo, hi = word & (LO - 1), (word >> 8) & 255
    lo_iota = lax.broadcasted_iota(I32, (LO, beads), 0)
    picks = [jnp.where(lo_iota == lo[q : q + 1], 1.0, 0.0).astype(BF16) for q in range(count)]
    pick = jnp.concatenate(picks, axis=1)
    sampled = jnp.dot(
        field_ref[...], jnp.concatenate([pick, pick], axis=0), preferred_element_type=F32
    )

    def finish():
        sub_iota = lax.broadcasted_iota(I32, (8, beads), 0)
        for q in range(count):
            own = jnp.broadcast_to(hi[q : q + 1], (8, beads))
            group, within = own >> 3, (own & 7) == sub_iota
            found = [jnp.zeros((8, beads), F32)] * 3
            for j in range(his // 8):
                here = group == j
                for k in range(3):
                    rows = slice(k * his + 8 * j, k * his + 8 * j + 8)
                    part = sampled[rows, q * beads : (q + 1) * beads]
                    found[k] = jnp.where(here, part, found[k])
            store(q, [jnp.sum(jnp.where(within, v, 0.0), axis=0, keepdims=True) for v in found])

    return finish


def sample_by_lanes(word, word_ref, scale_ref, lines, store):
    count, beads = word.shape
    tiles = word_ref.shape[1] // 128
    line_shift, lo_shift = lines.bit_length() - 1, LO.bit_length() - 1
    sub_iota = lax.broadcasted_iota(I32, (8, beads), 0)
    scale = scale_ref[0:1, :]
    for q in range(count):
        own = jnp.broadcast_to(word[q : q + 1], (8, beads))
        lo, hi = own & (LO - 1), (own >> lo_shift) & 255
        line = hi & (lines - 1)
        group = (line >> 3) * tiles + (hi >> line_shift) * (LO // 128) + (lo >> 7)
        within, lane = (line & 7) == sub_iota, lo & 127
        found = [jnp.zeros((8, beads), I32)] * 2
        for j in range(lines // 8 * tiles):
            here = group == j
            first, tile = j // tiles * 8, j % tiles * 128
            for k in range(2):
                table = word_ref[k * lines + first : k * lines + first + 8, tile : tile + 128]
                part = jnp.take_along_axis(table, lane, axis=1, mode="promise_in_bounds")
                found[k] = jnp.where(here, part, found[k])
        one, two = [jnp.sum(jnp.where(within, v, 0), axis=0, keepdims=True) for v in found]
        store(q, [v.astype(F32) * scale for v in unpack_three(one, two)])


def sample_kernel(
    lines, his, rb, by_lanes, start, got_ref, field_ref, word_ref, scale_ref, out_ref, force_ref
):
    slots = out_ref.shape[0]
    beads = got_ref.shape[1] // 3
    by_matmul = rb - by_lanes

    def body(i, carry):
        def store_from(first):
            def store(q, values):
                for k in range(3):
                    force_ref[k, pl.ds(i * rb + first + q, 1), :] = values[k]

            return store

        word = got_ref[pl.ds(start + i * rb, rb), 0:beads]
        finish = sample_by_matmul(word[:by_matmul], field_ref, his, store_from(0))
        rest = word[by_matmul:]
        sample_by_lanes(rest, word_ref, scale_ref, lines, store_from(by_matmul))
        finish()
        return carry

    lax.fori_loop(0, slots // rb, body, 0)
    rows = slice(start, start + slots)
    first, second = got_ref[rows, beads : 2 * beads], got_ref[rows, 2 * beads : 3 * beads]
    weight = (got_ref[rows, 0:beads] >> 16).astype(F32) * (1.0 / WEIGHT_SCALE)
    levers = [v.astype(F32) * (1.0 / LEVER_SCALE) for v in unpack_three(first, second)]
    force = [force_ref[k] * weight for k in range(3)]
    terms = force + [
        levers[1] * force[2] - levers[2] * force[1],
        levers[2] * force[0] - levers[0] * force[2],
        levers[0] * force[1] - levers[1] * force[0],
    ]
    lane = lax.broadcasted_iota(I32, out_ref.shape, 1)
    total = jnp.zeros(out_ref.shape, F32)
    for k, term in enumerate(terms):
        total = jnp.where(lane == k, jnp.sum(term, axis=1, keepdims=True), total)
    out_ref[...] = total


def join_kernel(most, *refs):
    *target_refs, model_ref, sum_ref, out_ref = refs
    bricks = out_ref.shape[0]
    lane = lax.broadcasted_iota(I32, out_ref.shape, 1)
    sums = sum_ref[0:1, :]
    for k in range(1, sum_ref.shape[0] // 8):
        sums = sums + sum_ref[8 * k : 8 * k + 1, :]
    total = jnp.zeros(out_ref.shape, F32)
    for k in range(most):
        rows = pl.ds(k, bricks, stride=most)
        parts = [ref[pl.ds(k, ref.shape[0] // most, stride=most), :] for ref in target_refs]
        own = jnp.concatenate(parts, axis=0)
        own = jnp.where(lane < 6, own, 0.0)
        own = own + pltpu.roll(jnp.where(lane < 6, model_ref[rows, :], 0.0), 6, 1)
        if k == 0:
            own = own + pltpu.roll(jnp.where(lane < 3, sums, 0.0), 12, 1)
        total = total + (pltpu.roll(own, FIELDS * k, 1) if k else own)
    out_ref[...] = total


def finish_kernel(most, voxel_total, place_ref, back_ref, out_ref):
    frags = out_ref.shape[1]
    bricks = back_ref.shape[0]
    row, rank = place_ref[0:1, :], place_ref[1:2, :]
    place = jnp.where(lax.broadcasted_iota(I32, (bricks, frags), 0) == row, 1.0, 0.0).astype(F32)
    back = back_ref[...]
    sums = jnp.sum(back, axis=0, keepdims=True)
    cross, model_sq, target_sq = sums[:, 12:13], sums[:, 13:14], sums[:, 14:15]
    norm_model = jnp.sqrt(model_sq + EPSILON)
    norm_target = jnp.sqrt(target_sq + EPSILON)
    corr = cross / (norm_model * norm_target)
    scale_target = voxel_total / (norm_model * norm_target)
    scale_model = voxel_total * corr / (norm_model * norm_model)
    found = lax.dot_general(
        back, place, (((0,), (0,)), ((), ())), precision=HIGHEST, preferred_element_type=F32
    )
    mine = jnp.zeros((FIELDS, frags), F32)
    for k in range(most):
        mine = jnp.where(rank == k, found[FIELDS * k : FIELDS * (k + 1)], mine)
    out_ref[...] = scale_target * mine[0:6] - scale_model * mine[6:12]


def cost(macs, nbytes):
    return pl.CostEstimate(flops=2 * macs, bytes_accessed=nbytes, transcendentals=0)


def call(
    kernel, out_shape, *args, scratch=(), name=None, macs=0, in_specs=None, vmem=VMEM_BYTES
):
    kwargs = {} if in_specs is None else {"in_specs": in_specs}
    return pl.pallas_call(
        kernel,
        out_shape=out_shape,
        scratch_shapes=list(scratch),
        compiler_params=pltpu.CompilerParams(vmem_limit_bytes=vmem),
        cost_estimate=cost(macs, 4 * sum(a.size for a in args)),
        name=name,
        **kwargs,
    )(*args)


def call_at(kernel, out_shape, index, table, *args, name=None, macs=0):
    vmem = pl.BlockSpec(memory_space=pltpu.VMEM)
    return call(
        kernel,
        out_shape,
        index, table, *args,
        in_specs=[pl.BlockSpec(memory_space=pltpu.SMEM)] + [vmem] * (1 + len(args)),
        name=name,
        macs=macs,
    )


def looked_up(values, position):
    found = jnp.full((), int(values[0]), I32)
    for i in range(1, len(values)):
        step = int(values[i]) - int(values[i - 1])
        if step:
            found = found + step * (position >= i).astype(I32)
    return found


def shifted(value, axis, step):
    size = lax.axis_size(axis)
    pairs = [(i, i + step) for i in range(size) if 0 <= i + step < size]
    return lax.ppermute(value, axis, pairs)


def paired(own, left, right):
    return lambda b: [own, right, left] if b % 2 == 0 else [own, left, right]


def swapped(first, second):
    size = lax.axis_size("brick")
    found = []
    for value, start in ((first, 0), (second, 1)):
        pairs = [(i, i + 1) for i in range(start, size - 1, 2)]
        found.append(lax.ppermute(value, "brick", pairs + [(j, i) for i, j in pairs]))
    return found


def relay_blocks(value, reach):
    size = lax.axis_size("relay")
    if size == 2:
        return [value, lax.ppermute(value, "relay", [(0, 1), (1, 0)])]
    blocks = [value]
    for step in range(1, min(reach, size - 1) + 1):
        blocks += [shifted(value, "relay", step), shifted(value, "relay", -step)]
    return blocks


def relay_order(size, reach):
    if size == 2:
        return lambda r: [r, 1 - r]
    steps = [0]
    for step in range(1, min(reach, size - 1) + 1):
        steps += [-step, step]
    return lambda r: [r + s for s in steps]


def relay_total(value):
    size = lax.axis_size("relay")
    values, moving = [value], value
    for _ in range(size - 1):
        moving = lax.ppermute(moving, "relay", [(i, (i + 1) % size) for i in range(size)])
        values.append(moving)
    return jnp.concatenate(values, axis=0)


def shards(target, frag_brick, bead_cell, bead_weight, bead_arm, frag_angle):
    brick_count, relay_count = lax.axis_size("brick"), lax.axis_size("relay")
    frags, beads = bead_cell.shape
    planes, columns, rows = target.shape
    lines = planes * columns
    his = lines * (rows // LO)
    assert rows % LO == 0 and his <= 256 and columns >= 2 * KR
    assert beads == 128 and lines & (lines - 1) == 0
    voxel_total = float(brick_count * columns * relay_count * planes * rows)
    most = max(2, 2 * frags // brick_count)
    slots = brick_count * most
    assert most * FIELDS <= 128

    z_total, x_total = relay_count * planes, brick_count * columns
    gz, dz = axis_matrix(z_total, False), axis_matrix(z_total, True)
    gx, dx = axis_matrix(x_total, False), axis_matrix(x_total, True)
    near = 2 if relay_count == 2 else 1
    reach_one, reach_two = -(-KR // planes), -(-2 * KR // planes)
    target_table, tz, tx, tn = weight_table(
        [gz, gz, dz], [dx, gx, gx], lambda r: [r] * 3, planes, relay_count, relay_order(relay_count, reach_one),
        columns, brick_count,
        paired(np.arange(columns), np.arange(-KR, 0), np.arange(columns, columns + KR)),
    )
    model_table, mz, mx, mn = weight_table(
        [gz @ gz, gz @ gz, dz @ gz] + [gz] * near, [dx @ gx, gx @ gx, gx @ gx] + [gx] * near,
        lambda r: [r] * 4 + [1 - r] * (near - 1),
        planes, relay_count, relay_order(relay_count, reach_two), columns, brick_count,
        paired(np.arange(columns), np.arange(-columns, 0), np.arange(columns, 2 * columns)),
    )
    r, b = lax.axis_index("relay"), lax.axis_index("brick")
    target_index = (looked_up(tz, r) * tn + looked_up(tx, b)).reshape(1)
    model_index = (looked_up(mz, r) * mn + looked_up(mx, b)).reshape(1)

    target_lines = target.reshape(lines, rows)
    words = jax.ShapeDtypeStruct((lines // 2, rows + SCALE_LANES), I32)
    hbm = pl.BlockSpec(memory_space=pltpu.HBM)
    packed = [frag_brick.reshape(1, frags), frag_angle, bead_cell, bead_weight, bead_arm]
    packed += [target_lines]
    sent, place, target_code = call(
        functools.partial(pack_kernel, most, lines, rows),
        [
            jax.ShapeDtypeStruct((slots, 3 * beads), I32),
            jax.ShapeDtypeStruct((8, frags), I32),
            words,
        ],
        *packed,
        in_specs=[hbm] * len(packed),
        scratch=[pltpu.VMEM(a.shape, a.dtype) for a in packed]
        + [pltpu.SemaphoreType.DMA((len(packed),))],
        name="pack",
        vmem=PACK_VMEM_BYTES,
    )
    target_blocks = relay_blocks(target_code, reach_one)
    by_column = [t.reshape(-1, columns, rows + SCALE_LANES) for t in target_blocks]
    left_edge = jnp.concatenate([t[:, columns - KR :] for t in by_column], axis=0)
    right_edge = jnp.concatenate([t[:, :KR] for t in by_column], axis=0)
    first_edge = jnp.where(b % 2 == 0, left_edge, right_edge)
    second_edge = jnp.where(b % 2 == 0, right_edge, left_edge)
    target_near = swapped(
        first_edge.reshape(-1, rows + SCALE_LANES), second_edge.reshape(-1, rows + SCALE_LANES)
    )

    got = lax.all_to_all(sent, "brick", split_axis=0, concat_axis=0, tiled=True)
    smooth, coded = call(
        functools.partial(splat_kernel, lines, min(64, slots)),
        [jax.ShapeDtypeStruct((lines, rows), F32), words],
        got,
        scratch=[pltpu.VMEM((his, LO), F32)],
        name="splat",
        macs=slots * beads * his * LO,
    )
    coded, *target_near = lax.optimization_barrier((coded, *target_near))
    target_parts = [target_lines] + target_blocks[1:] + target_near
    blocks = relay_blocks(coded, reach_two)
    field_shapes = [
        jax.ShapeDtypeStruct((3 * his, 2 * LO), BF16),
        jax.ShapeDtypeStruct((2 * lines, rows), I32),
        jax.ShapeDtypeStruct((8, 128), F32),
    ]
    target_field = call_at(
        functools.partial(target_kernel, lines),
        field_shapes,
        target_index, jnp.asarray(target_table), *target_parts,
        name="target_fields",
        macs=9 * lines * rows * 128,
    )

    def sample(field, start, count, name):
        rb = min(32, count)
        return call(
            functools.partial(sample_kernel, lines, his, rb, rb * BY_LANES // 32, start),
            jax.ShapeDtypeStruct((count, 128), F32),
            got, *field,
            scratch=[pltpu.VMEM((3, count, beads), F32)],
            name=name,
            macs=6 * count * beads * his * LO,
        )

    part = slots // 4
    target_first = sample(target_field, 0, part, "target_sample_a")
    blocks, target_first, target_field = lax.optimization_barrier(
        (blocks, target_first, target_field)
    )
    beside = jnp.concatenate(blocks, axis=0)
    model_parts = [smooth] + blocks[1:]
    model_parts += swapped(beside, beside)
    target_second = sample(target_field, part, slots - part, "target_sample_b")
    target_second, *model_parts = lax.optimization_barrier((target_second, *model_parts))
    *model_field, partial = call_at(
        functools.partial(model_kernel, lines, near),
        field_shapes + [jax.ShapeDtypeStruct((8, 128), F32)],
        model_index, jnp.asarray(model_table), target_lines, *target_blocks[1:near], *model_parts,
        name="model_fields",
    )
    partials = partial if near == relay_count else relay_total(partial)
    model_sums = sample(model_field, 0, slots, "model_sample")
    leaving = call(
        functools.partial(join_kernel, most),
        jax.ShapeDtypeStruct((brick_count, 128), F32),
        target_first, target_second, model_sums, partials,
        name="join",
    )
    back = lax.all_to_all(leaving, "brick", split_axis=0, concat_axis=0, tiled=True)
    return call(
        functools.partial(finish_kernel, most, voxel_total),
        jax.ShapeDtypeStruct((6, frags), F32),
        place, back,
        name="finish",
    )


def solution(mesh):
    placed = (
        P("relay", "brick", None),
        P(("brick", "relay"), None),
        P(("brick", "relay"), None),
        P(("brick", "relay"), None),
        P(None, ("brick", "relay"), None),
        P(None, ("brick", "relay")),
    )
    return jax.shard_map(
        shards, mesh=mesh, in_specs=placed, out_specs=P(None, ("brick", "relay")), check_vma=False
    )
```
